256 devices in a mesh: space: 64 (over z, y, x_hi), rep: 4 (over x_lo, core).
Axes of the slice: x: 4 (x_hi: 2, x_lo: 2; x = x_hi * 2 + x_lo), y: 4, z: 8, core: 2. Of those that a mesh axis runs over, the one named last changes fastest.
Arguments:
- features: bfloat16 [1024, 64, 512], P(('space', 'rep')), may hold values from -6 to 6
- neighbours: int32 [1024, 27], P(('space', 'rep')), may hold values from -1 to 7, as said below
- counts: int32 [256], P(('space', 'rep')), may hold values from 1 to 4, as said below
- cotangent: bfloat16 [1024, 64, 128], P(('space', 'rep')), may hold values from -0.0234375 to 0.0234375
- conv_weight: bfloat16 [27, 64, 64], replicated, may hold values from -0.15625 to 0.15625
- down_weight: bfloat16 [8, 128, 64], replicated, may hold values from -0.25 to 0.25
Outputs:
- hidden: bfloat16 [1024, 64, 512], P(('space', 'rep'))
- conv_grad: float32 [27, 64, 64], replicated
- down_grad: float32 [8, 128, 64], replicated
The draws below stay inside these ranges and needn't reach their ends.
Inputs may be any that keep to these rules, and one draw needn't show every extreme that they name: `counts`: in every tile, of the two strips s and s + 32 at most one has more than 2 occupied blocks; some strip has exactly 4 and some exactly 2. Only live slots name neighbours, and they name only live slots; strip 0 names nothing below and the last strip nothing above.
All inputs are finite; a program needn't handle non-finite values.
Results may differ from the reference program's by a relative error of at most 0.0029.
Values may be sent and summed in bfloat16 or wider, within the bound.
A program may use at most 64 MiB of HBM per device.

```python
import jax
import jax.numpy as jnp
from jax import lax

C = 64
C2 = 128
SLOTS = 4
BLOCKS = 1024
N_SPACE = 64
N_REP = 4


def pair_counts(key):
    half_space = N_SPACE // 2
    key_side, key_heavy, key_light = jax.random.split(jax.random.fold_in(key, 7), 3)
    heavy_side = jax.random.randint(key_side, (half_space, N_REP), 0, 2)
    heavy_count = jax.random.randint(key_heavy, (half_space, N_REP), SLOTS // 2 + 1, SLOTS + 1)
    light_count = jax.random.randint(key_light, (half_space, N_REP), 1, SLOTS // 2 + 1)
    heavy_count = heavy_count.at[0, 0].set(SLOTS)
    light_count = light_count.at[0, 0].set(SLOTS // 2)
    first_half = jnp.where(heavy_side == 1, heavy_count, light_count)
    second_half = jnp.where(heavy_side == 1, light_count, heavy_count)
    return jnp.concatenate([first_half, second_half], 0).astype(jnp.int32)


def draw_counts(key, part):
    return pair_counts(key).reshape(N_SPACE * N_REP)


def draw_neighbours(key, part):
    strip_counts = pair_counts(key)
    key_bits, key_present, key_side = jax.random.split(jax.random.fold_in(key, 13), 3)
    shape = (N_SPACE, N_REP, SLOTS, 27)
    random_bits = jax.random.randint(key_bits, shape, 0, 1 << 20)
    present = jax.random.randint(key_present, shape, 0, 5) < 3
    side_pick = jax.random.randint(key_side, shape, 0, 2)
    zero_row = jnp.zeros((1, N_REP), jnp.int32)
    own_count = strip_counts[:, :, None, None]
    prev_count = jnp.concatenate([zero_row, strip_counts[:-1]], 0)[:, :, None, None]
    next_count = jnp.concatenate([strip_counts[1:], zero_row], 0)[:, :, None, None]
    column = jnp.arange(27, dtype=jnp.int32)
    use_prev = (column < 9) & (side_pick == 1) & (prev_count > 0)
    use_next = (column >= 18) & (side_pick == 1) & (next_count > 0)
    own_index = random_bits % own_count
    prev_index = SLOTS + random_bits % jnp.maximum(prev_count, 1)
    next_index = SLOTS + random_bits % jnp.maximum(next_count, 1)
    chosen = jnp.where(use_prev, prev_index, jnp.where(use_next, next_index, own_index))
    slot_index = jnp.arange(SLOTS, dtype=jnp.int32)[None, None, :, None]
    live_mask = slot_index < own_count
    chosen = jnp.where(present & live_mask, chosen, -1)
    chosen = jnp.where((column == 13) & live_mask, slot_index, chosen)
    return chosen.reshape(N_SPACE * N_REP * SLOTS, 27).astype(jnp.int32)


def level_of(stream_key, shape, shards, least, top_value):
    def one(dim, shards_of):
        draws = jax.random.uniform(jax.random.fold_in(jax.random.fold_in(stream_key, 6), dim), (shards_of,), jnp.float32, least / len(shards), top_value / len(shards))
        return jnp.repeat(jnp.exp(draws), shape[dim] // shards_of).reshape((-1,) + (1,) * (len(shape) - dim - 1))

    level = one(*shards[0])
    for cut in shards[1:]:
        level = level * one(*cut)
    return level


def noise(key, shape, width, bound, cuts=(), kind=jnp.bfloat16):
    result = width * jax.random.normal(key, shape, jnp.float32)
    if cuts:
        result = result * level_of(key, shape, cuts, -0.22, 0.18)
    return jnp.clip(result, -bound, bound).astype(kind)


def setup_inputs(seed: int = 0) -> dict:
    key_of = jax.random.split(jax.random.key(seed), 7)
    features = noise(key_of[0], (BLOCKS, C, 512), 1.0, 6.0, ((0, 256),))
    neighbours = draw_neighbours(jax.random.fold_in(key_of[6], 71), 0)
    counts = draw_counts(jax.random.fold_in(key_of[6], 71), 0)
    cotangent = noise(key_of[3], (BLOCKS, 64, C2), (0.125 / (N_SPACE * N_REP * SLOTS) ** 0.5), 0.0234375, ((0, 256),))
    conv_weight = noise(key_of[4], (27, C, C), (27 * C) ** -0.5, 0.15625)
    down_weight = noise(key_of[5], (8, C2, C), (8 * C) ** -0.5, 0.25)
    return {"features": features, "neighbours": neighbours, "counts": counts, "cotangent": cotangent, "conv_weight": conv_weight, "down_weight": down_weight}


def plane_slice(offset):
    if offset < 0:
        return slice(7, 8)
    if offset > 0:
        return slice(0, 1)
    return slice(0, 8)


def take_rows(source_table, index_rows):
    padding = jnp.zeros((1,) + source_table.shape[1:], source_table.dtype)
    extended = jnp.concatenate([source_table, padding], 0)
    safe_index = jnp.where(index_rows < 0, source_table.shape[0], index_rows).astype(jnp.int32)
    return jnp.take(extended, safe_index, axis=0)


def build_padded(features_live, prev_upper, next_lower, neighbours):
    count_rows, channels = features_live.shape[0], features_live.shape[1]
    blocks = features_live.reshape(count_rows, channels, 8, 8, 8)
    low_table = jnp.concatenate([blocks[:, :, 7:8], prev_upper.reshape(-1, channels, 1, 8, 8)], 0)
    high_table = jnp.concatenate([blocks[:, :, 0:1], next_lower.reshape(-1, channels, 1, 8, 8)], 0)
    layers = []
    for step_x, source_table in ((-1, low_table), (0, blocks), (1, high_table)):
        row_list = []
        for step_y in (-1, 0, 1):
            tile_list = []
            for step_z in (-1, 0, 1):
                column = (step_x + 1) * 9 + (step_y + 1) * 3 + step_z + 1
                if column == 13:
                    tile_list.append(blocks)
                else:
                    piece = source_table[:, :, :, plane_slice(step_y), plane_slice(step_z)]
                    tile_list.append(take_rows(piece, neighbours[:, column]))
            row_list.append(jnp.concatenate(tile_list, 4))
        layers.append(jnp.concatenate(row_list, 3))
    return jnp.concatenate(layers, 2)


def block_section(padded, grads_in, conv_weight, down_weight):
    count_rows, channels = padded.shape[0], padded.shape[1]
    out_channels = down_weight.shape[1]

    def shifted_at(column):
        step_x, step_y, step_z = column // 9 - 1, (column // 3) % 3 - 1, column % 3 - 1
        window = padded[:, :, 1 + step_x:9 + step_x, 1 + step_y:9 + step_y, 1 + step_z:9 + step_z]
        return window.reshape(count_rows, channels, 512).astype(jnp.float32)

    weights = conv_weight.astype(jnp.float32)
    pre_act = jnp.zeros((count_rows, channels, 512), jnp.float32)
    for column in range(27):
        pre_act = pre_act + jnp.einsum("oc,bcv->bov", weights[column], shifted_at(column))
    hidden = jnp.maximum(pre_act, 0.0).astype(jnp.bfloat16)
    hidden_cells = hidden.reshape(count_rows, channels, 4, 2, 4, 2, 4, 2).astype(jnp.float32)
    grid_grads = grads_in.reshape(count_rows, 4, 4, 4, out_channels).astype(jnp.float32)
    down_grad = jnp.einsum("bcxiyjzk,bxyzo->ijkoc", hidden_cells, grid_grads).reshape(8, out_channels, channels)
    kernel = down_weight.reshape(2, 2, 2, out_channels, channels).astype(jnp.float32)
    hidden_grad = jnp.einsum("ijkoc,bxyzo->bcxiyjzk", kernel, grid_grads).reshape(count_rows, channels, 512)
    act_grad = jnp.where(pre_act > 0, hidden_grad, 0.0).astype(jnp.bfloat16).astype(jnp.float32)
    conv_grad = jnp.stack([jnp.einsum("bov,bcv->oc", act_grad, shifted_at(column)) for column in range(27)])
    return hidden, conv_grad, down_grad


def reference(features, neighbours, counts, cotangent, conv_weight, down_weight):
    feats_all = features.reshape(N_SPACE, N_REP, SLOTS, C, 512)
    slot_index = jnp.arange(SLOTS, dtype=jnp.int32)
    live_mask = slot_index[None, None, :] < counts.reshape(N_SPACE, N_REP)[:, :, None]
    features_live = jnp.where(live_mask[..., None, None], feats_all, jnp.zeros_like(feats_all))
    grads_all = cotangent.reshape(N_SPACE, N_REP, SLOTS, 64, C2)
    grads_live = jnp.where(live_mask[..., None, None], grads_all, jnp.zeros_like(grads_all))
    links = neighbours.reshape(N_SPACE, N_REP, SLOTS, 27)
    upper = features_live[..., 448:]
    lower = features_live[..., :64]
    zero_plane = jnp.zeros_like(upper[:1])
    prev_upper = jnp.concatenate([zero_plane, upper[:-1]], 0)
    next_lower = jnp.concatenate([lower[1:], zero_plane], 0)

    def one_tile(feats_one, prev_one, next_one, links_one, grads_one):
        padded = build_padded(feats_one, prev_one, next_one, links_one)
        return block_section(padded, grads_one, conv_weight, down_weight)

    def one_strip(items):
        hidden, conv_part, down_part = jax.vmap(one_tile)(*items)
        return hidden, jnp.sum(conv_part, 0), jnp.sum(down_part, 0)

    hidden, conv_part, down_part = lax.map(one_strip, (features_live, prev_upper, next_lower, links, grads_live))
    return hidden.reshape(BLOCKS, C, 512), jnp.sum(conv_part, 0), jnp.sum(down_part, 0)
```

```python
import functools

import jax
import jax.numpy as jnp
from jax import lax
from jax.experimental import pallas as pl
from jax.experimental.pallas import tpu as pltpu
from jax.sharding import PartitionSpec as P

MESH = pl.DeviceIdType.MESH
F32, BF16 = jnp.float32, jnp.bfloat16
VM = pl.BlockSpec(memory_space=pltpu.VMEM)
SM = pl.BlockSpec(memory_space=pltpu.SMEM)
NX, NY, NZ = 4, 4, 8
NXY = NX * NY
CONV_ROWS, DOWN_ROWS = 32, 16
ROWS = CONV_ROWS + DOWN_ROWS


def dot(a, b, dims):
    return lax.dot_general(a, b, (dims, ((), ())), preferred_element_type=F32)


NN, NT, TN = ((1,), (0,)), ((1,), (1,)), ((0,), (0,))


def voxels_in_rows(block):
    wide = block.astype(F32)
    return jnp.concatenate([wide, wide], 0).T


def fill_weights(cw_ref, dw_ref, w_ref, dt_ref):
    for dy in range(3):
        for dx in range(3):
            row = [cw_ref[dx * 9 + dy * 3 + dz].astype(F32) for dz in range(3)]
            w_ref[dy, dx * 64 : dx * 64 + 64, :] = jnp.concatenate(row, 1).astype(BF16)
    for t in range(0, 8, 2):
        pair = jnp.concatenate([dw_ref[t], dw_ref[t + 1]], 0).astype(F32)
        dt_ref[:, t * 128 : t * 128 + 256] = pair.T.astype(BF16)


def fill_tables(f_ref, t_ref, lo_ref, hi_ref):
    for j in range(4):
        for q in range(4):
            part = voxels_in_rows(f_ref[j, :, q * 128 : q * 128 + 128])
            t_ref[j, q * 2 : q * 2 + 2] = part.reshape(2, 8, 8, 128)
        lo_ref[j] = t_ref[j, 7]
        hi_ref[j] = t_ref[j, 0]
    t_ref[4] = jnp.zeros((8, 8, 8, 128), F32)
    lo_ref[8] = jnp.zeros((8, 8, 128), F32)
    hi_ref[8] = jnp.zeros((8, 8, 128), F32)


def fill_halo(prev_ref, next_ref, lo_ref, hi_ref):
    for j in range(4):
        lo_ref[4 + j] = voxels_in_rows(prev_ref[j])[64:].reshape(8, 8, 128)
        hi_ref[4 + j] = voxels_in_rows(next_ref[j])[:64].reshape(8, 8, 128)


def store_plane(q_ref, b, xp, middle, below, above):
    z = lax.broadcasted_iota(jnp.int32, (10, 8, 128), 1)
    first = lax.broadcasted_iota(jnp.int32, (10, 8, 128), 2) < 64
    minus = pltpu.roll(jnp.where(z == 7, below, middle), 1, 1)
    plus = pltpu.roll(jnp.where(z == 0, above, middle), 7, 1)
    left = jnp.where(first, minus, middle)
    for dy in range(3):
        rows = slice(xp * 64, xp * 64 + 64)
        q_ref[b, dy, rows, 0:128] = left[dy : dy + 8].reshape(64, 128).astype(BF16)
        q_ref[b, dy, rows, 128:256] = plus[dy : dy + 8].reshape(64, 128).astype(BF16)


def link(nb_ref, b, ox, oy, oz, zero):
    j = nb_ref[b, (ox + 1) * 9 + (oy + 1) * 3 + oz + 1]
    return jnp.where(j < 0, zero, j)


def fill_inner(nb_ref, count, b, t_ref, q_ref):
    own = jnp.where(b < count, b, 4)
    idx = [[link(nb_ref, b, 0, oy, oz, 4) for oy in (-1, 0, 1)] for oz in (0, -1, 1)]
    idx[0][1] = own
    for xp in range(1, 9):
        cols = [
            jnp.concatenate(
                [t_ref[i0, xp - 1, 7:8], t_ref[i1, xp - 1], t_ref[i2, xp - 1, 0:1]], 0
            )
            for i0, i1, i2 in idx
        ]
        store_plane(q_ref, b, xp, *cols)


def fill_outer(nb_ref, b, lo_ref, hi_ref, q_ref):
    for ox, xp, table in ((-1, 0, lo_ref), (1, 9, hi_ref)):
        cols = []
        for oz in (0, -1, 1):
            i0, i1, i2 = [link(nb_ref, b, ox, oy, oz, 8) for oy in (-1, 0, 1)]
            cols.append(jnp.concatenate([table[i0, 7:8], table[i1], table[i2, 0:1]], 0))
        store_plane(q_ref, b, xp, *cols)


def expand_cotangent(g_ref, count, b, gexp_ref):
    v = lax.broadcasted_iota(jnp.int32, (64, 512), 1)
    u = lax.broadcasted_iota(jnp.int32, (64, 512), 0)
    cell = (v // 128) * 16 + (v // 16 % 4) * 4 + v % 8 // 2
    spread = (cell == u).astype(F32).astype(BF16)
    grads = jnp.where(b < count, g_ref[b].astype(F32), 0.0)
    up = dot(grads.T.astype(BF16), spread, NN)
    w = lax.broadcasted_iota(jnp.int32, (128, 512), 1)
    place = (w // 64 % 2) * 4 + (w // 8 % 2) * 2 + w % 2
    for t in range(8):
        gexp_ref[t * 128 : t * 128 + 128] = jnp.where(place == t, up, 0.0).astype(BF16)


def block_math(b, w_ref, dt_ref, q_ref, gexp_ref, hid_ref, cg_ref, dg_ref):
    acc = jnp.zeros((192, 640), F32)
    for dy in range(3):
        acc += dot(w_ref[dy], q_ref[b, dy, :, 0:192], NT)
    pre = acc[0:64, 0:512] + acc[64:128, 64:576] + acc[128:192, 128:640]
    hidden = jnp.maximum(pre, 0.0).astype(BF16)
    hid_ref[b] = hidden
    dg_ref[...] += dot(gexp_ref[...], hidden, NT)
    grad = dot(dt_ref[...], gexp_ref[...], NN)
    act = jnp.where(pre > 0, grad, 0.0)
    gap = jnp.zeros((64, 64), F32)
    shifted = jnp.concatenate(
        [
            jnp.concatenate([act, gap, gap], 1),
            jnp.concatenate([gap, act, gap], 1),
            jnp.concatenate([gap, gap, act], 1),
        ],
        0,
    ).astype(BF16)
    for dy in range(3):
        cg_ref[dy] += dot(shifted, q_ref[b, dy], NN)


def pack(cg_ref, dg_ref, v_ref):
    def put(at, rows):
        for i in range(0, rows.shape[0], CONV_ROWS):
            v_ref[(at + i) // CONV_ROWS, 0:CONV_ROWS] = rows[i : i + CONV_ROWS]

    for dy in range(3):
        put(dy * 192, cg_ref[dy, :, 0:128])
    first = lax.broadcasted_iota(jnp.int32, (192, 128), 1) < 64
    put(576, jnp.where(first, cg_ref[0, :, 128:256], cg_ref[1, :, 128:256]))
    put(768, cg_ref[2, :, 128:256])
    put(960, jnp.zeros((64, 128), F32))
    pairs = jnp.concatenate([dg_ref[0:512], dg_ref[512:1024]], 1)
    for p in range(32):
        v_ref[p, CONV_ROWS:ROWS] = pairs[p * 16 : p * 16 + 16]


def local_kernel(
    nb_ref, cnt_ref, f_ref, prev_ref, next_ref, g_ref, cw_ref, dw_ref, hid_ref, v_ref,
    t_ref, lo_ref, hi_ref, q_ref, w_ref, dt_ref, gexp_ref, cg_ref, dg_ref,
):
    count = cnt_ref[0]
    fill_weights(cw_ref, dw_ref, w_ref, dt_ref)
    fill_tables(f_ref, t_ref, lo_ref, hi_ref)
    fill_halo(prev_ref, next_ref, lo_ref, hi_ref)
    cg_ref[...] = jnp.zeros(cg_ref.shape, F32)
    dg_ref[...] = jnp.zeros(dg_ref.shape, F32)
    for b in range(4):
        fill_inner(nb_ref, count, b, t_ref, q_ref)
        fill_outer(nb_ref, b, lo_ref, hi_ref, q_ref)
        expand_cotangent(g_ref, count, b, gexp_ref)
        block_math(b, w_ref, dt_ref, q_ref, gexp_ref, hid_ref, cg_ref, dg_ref)
    pack(cg_ref, dg_ref, v_ref)


def local_math(features, neighbours, counts, cotangent, conv_weight, down_weight, prev, after):
    return pl.pallas_call(
        local_kernel,
        out_shape=(
            jax.ShapeDtypeStruct((4, 64, 512), BF16),
            jax.ShapeDtypeStruct((32, ROWS, 128), F32),
        ),
        in_specs=[SM, SM, VM, VM, VM, VM, VM, VM],
        out_specs=(VM, VM),
        scratch_shapes=[
            pltpu.VMEM((5, 8, 8, 8, 128), F32),
            pltpu.VMEM((9, 8, 8, 128), F32),
            pltpu.VMEM((9, 8, 8, 128), F32),
            pltpu.VMEM((4, 3, 640, 256), BF16),
            pltpu.VMEM((3, 192, 192), BF16),
            pltpu.VMEM((64, 1024), BF16),
            pltpu.VMEM((1024, 512), BF16),
            pltpu.VMEM((3, 192, 256), F32),
            pltpu.VMEM((1024, 64), F32),
        ],
        compiler_params=pltpu.CompilerParams(vmem_limit_bytes=48 << 20),
        name="local_math",
    )(neighbours, counts, features, prev, after, cotangent, conv_weight, down_weight)


def position():
    s, r = lax.axis_index("space"), lax.axis_index("rep")
    return s // 8, s // 2 % 4, s % 2 * 2 + r // 2, r % 2


def device(z, y, x, core):
    return {"space": z * 8 + y * 2 + x // 2, "rep": x % 2 * 2 + core}


def reduce_kernel(v_ref, o_ref, mate, outgoing, parts, along, gathered, ss, rs, zs, zr, gs, gr, cs, cr):
    z, y, x, core = position()
    me = y * NX + x
    sibling = device(z, y, x, 1 - core)
    plane = [((dy, dx)) for dy in range(NY) for dx in range(NX) if dy or dx]
    plane.sort(key=lambda o: -(min(o[0], NY - o[0]) + min(o[1], NX - o[1])))

    def plane_peer(o):
        py, px = (y + o[0]) % NY, (x + o[1]) % NX
        return device(z, py, px, core), py * NX + px

    def line_peer(dz):
        return device((z + dz) % NZ, y, x, core)

    barrier = pltpu.get_barrier_semaphore()
    greet = [sibling] + [plane_peer(o)[0] for o in plane] + [line_peer(d) for d in range(1, NZ)]
    for d in greet:
        pl.semaphore_signal(barrier, inc=1, device_id=d, device_id_type=MESH)
    pl.semaphore_wait(barrier, len(greet))

    half = pltpu.make_async_remote_copy(
        v_ref.at[pl.ds((1 - core) * NXY, NXY)], mate, cs.at[0], cr.at[0],
        device_id=sibling, device_id_type=MESH,
    )
    half.start()
    half.wait()
    mine = v_ref[pl.ds(core * NXY, NXY)] + mate[...]
    mate[...] = mine
    outgoing[...] = mine.astype(BF16)

    copies = []
    for i, o in enumerate(plane):
        peer, at = plane_peer(o)
        copies.append(
            pltpu.make_async_remote_copy(
                outgoing.at[at], parts.at[i], ss.at[i], rs.at[i],
                device_id=peer, device_id_type=MESH,
            )
        )
        copies[-1].start()
    total = mate[me]
    for i, c in enumerate(copies):
        c.wait_recv()
        total = total + parts[i].astype(F32)
    for c in copies:
        c.wait_send()

    along[z] = total.astype(BF16)
    copies = []
    for i, dz in enumerate((4, 3, 5, 2, 6, 1, 7)):
        copies.append(
            pltpu.make_async_remote_copy(
                along.at[z], along.at[z], zs.at[i], zr.at[i],
                device_id=line_peer(dz), device_id_type=MESH,
            )
        )
        copies[-1].start()
    for c in copies:
        c.wait()
    total = along[0].astype(F32)
    for i in range(1, NZ):
        total = total + along[i].astype(F32)

    gathered[core, me] = total
    copies = []
    for i, o in enumerate(plane):
        peer, _ = plane_peer(o)
        copies.append(
            pltpu.make_async_remote_copy(
                gathered.at[core, me], gathered.at[core, me], gs.at[i], gr.at[i],
                device_id=peer, device_id_type=MESH,
            )
        )
        copies[-1].start()
    for c in copies:
        c.wait()
    rest = pltpu.make_async_remote_copy(
        gathered.at[core], gathered.at[core], cs.at[1], cr.at[1],
        device_id=sibling, device_id_type=MESH,
    )
    rest.start()
    rest.wait()
    o_ref[...] = gathered[...].reshape(o_ref.shape)


def reduce_all(pieces):
    dma = pltpu.SemaphoreType.DMA
    return pl.pallas_call(
        reduce_kernel,
        out_shape=jax.ShapeDtypeStruct((32, ROWS, 128), F32),
        in_specs=[VM],
        out_specs=VM,
        scratch_shapes=[
            pltpu.VMEM((NXY, ROWS, 128), F32),
            pltpu.VMEM((NXY, ROWS, 128), BF16),
            pltpu.VMEM((NXY - 1, ROWS, 128), BF16),
            pltpu.VMEM((NZ, ROWS, 128), BF16),
            pltpu.VMEM((2, NXY, ROWS, 128), F32),
            dma((NXY - 1,)), dma((NXY - 1,)), dma((NZ - 1,)), dma((NZ - 1,)),
            dma((NXY - 1,)), dma((NXY - 1,)), dma((2,)), dma((2,)),
        ],
        compiler_params=pltpu.CompilerParams(
            collective_id=0, has_side_effects=True, vmem_limit_bytes=48 << 20
        ),
        name="reduce_all",
    )(pieces)


def unpack_kernel(v_ref, conv_ref, down_ref):
    conv = v_ref[:, 0:CONV_ROWS].reshape(1024, 128)
    for dy in range(3):
        for dx in range(3):
            at = dy * 192 + dx * 64
            pair = conv[at : at + 64]
            conv_ref[dx * 9 + dy * 3] = pair[:, 0:64]
            conv_ref[dx * 9 + dy * 3 + 1] = pair[:, 64:128]
            at = 768 + dx * 64 if dy == 2 else 576 + dx * 64
            side = 64 if dy == 1 else 0
            conv_ref[dx * 9 + dy * 3 + 2] = conv[at : at + 64, side : side + 64]
    down = v_ref[:, CONV_ROWS:ROWS].reshape(512, 128)
    for t in range(8):
        rows = down[t % 4 * 128 : t % 4 * 128 + 128]
        down_ref[t] = rows[:, t // 4 * 64 : t // 4 * 64 + 64]


def unpack(pieces):
    return pl.pallas_call(
        unpack_kernel,
        out_shape=(
            jax.ShapeDtypeStruct((27, 64, 64), F32),
            jax.ShapeDtypeStruct((8, 128, 64), F32),
        ),
        in_specs=[VM],
        out_specs=(VM, VM),
        name="unpack",
    )(pieces)


def shift_strip(planes, distance):
    n = lax.axis_size("space")
    route = [(i, i + distance) for i in range(n) if 0 <= i + distance < n]
    return lax.ppermute(planes, "space", route)


def body(features, neighbours, counts, cotangent, conv_weight, down_weight):
    prev = shift_strip(features[:, :, 384:], 1)
    after = shift_strip(features[:, :, :128], -1)
    hidden, pieces = local_math(
        features, neighbours, counts, cotangent, conv_weight, down_weight, prev, after
    )
    conv_grad, down_grad = unpack(reduce_all(pieces))
    return hidden, conv_grad, down_grad


def solution(mesh):
    both = ("space", "rep")
    return jax.shard_map(
        body,
        mesh=mesh,
        in_specs=(
            P(both, None, None), P(both, None), P(both), P(both, None, None), P(), P(),
        ),
        out_specs=(P(both, None, None), P(), P()),
        check_vma=False,
    )
```

```python
import jax
import jax.numpy as jnp
from jax import lax
from jax.experimental import pallas as pl
from jax.experimental.pallas import tpu as pltpu
from jax.sharding import PartitionSpec as P

MESH = pl.DeviceIdType.MESH
F32, BF16 = jnp.float32, jnp.bfloat16
VM = pl.BlockSpec(memory_space=pltpu.VMEM)
SM = pl.BlockSpec(memory_space=pltpu.SMEM)
ANY = pl.BlockSpec(memory_space=pl.ANY)
HBM = pl.BlockSpec(memory_space=pltpu.HBM)
NX, NY, NZ = 4, 4, 8
NXY = NX * NY
CONV_ROWS, DOWN_ROWS = 32, 16
ROWS = CONV_ROWS + DOWN_ROWS


def dot(a, b, dims):
    return lax.dot_general(a, b, (dims, ((), ())), preferred_element_type=F32)


NN, NT, TN = ((1,), (0,)), ((1,), (1,)), ((0,), (0,))


def voxels_in_rows(block):
    wide = block.astype(F32)
    return jnp.concatenate([wide, wide], 0).T


def fill_weights(cw_ref, w_ref):
    for dy in range(3):
        for dx in range(3):
            row = [cw_ref[dx * 9 + dy * 3 + dz].astype(F32) for dz in range(3)]
            w_ref[dy, dx * 64 : dx * 64 + 64, :] = jnp.concatenate(row, 1).astype(BF16)


def fill_tables(f_ref, t_ref, lo_ref, hi_ref):
    for j in range(4):
        for q in range(4):
            part = voxels_in_rows(f_ref[j, :, q * 128 : q * 128 + 128])
            t_ref[j, q * 2 : q * 2 + 2] = part.reshape(2, 8, 8, 128)
        lo_ref[j] = t_ref[j, 7]
        hi_ref[j] = t_ref[j, 0]
    t_ref[4] = jnp.zeros((8, 8, 8, 128), F32)
    lo_ref[8] = jnp.zeros((8, 8, 128), F32)
    hi_ref[8] = jnp.zeros((8, 8, 128), F32)


def fill_halo(prev_ref, next_ref, lo_ref, hi_ref):
    for j in range(4):
        lo_ref[4 + j] = voxels_in_rows(prev_ref[j])[64:].reshape(8, 8, 128)
        hi_ref[4 + j] = voxels_in_rows(next_ref[j])[:64].reshape(8, 8, 128)


def store_plane(put, middle, below, above):
    z = lax.broadcasted_iota(jnp.int32, (10, 8, 128), 1)
    first = lax.broadcasted_iota(jnp.int32, (10, 8, 128), 2) < 64
    minus = pltpu.roll(jnp.where(z == 7, below, middle), 1, 1)
    plus = pltpu.roll(jnp.where(z == 0, above, middle), 7, 1)
    left = jnp.where(first, minus, middle)
    for dy in range(3):
        put(dy, 0, left[dy : dy + 8].reshape(64, 128).astype(BF16))
        put(dy, 128, plus[dy : dy + 8].reshape(64, 128).astype(BF16))


def link(nb_ref, b, ox, oy, oz, zero):
    j = nb_ref[b, (ox + 1) * 9 + (oy + 1) * 3 + oz + 1]
    return jnp.where(j < 0, zero, j)


def fill_inner(nb_ref, count, b, t_ref, q_ref):
    own = jnp.where(b < count, b, 4)
    idx = [[link(nb_ref, b, 0, oy, oz, 4) for oy in (-1, 0, 1)] for oz in (0, -1, 1)]
    idx[0][1] = own
    for xp in range(1, 9):
        cols = [
            jnp.concatenate(
                [t_ref[i0, xp - 1, 7:8], t_ref[i1, xp - 1], t_ref[i2, xp - 1, 0:1]], 0
            )
            for i0, i1, i2 in idx
        ]
        row = b * 512 + (xp - 1) * 64

        def put(dy, lane, rows, row=row):
            q_ref[dy, row : row + 64, lane : lane + 128] = rows

        store_plane(put, *cols)


def fill_outer(nb_ref, b, lo_ref, hi_ref, qo_ref):
    for ox, side, table in ((-1, 0, lo_ref), (1, 1, hi_ref)):
        cols = []
        for oz in (0, -1, 1):
            i0, i1, i2 = [link(nb_ref, b, ox, oy, oz, 8) for oy in (-1, 0, 1)]
            cols.append(jnp.concatenate([table[i0, 7:8], table[i1], table[i2, 0:1]], 0))

        def put(dy, lane, rows, side=side):
            qo_ref[dy, side, b * 64 : b * 64 + 64, lane : lane + 128] = rows

        store_plane(put, *cols)


def place_of(shape):
    v = lax.broadcasted_iota(jnp.int32, shape, 1)
    return (v // 64 % 2) * 4 + (v // 8 % 2) * 2 + v % 2


def cell_gradients(g_ref, dw_ref, count, b, up_ref, grad_ref):
    v = lax.broadcasted_iota(jnp.int32, (64, 512), 1)
    u = lax.broadcasted_iota(jnp.int32, (64, 512), 0)
    cell = (v // 128) * 16 + (v // 16 % 4) * 4 + v % 8 // 2
    spread = (cell == u).astype(F32).astype(BF16)
    grads = jnp.where(b < count, g_ref[b].astype(F32), 0.0)
    up = dot(grads.T.astype(BF16), spread, NN).astype(BF16)
    up_ref[:, b * 512 : b * 512 + 512] = up
    every = dot(dw_ref[...].reshape(512, 128), up, NN)
    place = place_of((64, 512))
    grad = every[0:64]
    for t in range(1, 8):
        grad = jnp.where(place == t, every[t * 64 : t * 64 + 64], grad)
    grad_ref[b] = grad


def inner_forward(b, w_ref, q_ref, pre_ref):
    acc = jnp.zeros((192, 512), F32)
    for dy in range(3):
        acc += dot(w_ref[dy], q_ref[dy, b * 512 : b * 512 + 512, 0:192], NT)
    gap = jnp.zeros((64, 64), F32)
    low = jnp.concatenate([gap, acc[0:64, 0:448]], 1)
    high = jnp.concatenate([acc[128:192, 64:512], gap], 1)
    pre_ref[b] = acc[64:128] + low + high


def outer_forward(w_ref, qo_ref):
    low, high = jnp.zeros((64, 256), F32), jnp.zeros((64, 256), F32)
    for dy in range(3):
        low += dot(w_ref[dy, 0:64], qo_ref[dy, 0, :, 0:192], NT)
        high += dot(w_ref[dy, 128:192], qo_ref[dy, 1, :, 0:192], NT)
    return low, high


def finish_block(b, low, high, pre_ref, grad_ref, hid_ref, hexp_ref, sh_ref):
    gap = jnp.zeros((64, 64), F32)
    wide = jnp.zeros((64, 384), F32)
    lanes = slice(b * 64, b * 64 + 64)
    pre = pre_ref[b] + jnp.concatenate([low[:, lanes], wide, high[:, lanes]], 1)
    hidden = jnp.maximum(pre, 0.0)
    hid_ref[b] = hidden.astype(BF16)
    place = place_of((64, 512))
    cols = slice(b * 512, b * 512 + 512)
    for t in range(8):
        hexp_ref[t * 64 : t * 64 + 64, cols] = jnp.where(place == t, hidden, 0.0).astype(BF16)
    act = jnp.where(pre > 0, grad_ref[b], 0.0)
    sh_ref[0:64, cols] = jnp.concatenate([act[:, 64:512], gap], 1).astype(BF16)
    sh_ref[64:128, cols] = act.astype(BF16)
    sh_ref[128:192, cols] = jnp.concatenate([gap, act[:, 0:448]], 1).astype(BF16)
    return act[:, 0:64], act[:, 448:512]


def put_rows(v_ref, at, rows):
    for i in range(0, rows.shape[0], CONV_ROWS):
        p = (at + i) // CONV_ROWS
        v_ref[p // NXY, p % NXY, 0:CONV_ROWS] = rows[i : i + CONV_ROWS]


def kernel_gradients(q_ref, qo_ref, sh_ref, lows, highs, up_ref, hexp_ref, v_ref):
    down = dot(hexp_ref[...], up_ref[...], NT)
    for p in range(2 * NXY):
        v_ref[p // NXY, p % NXY, CONV_ROWS:ROWS] = down[p * 16 : p * 16 + 16]
    low = jnp.concatenate(lows, 1).astype(BF16)
    high = jnp.concatenate(highs, 1).astype(BF16)
    plus = []
    for dy in range(3):
        grads = dot(sh_ref[...], q_ref[dy], NN)
        grads = jnp.concatenate(
            [
                grads[0:64] + dot(low, qo_ref[dy, 0], NN),
                grads[64:128],
                grads[128:192] + dot(high, qo_ref[dy, 1], NN),
            ],
            0,
        )
        put_rows(v_ref, dy * 192, grads[:, 0:128])
        plus.append(grads[:, 128:256])
    first = lax.broadcasted_iota(jnp.int32, (192, 128), 1) < 64
    put_rows(v_ref, 576, jnp.where(first, plus[0], plus[1]))
    put_rows(v_ref, 768, plus[2])
    put_rows(v_ref, 960, jnp.zeros((64, 128), F32))


def position():
    s, r = lax.axis_index("space"), lax.axis_index("rep")
    return s // 8, s // 2 % 4, s % 2 * 2 + r // 2, r % 2


def device(z, y, x, core):
    return {"space": z * 8 + y * 2 + x // 2, "rep": x % 2 * 2 + core}


def section_kernel(
    nb_ref, cnt_ref, f_hbm, g_hbm, cw_hbm, dw_hbm, hid_hbm, o_ref,
    f_ref, g_ref, cw_ref, dw_ref, prev_ref, next_ref, t_ref, lo_ref, hi_ref, q_ref, qo_ref, w_ref,
    up_ref, grad_ref, pre_ref, hid_ref, hexp_ref, sh_ref,
    v_ref, mate, outgoing, parts, along, ls, hs, hr, ss, rs, zs, zr, gs, gr, cs, cr,
):
    z, y, x, core = position()
    me = y * NX + x
    sibling = device(z, y, x, 1 - core)
    plane = [(dy, dx) for dy in range(NY) for dx in range(NX) if dy or dx]
    plane.sort(key=lambda o: -(min(o[0], NY - o[0]) + min(o[1], NX - o[1])))

    def plane_peer(o):
        py, px = (y + o[0]) % NY, (x + o[1]) % NX
        return device(z, py, px, core), py * NX + px

    def line_peer(dz):
        return device((z + dz) % NZ, y, x, core)

    strip, tile = lax.axis_index("space"), lax.axis_index("rep")
    strips = NX // 2 * NY * NZ
    above = {"space": (strip + 1) % strips, "rep": tile}
    below = {"space": (strip + strips - 1) % strips, "rep": tile}

    barrier = pltpu.get_barrier_semaphore()
    greet = [above, below] + [plane_peer(o)[0] for o in plane] + [line_peer(d) for d in range(1, NZ)]
    greet.append(sibling)
    for d in greet:
        pl.semaphore_signal(barrier, inc=1, device_id=d, device_id_type=MESH)
    loads = [
        pltpu.make_async_copy(src, dst, ls.at[i])
        for i, (src, dst) in enumerate(
            ((f_hbm, f_ref), (cw_hbm, cw_ref), (g_hbm, g_ref), (dw_hbm, dw_ref))
        )
    ]
    for c in loads:
        c.start()
    count = cnt_ref[0]

    loads[0].wait()
    fill_tables(f_ref, t_ref, lo_ref, hi_ref)
    pl.semaphore_wait(barrier, len(greet))
    halo = [
        pltpu.make_async_remote_copy(
            f_ref.at[:, :, pl.ds(384, 128)], prev_ref, hs.at[0], hr.at[0],
            device_id=above, device_id_type=MESH,
        ),
        pltpu.make_async_remote_copy(
            f_ref.at[:, :, pl.ds(0, 128)], next_ref, hs.at[1], hr.at[1],
            device_id=below, device_id_type=MESH,
        ),
    ]
    for c in halo:
        c.start()
    loads[1].wait()
    fill_weights(cw_ref, w_ref)
    loads[2].wait()
    loads[3].wait()
    for b in range(4):
        fill_inner(nb_ref, count, b, t_ref, q_ref)
        cell_gradients(g_ref, dw_ref, count, b, up_ref, grad_ref)
        inner_forward(b, w_ref, q_ref, pre_ref)

    for c in halo:
        c.wait()
    fill_halo(prev_ref, next_ref, lo_ref, hi_ref)
    for b in range(4):
        fill_outer(nb_ref, b, lo_ref, hi_ref, qo_ref)
    low, high = outer_forward(w_ref, qo_ref)
    ends = [
        finish_block(b, low, high, pre_ref, grad_ref, hid_ref, hexp_ref, sh_ref)
        for b in range(4)
    ]
    hidden_out = pltpu.make_async_copy(hid_ref, hid_hbm, ls.at[4])
    hidden_out.start()
    kernel_gradients(
        q_ref, qo_ref, sh_ref, [e[0] for e in ends], [e[1] for e in ends], up_ref, hexp_ref, v_ref
    )

    order = [plane_peer(o) for o in plane]
    halves = []
    for i, at in enumerate([at for _, at in order] + [me]):
        halves.append(
            pltpu.make_async_remote_copy(
                v_ref.at[1 - core, at], mate.at[at], cs.at[i], cr.at[i],
                device_id=sibling, device_id_type=MESH,
            )
        )
        halves[-1].start()
    copies = []
    for i, (peer, at) in enumerate(order):
        halves[i].wait_recv()
        outgoing[i] = (v_ref[core, at] + mate[at]).astype(BF16)
        copies.append(
            pltpu.make_async_remote_copy(
                outgoing.at[i], parts.at[i], ss.at[i], rs.at[i],
                device_id=peer, device_id_type=MESH,
            )
        )
        copies[-1].start()
    halves[-1].wait_recv()
    total = v_ref[core, me] + mate[me]
    for i, c in enumerate(copies):
        c.wait_recv()
        total = total + parts[i].astype(F32)

    along[z] = total.astype(BF16)
    lines = []
    for i, dz in enumerate((4, 3, 5, 2, 6, 1, 7)):
        lines.append(
            pltpu.make_async_remote_copy(
                along.at[z], along.at[z], zs.at[i], zr.at[i],
                device_id=line_peer(dz), device_id_type=MESH,
            )
        )
        lines[-1].start()
    for c in halves + copies:
        c.wait_send()
    for c in lines:
        c.wait_recv()
    total = along[0].astype(F32)
    for i in range(1, NZ):
        total = total + along[i].astype(F32)

    half = core * NXY
    o_ref[half + me] = total
    last = []
    for i, (peer, _) in enumerate(order):
        last.append(
            pltpu.make_async_remote_copy(
                o_ref.at[half + me], o_ref.at[half + me], gs.at[i], gr.at[i],
                device_id=peer, device_id_type=MESH,
            )
        )
        last[-1].start()
    for c in lines:
        c.wait_send()
    for c in last:
        c.wait()
    rest = pltpu.make_async_remote_copy(
        o_ref.at[pl.ds(half, NXY)], o_ref.at[pl.ds(half, NXY)], cs.at[NXY], cr.at[NXY],
        device_id=sibling, device_id_type=MESH,
    )
    rest.start()
    rest.wait()
    hidden_out.wait()


def section(features, neighbours, counts, cotangent, conv_weight, down_weight):
    dma = pltpu.SemaphoreType.DMA
    vm = pltpu.VMEM
    near, line = NXY - 1, NZ - 1
    return pl.pallas_call(
        section_kernel,
        out_shape=(
            jax.ShapeDtypeStruct((4, 64, 512), BF16),
            jax.ShapeDtypeStruct((32, ROWS, 128), F32),
        ),
        in_specs=[SM, SM, HBM, HBM, HBM, HBM],
        out_specs=(ANY, VM),
        scratch_shapes=[
            vm((4, 64, 512), BF16), vm((4, 64, 128), BF16), vm((27, 64, 64), BF16), vm((8, 64, 128), BF16),
            vm((4, 64, 128), BF16), vm((4, 64, 128), BF16),
            vm((5, 8, 8, 8, 128), F32), vm((9, 8, 8, 128), F32), vm((9, 8, 8, 128), F32),
            vm((3, 2048, 256), BF16), vm((3, 2, 256, 256), BF16), vm((3, 192, 192), BF16),
            vm((128, 2048), BF16), vm((4, 64, 512), F32), vm((4, 64, 512), F32), vm((4, 64, 512), BF16),
            vm((512, 2048), BF16), vm((192, 2048), BF16),
            vm((2, NXY, ROWS, 128), F32), vm((NXY, ROWS, 128), F32),
            vm((near, ROWS, 128), BF16), vm((near, ROWS, 128), BF16), vm((NZ, ROWS, 128), BF16),
            dma((5,)), dma((2,)), dma((2,)), dma((near,)), dma((near,)), dma((line,)), dma((line,)),
            dma((near,)), dma((near,)), dma((NXY + 1,)), dma((NXY + 1,)),
        ],
        compiler_params=pltpu.CompilerParams(
            collective_id=0, has_side_effects=True, vmem_limit_bytes=48 << 20
        ),
        name="section",
    )(neighbours, counts, features, cotangent, conv_weight, down_weight)


def unpack_kernel(v_ref, hid_hbm, conv_ref, down_ref, out_hbm, sem):
    through = pltpu.make_async_copy(hid_hbm, out_hbm, sem)
    through.start()
    conv = v_ref[:, 0:CONV_ROWS].reshape(1024, 128)
    for dy in range(3):
        for dx in range(3):
            at = dy * 192 + dx * 64
            pair = conv[at : at + 64]
            conv_ref[dx * 9 + dy * 3] = pair[:, 0:64]
            conv_ref[dx * 9 + dy * 3 + 1] = pair[:, 64:128]
            at = 768 + dx * 64 if dy == 2 else 576 + dx * 64
            side = 64 if dy == 1 else 0
            conv_ref[dx * 9 + dy * 3 + 2] = conv[at : at + 64, side : side + 64]
    down_ref[...] = v_ref[:, CONV_ROWS:ROWS].reshape(8, 64, 128)
    through.wait()


def unpack(pieces, hidden):
    return pl.pallas_call(
        unpack_kernel,
        out_shape=(
            jax.ShapeDtypeStruct((27, 64, 64), F32),
            jax.ShapeDtypeStruct((8, 64, 128), F32),
            jax.ShapeDtypeStruct((4, 64, 512), BF16),
        ),
        in_specs=[VM, ANY],
        out_specs=(VM, VM, ANY),
        scratch_shapes=[pltpu.SemaphoreType.DMA],
        compiler_params=pltpu.CompilerParams(vmem_limit_bytes=16 << 20),
        name="unpack",
    )(pieces, hidden)


def body(features, neighbours, counts, cotangent, conv_weight, down_weight):
    down_rows = jnp.swapaxes(down_weight, 1, 2)
    hidden, pieces = section(features, neighbours, counts, cotangent, conv_weight, down_rows)
    conv_grad, down_grad, hidden = unpack(pieces, hidden)
    return hidden, conv_grad, jnp.swapaxes(down_grad, 1, 2)


def solution(mesh):
    both = ("space", "rep")
    return jax.shard_map(
        body,
        mesh=mesh,
        in_specs=(
            P(both, None, None), P(both, None), P(both), P(both, None, None), P(), P(),
        ),
        out_specs=(P(both, None, None), P(), P()),
        check_vma=False,
    )
```

```python
import jax
import jax.numpy as jnp
from jax import lax
from jax.experimental import pallas as pl
from jax.experimental.pallas import tpu as pltpu
from jax.sharding import PartitionSpec as P

MESH = pl.DeviceIdType.MESH
F32, BF16 = jnp.float32, jnp.bfloat16
VM = pl.BlockSpec(memory_space=pltpu.VMEM)
SM = pl.BlockSpec(memory_space=pltpu.SMEM)
ANY = pl.BlockSpec(memory_space=pl.ANY)
NX, NY, NZ = 4, 4, 8
NXY = NX * NY
CONV_ROWS, DOWN_ROWS = 32, 16
ROWS = CONV_ROWS + DOWN_ROWS


def dot(a, b, dims):
    return lax.dot_general(a, b, (dims, ((), ())), preferred_element_type=F32)


NN, NT, TN = ((1,), (0,)), ((1,), (1,)), ((0,), (0,))


def voxels_in_rows(block):
    wide = block.astype(F32)
    return jnp.concatenate([wide, wide], 0).T


def fill_weights(cw_ref, w_ref):
    for dy in range(3):
        for dx in range(3):
            row = [cw_ref[dx * 9 + dy * 3 + dz].astype(F32) for dz in range(3)]
            w_ref[dy, dx * 64 : dx * 64 + 64, :] = jnp.concatenate(row, 1).astype(BF16)


def fill_tables(f_ref, t_ref, lo_ref, hi_ref):
    for j in range(4):
        for q in range(4):
            part = voxels_in_rows(f_ref[j, :, q * 128 : q * 128 + 128])
            t_ref[j, q * 2 : q * 2 + 2] = part.reshape(2, 8, 8, 128)
        lo_ref[j] = t_ref[j, 7]
        hi_ref[j] = t_ref[j, 0]
    t_ref[4] = jnp.zeros((8, 8, 8, 128), F32)
    lo_ref[8] = jnp.zeros((8, 8, 128), F32)
    hi_ref[8] = jnp.zeros((8, 8, 128), F32)


def fill_halo(prev_ref, next_ref, lo_ref, hi_ref):
    for j in range(4):
        lo_ref[4 + j] = voxels_in_rows(prev_ref[j])[64:].reshape(8, 8, 128)
        hi_ref[4 + j] = voxels_in_rows(next_ref[j])[:64].reshape(8, 8, 128)


def store_plane(put, middle, below, above):
    z = lax.broadcasted_iota(jnp.int32, (10, 8, 128), 1)
    first = lax.broadcasted_iota(jnp.int32, (10, 8, 128), 2) < 64
    minus = pltpu.roll(jnp.where(z == 7, below, middle), 1, 1)
    plus = pltpu.roll(jnp.where(z == 0, above, middle), 7, 1)
    left = jnp.where(first, minus, middle)
    for dy in range(3):
        put(dy, 0, left[dy : dy + 8].reshape(64, 128).astype(BF16))
        put(dy, 128, plus[dy : dy + 8].reshape(64, 128).astype(BF16))


def link(nb_ref, b, ox, oy, oz, zero):
    j = nb_ref[b, (ox + 1) * 9 + (oy + 1) * 3 + oz + 1]
    return jnp.where(j < 0, zero, j)


def fill_inner(nb_ref, count, b, t_ref, q_ref):
    own = jnp.where(b < count, b, 4)
    idx = [[link(nb_ref, b, 0, oy, oz, 4) for oy in (-1, 0, 1)] for oz in (0, -1, 1)]
    idx[0][1] = own
    for xp in range(1, 9):
        cols = [
            jnp.concatenate(
                [t_ref[i0, xp - 1, 7:8], t_ref[i1, xp - 1], t_ref[i2, xp - 1, 0:1]], 0
            )
            for i0, i1, i2 in idx
        ]
        row = b * 512 + (xp - 1) * 64

        def put(dy, lane, rows, row=row):
            q_ref[dy, row : row + 64, lane : lane + 128] = rows

        store_plane(put, *cols)


def fill_outer(nb_ref, b, lo_ref, hi_ref, qo_ref):
    for ox, side, table in ((-1, 0, lo_ref), (1, 1, hi_ref)):
        cols = []
        for oz in (0, -1, 1):
            i0, i1, i2 = [link(nb_ref, b, ox, oy, oz, 8) for oy in (-1, 0, 1)]
            cols.append(jnp.concatenate([table[i0, 7:8], table[i1], table[i2, 0:1]], 0))

        def put(dy, lane, rows, side=side):
            qo_ref[dy, side, b * 64 : b * 64 + 64, lane : lane + 128] = rows

        store_plane(put, *cols)


def place_of(shape):
    v = lax.broadcasted_iota(jnp.int32, shape, 1)
    return (v // 64 % 2) * 4 + (v // 8 % 2) * 2 + v % 2


def cell_gradients(g_ref, dw_ref, count, b, up_ref, grad_ref):
    v = lax.broadcasted_iota(jnp.int32, (64, 512), 1)
    u = lax.broadcasted_iota(jnp.int32, (64, 512), 0)
    cell = (v // 128) * 16 + (v // 16 % 4) * 4 + v % 8 // 2
    spread = (cell == u).astype(F32).astype(BF16)
    grads = jnp.where(b < count, g_ref[b].astype(F32), 0.0)
    up = dot(grads.T.astype(BF16), spread, NN).astype(BF16)
    up_ref[:, b * 512 : b * 512 + 512] = up
    every = dot(dw_ref[...].reshape(512, 128), up, NN)
    place = place_of((64, 512))
    grad = every[0:64]
    for t in range(1, 8):
        grad = jnp.where(place == t, every[t * 64 : t * 64 + 64], grad)
    grad_ref[b] = grad


def inner_forward(b, w_ref, q_ref, pre_ref):
    acc = jnp.zeros((192, 512), F32)
    for dy in range(3):
        acc += dot(w_ref[dy], q_ref[dy, b * 512 : b * 512 + 512, 0:192], NT)
    gap = jnp.zeros((64, 64), F32)
    low = jnp.concatenate([gap, acc[0:64, 0:448]], 1)
    high = jnp.concatenate([acc[128:192, 64:512], gap], 1)
    pre_ref[b] = acc[64:128] + low + high


def outer_forward(w_ref, qo_ref):
    low, high = jnp.zeros((64, 256), F32), jnp.zeros((64, 256), F32)
    for dy in range(3):
        low += dot(w_ref[dy, 0:64], qo_ref[dy, 0, :, 0:192], NT)
        high += dot(w_ref[dy, 128:192], qo_ref[dy, 1, :, 0:192], NT)
    return low, high


def finish_block(b, low, high, pre_ref, grad_ref, hid_ref, hexp_ref, sh_ref):
    gap = jnp.zeros((64, 64), F32)
    wide = jnp.zeros((64, 384), F32)
    lanes = slice(b * 64, b * 64 + 64)
    pre = pre_ref[b] + jnp.concatenate([low[:, lanes], wide, high[:, lanes]], 1)
    hidden = jnp.maximum(pre, 0.0)
    hid_ref[b] = hidden.astype(BF16)
    place = place_of((64, 512))
    cols = slice(b * 512, b * 512 + 512)
    for t in range(8):
        hexp_ref[t * 64 : t * 64 + 64, cols] = jnp.where(place == t, hidden, 0.0).astype(BF16)
    act = jnp.where(pre > 0, grad_ref[b], 0.0)
    sh_ref[0:64, cols] = jnp.concatenate([act[:, 64:512], gap], 1).astype(BF16)
    sh_ref[64:128, cols] = act.astype(BF16)
    sh_ref[128:192, cols] = jnp.concatenate([gap, act[:, 0:448]], 1).astype(BF16)
    return act[:, 0:64], act[:, 448:512]


def put_rows(v_ref, at, rows):
    for i in range(0, rows.shape[0], CONV_ROWS):
        p = (at + i) // CONV_ROWS
        v_ref[p // NXY, p % NXY, 0:CONV_ROWS] = rows[i : i + CONV_ROWS]


def kernel_gradients(q_ref, qo_ref, sh_ref, lows, highs, up_ref, hexp_ref, v_ref):
    down = dot(hexp_ref[...], up_ref[...], NT)
    for p in range(2 * NXY):
        v_ref[p // NXY, p % NXY, CONV_ROWS:ROWS] = down[p * 16 : p * 16 + 16]
    low = jnp.concatenate(lows, 1).astype(BF16)
    high = jnp.concatenate(highs, 1).astype(BF16)
    plus = []
    for dy in range(3):
        grads = dot(sh_ref[...], q_ref[dy], NN)
        grads = jnp.concatenate(
            [
                grads[0:64] + dot(low, qo_ref[dy, 0], NN),
                grads[64:128],
                grads[128:192] + dot(high, qo_ref[dy, 1], NN),
            ],
            0,
        )
        put_rows(v_ref, dy * 192, grads[:, 0:128])
        plus.append(grads[:, 128:256])
    first = lax.broadcasted_iota(jnp.int32, (192, 128), 1) < 64
    put_rows(v_ref, 576, jnp.where(first, plus[0], plus[1]))
    put_rows(v_ref, 768, plus[2])
    put_rows(v_ref, 960, jnp.zeros((64, 128), F32))


def position():
    s, r = lax.axis_index("space"), lax.axis_index("rep")
    return s // 8, s // 2 % 4, s % 2 * 2 + r // 2, r % 2


def device(z, y, x, core):
    return {"space": z * 8 + y * 2 + x // 2, "rep": x % 2 * 2 + core}


def section_kernel(
    nb_ref, cnt_ref, f_hbm, g_hbm, cw_hbm, dw_hbm, hid_ref, o_ref,
    f_ref, g_ref, cw_ref, dw_ref, prev_ref, next_ref, t_ref, lo_ref, hi_ref, q_ref, qo_ref, w_ref,
    up_ref, grad_ref, pre_ref, hexp_ref, sh_ref,
    v_ref, mate, outgoing, parts, along, ls, hs, hr, ss, rs, zs, zr, gs, gr, cs, cr,
):
    z, y, x, core = position()
    me = y * NX + x
    sibling = device(z, y, x, 1 - core)
    plane = [(dy, dx) for dy in range(NY) for dx in range(NX) if dy or dx]
    plane.sort(key=lambda o: -(min(o[0], NY - o[0]) + min(o[1], NX - o[1])))

    def plane_peer(o):
        py, px = (y + o[0]) % NY, (x + o[1]) % NX
        return device(z, py, px, core), py * NX + px

    def line_peer(dz):
        return device((z + dz) % NZ, y, x, core)

    strip, tile = lax.axis_index("space"), lax.axis_index("rep")
    strips = NX // 2 * NY * NZ
    above = {"space": (strip + 1) % strips, "rep": tile}
    below = {"space": (strip + strips - 1) % strips, "rep": tile}

    loads = [
        pltpu.make_async_copy(src, dst, ls.at[i])
        for i, (src, dst) in enumerate(
            ((f_hbm, f_ref), (cw_hbm, cw_ref), (g_hbm, g_ref), (dw_hbm, dw_ref))
        )
    ]
    for c in loads:
        c.start()
    barrier = pltpu.get_barrier_semaphore()
    greet = [above, below] + [plane_peer(o)[0] for o in plane] + [line_peer(d) for d in range(1, NZ)]
    greet.append(sibling)
    for d in greet:
        pl.semaphore_signal(barrier, inc=1, device_id=d, device_id_type=MESH)
    count = cnt_ref[0]

    loads[0].wait()
    fill_tables(f_ref, t_ref, lo_ref, hi_ref)
    pl.semaphore_wait(barrier, len(greet))
    halo = [
        pltpu.make_async_remote_copy(
            f_ref.at[:, :, pl.ds(384, 128)], prev_ref, hs.at[0], hr.at[0],
            device_id=above, device_id_type=MESH,
        ),
        pltpu.make_async_remote_copy(
            f_ref.at[:, :, pl.ds(0, 128)], next_ref, hs.at[1], hr.at[1],
            device_id=below, device_id_type=MESH,
        ),
    ]
    for c in halo:
        c.start()
    loads[1].wait()
    fill_weights(cw_ref, w_ref)
    loads[2].wait()
    loads[3].wait()
    for b in range(4):
        fill_inner(nb_ref, count, b, t_ref, q_ref)
        cell_gradients(g_ref, dw_ref, count, b, up_ref, grad_ref)
        inner_forward(b, w_ref, q_ref, pre_ref)

    for c in halo:
        c.wait()
    fill_halo(prev_ref, next_ref, lo_ref, hi_ref)
    for b in range(4):
        fill_outer(nb_ref, b, lo_ref, hi_ref, qo_ref)
    low, high = outer_forward(w_ref, qo_ref)
    ends = [
        finish_block(b, low, high, pre_ref, grad_ref, hid_ref, hexp_ref, sh_ref)
        for b in range(4)
    ]
    kernel_gradients(
        q_ref, qo_ref, sh_ref, [e[0] for e in ends], [e[1] for e in ends], up_ref, hexp_ref, v_ref
    )

    order = [plane_peer(o) for o in plane]
    halves = []
    for i, at in enumerate([at for _, at in order] + [me]):
        halves.append(
            pltpu.make_async_remote_copy(
                v_ref.at[1 - core, at], mate.at[at], cs.at[i], cr.at[i],
                device_id=sibling, device_id_type=MESH,
            )
        )
        halves[-1].start()
    copies = []
    for i, (peer, at) in enumerate(order):
        halves[i].wait_recv()
        outgoing[i] = (v_ref[core, at] + mate[at]).astype(BF16)
        copies.append(
            pltpu.make_async_remote_copy(
                outgoing.at[i], parts.at[i], ss.at[i], rs.at[i],
                device_id=peer, device_id_type=MESH,
            )
        )
        copies[-1].start()
    halves[-1].wait_recv()
    total = v_ref[core, me] + mate[me]
    for i, c in enumerate(copies):
        c.wait_recv()
        total = total + parts[i].astype(F32)

    along[z] = total.astype(BF16)
    lines = []
    for i, dz in enumerate((4, 3, 5, 2, 6, 1, 7)):
        lines.append(
            pltpu.make_async_remote_copy(
                along.at[z], along.at[z], zs.at[i], zr.at[i],
                device_id=line_peer(dz), device_id_type=MESH,
            )
        )
        lines[-1].start()
    for c in halves + copies:
        c.wait_send()
    for c in lines:
        c.wait_recv()
    total = along[0].astype(F32)
    for i in range(1, NZ):
        total = total + along[i].astype(F32)

    half = core * NXY
    o_ref[half + me] = total
    last = []
    for i, (peer, _) in enumerate(order):
        last.append(
            pltpu.make_async_remote_copy(
                o_ref.at[half + me], o_ref.at[half + me], gs.at[i], gr.at[i],
                device_id=peer, device_id_type=MESH,
            )
        )
        last[-1].start()
    for c in lines:
        c.wait_send()
    for c in last:
        c.wait()
    rest = pltpu.make_async_remote_copy(
        o_ref.at[pl.ds(half, NXY)], o_ref.at[pl.ds(half, NXY)], cs.at[NXY], cr.at[NXY],
        device_id=sibling, device_id_type=MESH,
    )
    rest.start()
    rest.wait()


def section(features, neighbours, counts, cotangent, conv_weight, down_weight):
    dma = pltpu.SemaphoreType.DMA
    vm = pltpu.VMEM
    near, line = NXY - 1, NZ - 1
    return pl.pallas_call(
        section_kernel,
        out_shape=(
            pltpu.VMEM((4, 64, 512), BF16),
            pltpu.VMEM((32, ROWS, 128), F32),
        ),
        in_specs=[SM, SM, ANY, ANY, ANY, ANY],
        out_specs=(VM, VM),
        scratch_shapes=[
            vm((4, 64, 512), BF16), vm((4, 64, 128), BF16), vm((27, 64, 64), BF16), vm((8, 64, 128), BF16),
            vm((4, 64, 128), BF16), vm((4, 64, 128), BF16),
            vm((5, 8, 8, 8, 128), F32), vm((9, 8, 8, 128), F32), vm((9, 8, 8, 128), F32),
            vm((3, 2048, 256), BF16), vm((3, 2, 256, 256), BF16), vm((3, 192, 192), BF16),
            vm((128, 2048), BF16), vm((4, 64, 512), F32), vm((4, 64, 512), F32),
            vm((512, 2048), BF16), vm((192, 2048), BF16),
            vm((2, NXY, ROWS, 128), F32), vm((NXY, ROWS, 128), F32),
            vm((near, ROWS, 128), BF16), vm((near, ROWS, 128), BF16), vm((NZ, ROWS, 128), BF16),
            dma((4,)), dma((2,)), dma((2,)), dma((near,)), dma((near,)), dma((line,)), dma((line,)),
            dma((near,)), dma((near,)), dma((NXY + 1,)), dma((NXY + 1,)),
        ],
        compiler_params=pltpu.CompilerParams(
            collective_id=0, has_side_effects=True, vmem_limit_bytes=56 << 20
        ),
        name="section",
    )(neighbours, counts, features, cotangent, conv_weight, down_weight)


def unpack_kernel(v_ref, hid_ref, conv_hbm, down_hbm, hid_hbm, conv_ref, sem):
    moves = [
        pltpu.make_async_copy(v_ref.at[:, pl.ds(CONV_ROWS, DOWN_ROWS), :], down_hbm, sem.at[0]),
        pltpu.make_async_copy(hid_ref, hid_hbm, sem.at[1]),
    ]
    for m in moves:
        m.start()
    conv = v_ref[:, 0:CONV_ROWS].reshape(1024, 128)
    for dx in range(3):
        for dy in range(3):
            at = dy * 192 + dx * 64
            pair = conv[at : at + 64]
            conv_ref[dx * 9 + dy * 3] = pair[:, 0:64]
            conv_ref[dx * 9 + dy * 3 + 1] = pair[:, 64:128]
            at = 768 + dx * 64 if dy == 2 else 576 + dx * 64
            side = 64 if dy == 1 else 0
            conv_ref[dx * 9 + dy * 3 + 2] = conv[at : at + 64, side : side + 64]
        part = pl.ds(dx * 9, 9)
        moves.append(
            pltpu.make_async_copy(conv_ref.at[part], conv_hbm.at[part], sem.at[2 + dx])
        )
        moves[-1].start()
    for m in moves:
        m.wait()


def unpack(pieces, hidden):
    return pl.pallas_call(
        unpack_kernel,
        out_shape=(
            jax.ShapeDtypeStruct((27, 64, 64), F32),
            jax.ShapeDtypeStruct((32, DOWN_ROWS, 128), F32),
            jax.ShapeDtypeStruct((4, 64, 512), BF16),
        ),
        in_specs=[VM, VM],
        out_specs=(ANY, ANY, ANY),
        scratch_shapes=[pltpu.VMEM((27, 64, 64), F32), pltpu.SemaphoreType.DMA((5,))],
        compiler_params=pltpu.CompilerParams(vmem_limit_bytes=48 << 20),
        name="unpack",
    )(pieces, hidden)


def body(features, neighbours, counts, cotangent, conv_weight, down_weight):
    down_rows = jnp.swapaxes(down_weight, 1, 2)
    hidden, pieces = section(features, neighbours, counts, cotangent, conv_weight, down_rows)
    conv_grad, down_grad, hidden = unpack(pieces, hidden)
    return hidden, conv_grad, jnp.swapaxes(down_grad.reshape(8, 64, 128), 1, 2)


def solution(mesh):
    both = ("space", "rep")
    return jax.shard_map(
        body,
        mesh=mesh,
        in_specs=(
            P(both, None, None), P(both, None), P(both), P(both, None, None), P(), P(),
        ),
        out_specs=(P(both, None, None), P(), P()),
        check_vma=False,
    )
```

```python
import jax
import jax.numpy as jnp
from jax import lax
from jax.experimental import pallas as pl
from jax.experimental.pallas import tpu as pltpu
from jax.sharding import PartitionSpec as P

MESH = pl.DeviceIdType.MESH
F32, BF16 = jnp.float32, jnp.bfloat16
VM = pl.BlockSpec(memory_space=pltpu.VMEM)
SM = pl.BlockSpec(memory_space=pltpu.SMEM)
ANY = pl.BlockSpec(memory_space=pl.ANY)
NX, NY, NZ = 4, 4, 8
NXY = NX * NY
CONV_ROWS, DOWN_ROWS = 32, 16
ROWS = CONV_ROWS + DOWN_ROWS


def dot(a, b, dims):
    return lax.dot_general(a, b, (dims, ((), ())), preferred_element_type=F32)


NN, NT, TN = ((1,), (0,)), ((1,), (1,)), ((0,), (0,))


def voxels_in_rows(block):
    wide = block.astype(F32)
    return jnp.concatenate([wide, wide], 0).T


def fill_weights(cw_ref, w_ref):
    for dy in range(3):
        for dx in range(3):
            row = [cw_ref[dx * 9 + dy * 3 + dz].astype(F32) for dz in range(3)]
            w_ref[dy, dx * 64 : dx * 64 + 64, :] = jnp.concatenate(row, 1).astype(BF16)


def fill_tables(f_ref, t_ref, lo_ref, hi_ref):
    for j in range(4):
        for q in range(4):
            part = voxels_in_rows(f_ref[j, :, q * 128 : q * 128 + 128])
            t_ref[j, q * 2 : q * 2 + 2] = part.reshape(2, 8, 8, 128)
        lo_ref[j] = t_ref[j, 7]
        hi_ref[j] = t_ref[j, 0]
    t_ref[4] = jnp.zeros((8, 8, 8, 128), F32)
    lo_ref[8] = jnp.zeros((8, 8, 128), F32)
    hi_ref[8] = jnp.zeros((8, 8, 128), F32)


def fill_halo(prev_ref, next_ref, lo_ref, hi_ref):
    for j in range(4):
        lo_ref[4 + j] = voxels_in_rows(prev_ref[j])[64:].reshape(8, 8, 128)
        hi_ref[4 + j] = voxels_in_rows(next_ref[j])[:64].reshape(8, 8, 128)


def store_plane(put, middle, below, above):
    z = lax.broadcasted_iota(jnp.int32, (10, 8, 128), 1)
    first = lax.broadcasted_iota(jnp.int32, (10, 8, 128), 2) < 64
    minus = pltpu.roll(jnp.where(z == 7, below, middle), 1, 1)
    plus = pltpu.roll(jnp.where(z == 0, above, middle), 7, 1)
    left = jnp.where(first, minus, middle)
    for dy in range(3):
        put(dy, 0, left[dy : dy + 8].reshape(64, 128).astype(BF16))
        put(dy, 128, plus[dy : dy + 8].reshape(64, 128).astype(BF16))


def link(nb_ref, b, ox, oy, oz, zero):
    j = nb_ref[b, (ox + 1) * 9 + (oy + 1) * 3 + oz + 1]
    return jnp.where(j < 0, zero, j)


def fill_inner(nb_ref, count, b, t_ref, q_ref, qe_ref):
    own = jnp.where(b < count, b, 4)
    idx = [[link(nb_ref, b, 0, oy, oz, 4) for oy in (-1, 0, 1)] for oz in (0, -1, 1)]
    idx[0][1] = own
    for xp in range(1, 9):
        cols = [
            jnp.concatenate(
                [t_ref[i0, xp - 1, 7:8], t_ref[i1, xp - 1], t_ref[i2, xp - 1, 0:1]], 0
            )
            for i0, i1, i2 in idx
        ]
        row, edge = b * 512 + (xp - 1) * 64, b * 64

        def put(dy, lane, rows, row=row, edge=edge, xp=xp):
            q_ref[dy, row : row + 64, lane : lane + 128] = rows
            if xp in (1, 2):
                qe_ref[dy, xp, edge : edge + 64, lane : lane + 128] = rows
            if xp in (7, 8):
                qe_ref[dy, xp - 7, 256 + edge : 320 + edge, lane : lane + 128] = rows

        store_plane(put, *cols)


def fill_outer(nb_ref, b, lo_ref, hi_ref, qe_ref):
    for ox, side, table in ((-1, 0, lo_ref), (1, 1, hi_ref)):
        cols = []
        for oz in (0, -1, 1):
            i0, i1, i2 = [link(nb_ref, b, ox, oy, oz, 8) for oy in (-1, 0, 1)]
            cols.append(jnp.concatenate([table[i0, 7:8], table[i1], table[i2, 0:1]], 0))

        row = side * 256 + b * 64

        def put(dy, lane, rows, side=side, row=row):
            qe_ref[dy, 2 * side, row : row + 64, lane : lane + 128] = rows

        store_plane(put, *cols)


def place_of(shape):
    v = lax.broadcasted_iota(jnp.int32, shape, 1)
    return (v // 64 % 2) * 4 + (v // 8 % 2) * 2 + v % 2


def cell_gradients(g_ref, dw_ref, count, b, up_ref, grad_ref):
    v = lax.broadcasted_iota(jnp.int32, (64, 512), 1)
    u = lax.broadcasted_iota(jnp.int32, (64, 512), 0)
    cell = (v // 128) * 16 + (v // 16 % 4) * 4 + v % 8 // 2
    spread = (cell == u).astype(F32).astype(BF16)
    grads = jnp.where(b < count, g_ref[b].astype(F32), 0.0)
    up = dot(grads.T.astype(BF16), spread, NN).astype(BF16)
    up_ref[:, b * 512 : b * 512 + 512] = up
    every = dot(dw_ref[...].reshape(512, 128), up, NN)
    place = place_of((64, 512))
    grad = every[0:64]
    for t in range(1, 8):
        grad = jnp.where(place == t, every[t * 64 : t * 64 + 64], grad)
    grad_ref[b] = grad


def inner_forward(b, w_ref, q_ref, pre_ref):
    acc = jnp.zeros((192, 512), F32)
    for dy in range(3):
        acc += dot(w_ref[dy], q_ref[dy, b * 512 : b * 512 + 512, 0:192], NT)
    gap = jnp.zeros((64, 64), F32)
    low = jnp.concatenate([gap, acc[0:64, 0:448]], 1)
    high = jnp.concatenate([acc[128:192, 64:512], gap], 1)
    pre_ref[b] = acc[64:128] + low + high


def outer_forward(w_ref, qe_ref):
    low, high = jnp.zeros((64, 256), F32), jnp.zeros((64, 256), F32)
    for dy in range(3):
        low += dot(w_ref[dy, 0:64], qe_ref[dy, 0, 0:256, 0:192], NT)
        high += dot(w_ref[dy, 128:192], qe_ref[dy, 2, 256:512, 0:192], NT)
    return low, high


def inner_block(b, pre_ref, grad_ref, hid_ref, hexp_ref, sh_ref):
    lane = lax.broadcasted_iota(jnp.int32, (64, 512), 1)
    inside = (lane >= 64) & (lane < 448)
    gap = jnp.zeros((64, 64), F32)
    pre = jnp.where(inside, pre_ref[b], 0.0)
    hidden = jnp.maximum(pre, 0.0)
    hid_ref[b] = hidden.astype(BF16)
    place = place_of((64, 512))
    cols = slice(b * 512, b * 512 + 512)
    for t in range(8):
        hexp_ref[t * 64 : t * 64 + 64, cols] = jnp.where(place == t, hidden, 0.0).astype(BF16)
    act = jnp.where(pre > 0, grad_ref[b], 0.0)
    sh_ref[0:64, cols] = jnp.concatenate([act[:, 64:512], gap], 1).astype(BF16)
    sh_ref[64:128, cols] = act.astype(BF16)
    sh_ref[128:192, cols] = jnp.concatenate([gap, act[:, 0:448]], 1).astype(BF16)


def edge_lanes(side):
    return slice(448, 512) if side else slice(0, 64)


def stash_edges(pre_ref, grad_ref, up_ref, pe_ref, ge_ref, ue_ref):
    for side in range(2):
        at = edge_lanes(side)
        pe_ref[side] = jnp.concatenate([pre_ref[b, :, at] for b in range(4)], 1)
        ge_ref[side] = jnp.concatenate([grad_ref[b, :, at] for b in range(4)], 1)
        ups = [up_ref[:, b * 512 + at.start : b * 512 + at.stop].astype(F32) for b in range(4)]
        ue_ref[side] = jnp.concatenate(ups, 1).astype(BF16)


def edge_planes(sums, pe_ref, ge_ref, ue_ref, hid_ref, dg_ref, down_ref):
    v = lax.broadcasted_iota(jnp.int32, (64, 256), 1)
    place = (v // 8 % 2) * 2 + v % 2
    first = lax.broadcasted_iota(jnp.int32, (64, 128), 1) < 64
    acts = []
    for side in range(2):
        pre = pe_ref[side] + sums[side]
        hidden = jnp.maximum(pre, 0.0)
        acts.append(jnp.where(pre > 0, ge_ref[side], 0.0))
        spread = jnp.concatenate([jnp.where(place == t, hidden, 0.0) for t in range(4)], 0)
        down = dg_ref[side * 256 : side * 256 + 256] + dot(spread.astype(BF16), ue_ref[side], NT)
        for p in range(NXY):
            down_ref[side, p] = down[p * 16 : p * 16 + 16]
        tile = slice(384, 512) if side else slice(0, 128)
        for b in range(4):
            mine = hidden[:, b // 2 * 128 : b // 2 * 128 + 128]
            if b % 2 != side:
                mine = pltpu.roll(mine, 64, 1)
            old = hid_ref[b, :, tile].astype(F32)
            hid_ref[b, :, tile] = jnp.where(first != (side == 1), mine, old).astype(BF16)
    return jnp.concatenate(acts, 1).astype(BF16)


def put_rows(v_ref, at, rows):
    for i in range(0, rows.shape[0], CONV_ROWS):
        p = (at + i) // CONV_ROWS
        v_ref[p // NXY, p % NXY] = rows[i : i + CONV_ROWS]


def conv_gradient(acts, qe_ref, cg_ref, conv_ref):
    plus = []
    for dy in range(3):
        parts = [
            cg_ref[dy, dx * 64 : dx * 64 + 64] + dot(acts, qe_ref[dy, dx], NN) for dx in range(3)
        ]
        grads = jnp.concatenate(parts, 0)
        put_rows(conv_ref, dy * 192, grads[:, 0:128])
        plus.append(grads[:, 128:256])
    first = lax.broadcasted_iota(jnp.int32, (192, 128), 1) < 64
    put_rows(conv_ref, 576, jnp.where(first, plus[0], plus[1]))
    put_rows(conv_ref, 768, plus[2])
    put_rows(conv_ref, 960, jnp.zeros((64, 128), F32))


def remote(src, dst, send, recv, peer):
    return pltpu.make_async_remote_copy(
        src, dst, send, recv, device_id=peer, device_id_type=MESH
    )


def section_kernel(
    nb_ref, cnt_ref, f_hbm, g_hbm, cw_hbm, dw_hbm, hid_ref, o_ref,
    f_ref, g_ref, cw_ref, dw_ref, prev_ref, next_ref, t_ref, lo_ref, hi_ref, q_ref, qe_ref, w_ref,
    up_ref, grad_ref, pre_ref, hexp_ref, sh_ref, pe_ref, ge_ref, ue_ref, dg_ref, cg_ref,
    conv_ref, down_ref, mate_conv, mate_down, outgoing, parts, along,
    ls, hs, hr, cs, cr, ss, rs, zs, zr, gs, gr, es, er,
):
    strip, tile = lax.axis_index("space"), lax.axis_index("rep")
    z, rest = lax.div(strip, 8), lax.rem(strip, 8)
    y, x_hi = lax.div(rest, 2), lax.rem(rest, 2)
    x_lo, core = lax.div(tile, 2), lax.rem(tile, 2)
    x = x_hi * 2 + x_lo
    me = y * NX + x
    sibling = {"space": strip, "rep": x_lo * 2 + 1 - core}

    ys = [y] + [lax.rem(y + d, NY) for d in range(1, NY)]
    xs = [x] + [lax.rem(x + d, NX) for d in range(1, NX)]
    x_his = [lax.div(v, 2) for v in xs]
    tiles = [lax.rem(v, 2) * 2 + core for v in xs]
    rows = [z * 8 + v * 2 for v in ys]
    slots = [v * NX for v in ys]
    plane = [(dy, dx) for dy in range(NY) for dx in range(NX) if dy or dx]
    plane.sort(key=lambda o: -(min(o[0], NY - o[0]) + min(o[1], NX - o[1])))
    peers = {
        (dy, dx): ({"space": rows[dy] + x_his[dx], "rep": tiles[dx]}, slots[dy] + xs[dx])
        for dy, dx in plane
    }
    order = [peers[o] for o in plane]
    line = [{"space": lax.rem(z + d, NZ) * 8 + rest, "rep": tile} for d in (4, 3, 5, 2, 6, 1, 7)]
    strips = NX // 2 * NY * NZ
    above = {"space": lax.rem(strip + 1, strips), "rep": tile}
    below = {"space": lax.rem(strip + strips - 1, strips), "rep": tile}

    loads = [
        pltpu.make_async_copy(src, dst, ls.at[i])
        for i, (src, dst) in enumerate(
            ((f_hbm, f_ref), (cw_hbm, cw_ref), (g_hbm, g_ref), (dw_hbm, dw_ref))
        )
    ]
    for c in loads:
        c.start()
    barrier = pltpu.get_barrier_semaphore()
    greet = [above, below] + [peer for peer, _ in order] + line + [sibling]
    for d in greet:
        pl.semaphore_signal(barrier, inc=1, device_id=d, device_id_type=MESH)
    count = cnt_ref[0]

    loads[0].wait()
    fill_tables(f_ref, t_ref, lo_ref, hi_ref)
    pl.semaphore_wait(barrier, len(greet))
    halo = [
        pltpu.make_async_remote_copy(
            f_ref.at[:, :, pl.ds(384, 128)], prev_ref, hs.at[0], hr.at[0],
            device_id=above, device_id_type=MESH,
        ),
        pltpu.make_async_remote_copy(
            f_ref.at[:, :, pl.ds(0, 128)], next_ref, hs.at[1], hr.at[1],
            device_id=below, device_id_type=MESH,
        ),
    ]
    for c in halo:
        c.start()
    loads[1].wait()
    fill_weights(cw_ref, w_ref)
    loads[2].wait()
    loads[3].wait()
    for b in range(4):
        fill_inner(nb_ref, count, b, t_ref, q_ref, qe_ref)
        cell_gradients(g_ref, dw_ref, count, b, up_ref, grad_ref)
        inner_forward(b, w_ref, q_ref, pre_ref)
        inner_block(b, pre_ref, grad_ref, hid_ref, hexp_ref, sh_ref)
    stash_edges(pre_ref, grad_ref, up_ref, pe_ref, ge_ref, ue_ref)
    dg_ref[...] = dot(hexp_ref[...], up_ref[...], NT)
    for dy in range(3):
        cg_ref[dy] = dot(sh_ref[...], q_ref[dy], NN)

    for c in halo:
        c.wait()
    fill_halo(prev_ref, next_ref, lo_ref, hi_ref)
    for b in range(4):
        fill_outer(nb_ref, b, lo_ref, hi_ref, qe_ref)
    sums = outer_forward(w_ref, qe_ref)

    acts = edge_planes(sums, pe_ref, ge_ref, ue_ref, hid_ref, dg_ref, down_ref)
    swap_down = remote(down_ref.at[1 - core], mate_down, cs.at[0], cr.at[0], sibling)
    swap_down.start()
    conv_gradient(acts, qe_ref, cg_ref, conv_ref)
    swap_conv = remote(conv_ref.at[1 - core], mate_conv, cs.at[1], cr.at[1], sibling)
    swap_conv.start()

    def summed(at):
        return (
            conv_ref[core, at] + mate_conv[at],
            down_ref[core, at] + mate_down[at],
        )

    swap_down.wait_recv()
    swap_conv.wait_recv()
    copies = []
    for i, (peer, at) in enumerate(order):
        conv, down = summed(at)
        outgoing[i, 0:CONV_ROWS] = conv.astype(BF16)
        outgoing[i, CONV_ROWS:ROWS] = down.astype(BF16)
        copies.append(remote(outgoing.at[i], parts.at[i], ss.at[i], rs.at[i], peer))
        copies[-1].start()
    total = jnp.concatenate(summed(me), 0)
    for i in reversed(range(NXY - 1)):
        copies[i].wait_recv()
        total = total + parts[i].astype(F32)

    along[z] = total.astype(BF16)
    lines = []
    for i, peer in enumerate(line):
        lines.append(remote(along.at[z], along.at[z], zs.at[i], zr.at[i], peer))
        lines[-1].start()
    for c in [swap_down, swap_conv] + copies:
        c.wait_send()
    for c in lines:
        c.wait_recv()
    total = along[0].astype(F32)
    for i in range(1, NZ):
        total = total + along[i].astype(F32)

    half = core * NXY
    own = o_ref.at[half + me]
    o_ref[half + me] = total
    last = []
    for i, (peer, _) in enumerate(order):
        last.append(remote(own, own, gs.at[i], gr.at[i], peer))
        last[-1].start()
    shared = [remote(own, own, es.at[NXY - 1], er.at[NXY - 1], sibling)]
    shared[0].start()
    for c in lines:
        c.wait_send()
    for i in reversed(range(NXY - 1)):
        last[i].wait_recv()
        _, at = peers[-plane[i][0] % NY, -plane[i][1] % NX]
        piece = o_ref.at[half + at]
        shared.append(remote(piece, piece, es.at[i], er.at[i], sibling))
        shared[-1].start()
    for c in last:
        c.wait_send()
    for c in shared:
        c.wait()


def section(features, neighbours, counts, cotangent, conv_weight, down_weight):
    dma = pltpu.SemaphoreType.DMA
    vm = pltpu.VMEM
    near, line = NXY - 1, NZ - 1

    return pl.pallas_call(
        section_kernel,
        out_shape=(
            pltpu.VMEM((4, 64, 512), BF16),
            pltpu.VMEM((32, ROWS, 128), F32),
        ),
        in_specs=[SM, SM, ANY, ANY, ANY, ANY],
        out_specs=(VM, VM),
        scratch_shapes=[
            vm((4, 64, 512), BF16), vm((4, 64, 128), BF16), vm((27, 64, 64), BF16), vm((8, 64, 128), BF16),
            vm((4, 64, 128), BF16), vm((4, 64, 128), BF16),
            vm((5, 8, 8, 8, 128), F32), vm((9, 8, 8, 128), F32), vm((9, 8, 8, 128), F32),
            vm((3, 2048, 256), BF16), vm((3, 3, 512, 256), BF16), vm((3, 192, 192), BF16),
            vm((128, 2048), BF16), vm((4, 64, 512), F32), vm((4, 64, 512), F32),
            vm((512, 2048), BF16), vm((192, 2048), BF16),
            vm((2, 64, 256), F32), vm((2, 64, 256), F32), vm((2, 128, 256), BF16),
            vm((512, 128), F32), vm((3, 192, 256), F32),
            vm((2, NXY, CONV_ROWS, 128), F32), vm((2, NXY, DOWN_ROWS, 128), F32),
            vm((NXY, CONV_ROWS, 128), F32), vm((NXY, DOWN_ROWS, 128), F32),
            vm((near, ROWS, 128), BF16), vm((near, ROWS, 128), BF16), vm((NZ, ROWS, 128), BF16),
            dma((4,)), dma((2,)), dma((2,)), dma((2,)), dma((2,)), dma((near,)), dma((near,)),
            dma((line,)), dma((line,)), dma((near,)), dma((near,)), dma((NXY,)), dma((NXY,)),
        ],
        compiler_params=pltpu.CompilerParams(
            collective_id=0, has_side_effects=True, vmem_limit_bytes=56 << 20
        ),
        name="section",
    )(neighbours, counts, features, cotangent, conv_weight, down_weight)


def unpack_kernel(v_ref, hid_ref, conv_hbm, down_hbm, hid_hbm, conv_ref, sem):
    moves = [
        pltpu.make_async_copy(v_ref.at[:, pl.ds(CONV_ROWS, DOWN_ROWS), :], down_hbm, sem.at[0]),
        pltpu.make_async_copy(hid_ref, hid_hbm, sem.at[1]),
    ]
    for m in moves:
        m.start()
    conv = v_ref[:, 0:CONV_ROWS].reshape(1024, 128)
    for dx in range(3):
        for dy in range(3):
            at = dy * 192 + dx * 64
            pair = conv[at : at + 64]
            conv_ref[dx * 9 + dy * 3] = pair[:, 0:64]
            conv_ref[dx * 9 + dy * 3 + 1] = pair[:, 64:128]
            at = 768 + dx * 64 if dy == 2 else 576 + dx * 64
            side = 64 if dy == 1 else 0
            conv_ref[dx * 9 + dy * 3 + 2] = conv[at : at + 64, side : side + 64]
        part = pl.ds(dx * 9, 9)
        moves.append(
            pltpu.make_async_copy(conv_ref.at[part], conv_hbm.at[part], sem.at[2 + dx])
        )
        moves[-1].start()
    for m in moves:
        m.wait()


def unpack(pieces, hidden):
    return pl.pallas_call(
        unpack_kernel,
        out_shape=(
            jax.ShapeDtypeStruct((27, 64, 64), F32),
            jax.ShapeDtypeStruct((32, DOWN_ROWS, 128), F32),
            jax.ShapeDtypeStruct((4, 64, 512), BF16),
        ),
        in_specs=[VM, VM],
        out_specs=(ANY, ANY, ANY),
        scratch_shapes=[pltpu.VMEM((27, 64, 64), F32), pltpu.SemaphoreType.DMA((5,))],
        compiler_params=pltpu.CompilerParams(vmem_limit_bytes=48 << 20),
        name="unpack",
    )(pieces, hidden)


def body(features, neighbours, counts, cotangent, conv_weight, down_weight):
    down_rows = jnp.swapaxes(down_weight, 1, 2)
    hidden, pieces = section(features, neighbours, counts, cotangent, conv_weight, down_rows)
    conv_grad, down_grad, hidden = unpack(pieces, hidden)
    return hidden, conv_grad, jnp.swapaxes(down_grad.reshape(8, 64, 128), 1, 2)


def solution(mesh):
    both = ("space", "rep")
    return jax.shard_map(
        body,
        mesh=mesh,
        in_specs=(
            P(both, None, None), P(both, None), P(both), P(both, None, None), P(), P(),
        ),
        out_specs=(P(both, None, None), P(), P()),
        check_vma=False,
    )
```

```python
import jax
import jax.numpy as jnp
from jax import lax
from jax.experimental import pallas as pl
from jax.experimental.pallas import tpu as pltpu
from jax.sharding import PartitionSpec as P

MESH = pl.DeviceIdType.MESH
F32, BF16 = jnp.float32, jnp.bfloat16
VM = pl.BlockSpec(memory_space=pltpu.VMEM)
SM = pl.BlockSpec(memory_space=pltpu.SMEM)
ANY = pl.BlockSpec(memory_space=pl.ANY)
NX, NY, NZ = 4, 4, 8
NXY = NX * NY
CONV_ROWS, DOWN_ROWS = 32, 16
ROWS = CONV_ROWS + DOWN_ROWS


def dot(a, b, dims):
    return lax.dot_general(a, b, (dims, ((), ())), preferred_element_type=F32)


NN, NT, TN = ((1,), (0,)), ((1,), (1,)), ((0,), (0,))


def voxels_in_rows(block):
    wide = block.astype(F32)
    return jnp.concatenate([wide, wide], 0).T


def fill_weights(cw_ref, w_ref):
    for dy in range(3):
        for dx in range(3):
            row = [cw_ref[dx * 9 + dy * 3 + dz].astype(F32) for dz in range(3)]
            w_ref[dy, dx * 64 : dx * 64 + 64, :] = jnp.concatenate(row, 1).astype(BF16)


def fill_tables(f_ref, t_ref, lo_ref, hi_ref):
    for j in range(4):
        for q in range(4):
            part = voxels_in_rows(f_ref[j, :, q * 128 : q * 128 + 128])
            t_ref[j, q * 2 : q * 2 + 2] = part.reshape(2, 8, 8, 128)
        lo_ref[j] = t_ref[j, 7]
        hi_ref[j] = t_ref[j, 0]
    t_ref[4] = jnp.zeros((8, 8, 8, 128), F32)
    lo_ref[8] = jnp.zeros((8, 8, 128), F32)
    hi_ref[8] = jnp.zeros((8, 8, 128), F32)


def first_half(shape):
    return lax.broadcasted_iota(jnp.int32, shape, 1) < 64


def pack_halo(lo_ref, hi_ref, out_ref):
    first = first_half((64, 128))
    for way, table in enumerate((lo_ref, hi_ref)):
        for j in range(0, 4, 2):
            pair = [table[j + i].reshape(64, 128) for i in range(2)]
            out_ref[way, j // 2] = jnp.where(first, *pair).astype(BF16)


def fill_halo(in_ref, lo_ref, hi_ref):
    first = first_half((64, 128))
    for way, table in enumerate((lo_ref, hi_ref)):
        for j in range(0, 4, 2):
            pair = in_ref[way, j // 2].astype(F32)
            turned = pltpu.roll(pair, 64, 1)
            table[4 + j] = jnp.where(first, pair, turned).reshape(8, 8, 128)
            table[5 + j] = jnp.where(first, turned, pair).reshape(8, 8, 128)


def store_plane(put, middle, below, above):
    z = lax.broadcasted_iota(jnp.int32, (10, 8, 128), 1)
    first = lax.broadcasted_iota(jnp.int32, (10, 8, 128), 2) < 64
    minus = pltpu.roll(jnp.where(z == 7, below, middle), 1, 1)
    plus = pltpu.roll(jnp.where(z == 0, above, middle), 7, 1)
    left = jnp.where(first, minus, middle)
    for dy in range(3):
        put(dy, 0, left[dy : dy + 8].reshape(64, 128).astype(BF16))
        put(dy, 128, plus[dy : dy + 8].reshape(64, 128).astype(BF16))


def link(nb_ref, b, ox, oy, oz, zero):
    j = nb_ref[b, (ox + 1) * 9 + (oy + 1) * 3 + oz + 1]
    return jnp.where(j < 0, zero, j)


def fill_inner(nb_ref, count, b, t_ref, q_ref, qe_ref):
    own = jnp.where(b < count, b, 4)
    idx = [[link(nb_ref, b, 0, oy, oz, 4) for oy in (-1, 0, 1)] for oz in (0, -1, 1)]
    idx[0][1] = own
    for xp in range(1, 9):
        cols = [
            jnp.concatenate(
                [t_ref[i0, xp - 1, 7:8], t_ref[i1, xp - 1], t_ref[i2, xp - 1, 0:1]], 0
            )
            for i0, i1, i2 in idx
        ]
        row, edge = b * 512 + (xp - 1) * 64, b * 64

        def put(dy, lane, rows, row=row, edge=edge, xp=xp):
            q_ref[dy, row : row + 64, lane : lane + 128] = rows
            if xp in (1, 2):
                qe_ref[dy, xp, edge : edge + 64, lane : lane + 128] = rows
            if xp in (7, 8):
                qe_ref[dy, xp - 7, 256 + edge : 320 + edge, lane : lane + 128] = rows

        store_plane(put, *cols)


def fill_outer(nb_ref, b, lo_ref, hi_ref, qe_ref):
    for ox, side, table in ((-1, 0, lo_ref), (1, 1, hi_ref)):
        cols = []
        for oz in (0, -1, 1):
            i0, i1, i2 = [link(nb_ref, b, ox, oy, oz, 8) for oy in (-1, 0, 1)]
            cols.append(jnp.concatenate([table[i0, 7:8], table[i1], table[i2, 0:1]], 0))

        row = side * 256 + b * 64

        def put(dy, lane, rows, side=side, row=row):
            qe_ref[dy, 2 * side, row : row + 64, lane : lane + 128] = rows

        store_plane(put, *cols)


def regroup(m, outer, inner):
    first = first_half((64, 128))
    out = []
    for i in range(0, inner, 2):
        even, odd = [], []
        for o in range(0, outer, 2):
            x0 = m[o * 64 : o * 64 + 64, i * 64 : i * 64 + 128]
            x1 = m[o * 64 + 64 : o * 64 + 128, i * 64 : i * 64 + 128]
            even.append(jnp.where(first, x0, pltpu.roll(x1, 64, 1)))
            odd.append(jnp.where(first, pltpu.roll(x0, 64, 1), x1))
        out += [jnp.concatenate(even, 1), jnp.concatenate(odd, 1)]
    return jnp.concatenate(out, 0)


def fill_permutation(s_ref):
    v = lax.broadcasted_iota(jnp.int32, (64, 512), 1)
    u = lax.broadcasted_iota(jnp.int32, (64, 512), 0)
    place = (v // 64 % 2) * 4 + (v // 8 % 2) * 2 + v % 2
    cell = (v // 128) * 16 + (v // 16 % 4) * 4 + v % 8 // 2
    at = place * 64 + cell - u
    for t in range(8):
        s_ref[t * 64 : t * 64 + 64] = (at == t * 64).astype(F32).astype(BF16)


def cell_gradients(g_ref, dw_ref, count, s_ref, ga_ref, ue_ref, grad_ref):
    slot = lax.broadcasted_iota(jnp.int32, (256, 128), 0) // 64
    grads = jnp.where(slot < count, g_ref[...].reshape(256, 128).astype(F32), 0.0)
    ga_ref[...] = grads.astype(BF16)
    every = dot(dw_ref[...].reshape(512, 128), ga_ref[...], NT)
    every = regroup(every, 8, 4).astype(BF16)
    grad_ref[...] = dot(every, s_ref[...], NN).reshape(4, 64, 512)
    r = lax.broadcasted_iota(jnp.int32, (256, 256), 0)
    v = lax.broadcasted_iota(jnp.int32, (256, 256), 1)
    cell = v // 64 * 64 + v // 16 % 4 * 4 + v % 8 // 2
    turned = grads.T.astype(BF16)
    for side in range(2):
        spread = (r == cell + 48 * side).astype(F32).astype(BF16)
        ue_ref[side] = dot(turned, spread, NN).astype(BF16)


def inner_down(hid_ref, s_ref, ga_ref):
    cells = dot(hid_ref[...].reshape(256, 512), s_ref[...], NT)
    return dot(regroup(cells, 4, 8).astype(BF16), ga_ref[...], NN)


def inner_forward(b, w_ref, q_ref, pre_ref):
    acc = jnp.zeros((192, 512), F32)
    for dy in range(3):
        acc += dot(w_ref[dy], q_ref[dy, b * 512 : b * 512 + 512, 0:192], NT)
    gap = jnp.zeros((64, 64), F32)
    low = jnp.concatenate([gap, acc[0:64, 0:448]], 1)
    high = jnp.concatenate([acc[128:192, 64:512], gap], 1)
    pre_ref[b] = acc[64:128] + low + high


def outer_forward(w_ref, qe_ref):
    low, high = jnp.zeros((64, 256), F32), jnp.zeros((64, 256), F32)
    for dy in range(3):
        low += dot(w_ref[dy, 0:64], qe_ref[dy, 0, 0:256, 0:192], NT)
        high += dot(w_ref[dy, 128:192], qe_ref[dy, 2, 256:512, 0:192], NT)
    return low, high


def inner_block(b, pre_ref, grad_ref, hid_ref, sh_ref):
    lane = lax.broadcasted_iota(jnp.int32, (64, 512), 1)
    inside = (lane >= 64) & (lane < 448)
    gap = jnp.zeros((64, 64), F32)
    pre = jnp.where(inside, pre_ref[b], 0.0)
    hidden = jnp.maximum(pre, 0.0)
    hid_ref[b] = hidden.astype(BF16)
    cols = slice(b * 512, b * 512 + 512)
    act = jnp.where(pre > 0, grad_ref[b], 0.0)
    sh_ref[0:64, cols] = jnp.concatenate([act[:, 64:512], gap], 1).astype(BF16)
    sh_ref[64:128, cols] = act.astype(BF16)
    sh_ref[128:192, cols] = jnp.concatenate([gap, act[:, 0:448]], 1).astype(BF16)


def edge_lanes(side):
    return slice(448, 512) if side else slice(0, 64)


def stash_edges(pre_ref, grad_ref, pe_ref, ge_ref):
    for side in range(2):
        at = edge_lanes(side)
        pe_ref[side] = jnp.concatenate([pre_ref[b, :, at] for b in range(4)], 1)
        ge_ref[side] = jnp.concatenate([grad_ref[b, :, at] for b in range(4)], 1)


def edge_planes(sums, pe_ref, ge_ref, ue_ref, hid_ref, dg_ref, down_ref):
    v = lax.broadcasted_iota(jnp.int32, (64, 256), 1)
    place = (v // 8 % 2) * 2 + v % 2
    first = lax.broadcasted_iota(jnp.int32, (64, 128), 1) < 64
    acts = []
    for side in range(2):
        pre = pe_ref[side] + sums[side]
        hidden = jnp.maximum(pre, 0.0)
        acts.append(jnp.where(pre > 0, ge_ref[side], 0.0))
        spread = jnp.concatenate([jnp.where(place == t, hidden, 0.0) for t in range(4)], 0)
        down = dg_ref[side * 256 : side * 256 + 256] + dot(spread.astype(BF16), ue_ref[side], NT)
        for p in range(NXY):
            down_ref[side, p] = down[p * 16 : p * 16 + 16]
        tile = slice(384, 512) if side else slice(0, 128)
        for b in range(4):
            mine = hidden[:, b // 2 * 128 : b // 2 * 128 + 128]
            if b % 2 != side:
                mine = pltpu.roll(mine, 64, 1)
            old = hid_ref[b, :, tile].astype(F32)
            hid_ref[b, :, tile] = jnp.where(first != (side == 1), mine, old).astype(BF16)
    return jnp.concatenate(acts, 1).astype(BF16)


def put_rows(v_ref, at, rows):
    for i in range(0, rows.shape[0], CONV_ROWS):
        p = (at + i) // CONV_ROWS
        v_ref[p // NXY, p % NXY] = rows[i : i + CONV_ROWS]


def conv_gradient(acts, qe_ref, cg_ref, conv_ref):
    plus = []
    for dy in range(3):
        parts = [
            cg_ref[dy, dx * 64 : dx * 64 + 64] + dot(acts, qe_ref[dy, dx], NN) for dx in range(3)
        ]
        grads = jnp.concatenate(parts, 0)
        put_rows(conv_ref, dy * 192, grads[:, 0:128])
        plus.append(grads[:, 128:256])
    first = lax.broadcasted_iota(jnp.int32, (192, 128), 1) < 64
    put_rows(conv_ref, 576, jnp.where(first, plus[0], plus[1]))
    put_rows(conv_ref, 768, plus[2])
    put_rows(conv_ref, 960, jnp.zeros((64, 128), F32))


def remote(src, dst, send, recv, peer):
    return pltpu.make_async_remote_copy(
        src, dst, send, recv, device_id=peer, device_id_type=MESH
    )


def section_kernel(
    nb_ref, cnt_ref, f_hbm, g_hbm, cw_hbm, dw_hbm, hid_ref, o_ref,
    f_ref, g_ref, cw_ref, dw_ref, ho_ref, hi_in_ref, t_ref, lo_ref, hi_ref, q_ref, qe_ref, w_ref,
    s_ref, ga_ref, grad_ref, pre_ref, sh_ref, pe_ref, ge_ref, ue_ref, dg_ref, cg_ref,
    conv_ref, down_ref, mate_conv, mate_down, outgoing, parts, along,
    ls, hs, hr, cs, cr, ss, rs, zs, zr, gs, gr, es, er,
):
    strip, tile = lax.axis_index("space"), lax.axis_index("rep")
    z, rest = lax.div(strip, 8), lax.rem(strip, 8)
    y, x_hi = lax.div(rest, 2), lax.rem(rest, 2)
    x_lo, core = lax.div(tile, 2), lax.rem(tile, 2)
    x = x_hi * 2 + x_lo
    me = y * NX + x
    sibling = {"space": strip, "rep": x_lo * 2 + 1 - core}

    ys = [y] + [lax.rem(y + d, NY) for d in range(1, NY)]
    xs = [x] + [lax.rem(x + d, NX) for d in range(1, NX)]
    x_his = [lax.div(v, 2) for v in xs]
    tiles = [lax.rem(v, 2) * 2 + core for v in xs]
    rows = [z * 8 + v * 2 for v in ys]
    slots = [v * NX for v in ys]
    plane = [(dy, dx) for dy in range(NY) for dx in range(NX) if dy or dx]
    plane.sort(key=lambda o: -(min(o[0], NY - o[0]) + min(o[1], NX - o[1])))
    peers = {
        (dy, dx): ({"space": rows[dy] + x_his[dx], "rep": tiles[dx]}, slots[dy] + xs[dx])
        for dy, dx in plane
    }
    order = [peers[o] for o in plane]
    line = [{"space": lax.rem(z + d, NZ) * 8 + rest, "rep": tile} for d in (4, 3, 5, 2, 6, 1, 7)]
    strips = NX // 2 * NY * NZ
    above = {"space": lax.rem(strip + 1, strips), "rep": tile}
    below = {"space": lax.rem(strip + strips - 1, strips), "rep": tile}

    loads = [
        pltpu.make_async_copy(src, dst, ls.at[i])
        for i, (src, dst) in enumerate(
            ((f_hbm, f_ref), (cw_hbm, cw_ref), (g_hbm, g_ref), (dw_hbm, dw_ref))
        )
    ]
    for c in loads:
        c.start()
    barrier = pltpu.get_barrier_semaphore()
    greet = [above, below] + [peer for peer, _ in order] + line + [sibling]
    for d in greet:
        pl.semaphore_signal(barrier, inc=1, device_id=d, device_id_type=MESH)
    count = cnt_ref[0]

    loads[0].wait()
    fill_tables(f_ref, t_ref, lo_ref, hi_ref)
    pack_halo(lo_ref, hi_ref, ho_ref)
    pl.semaphore_wait(barrier, len(greet))
    halo = [
        pltpu.make_async_remote_copy(
            ho_ref.at[0], hi_in_ref.at[0], hs.at[0], hr.at[0],
            device_id=above, device_id_type=MESH,
        ),
        pltpu.make_async_remote_copy(
            ho_ref.at[1], hi_in_ref.at[1], hs.at[1], hr.at[1],
            device_id=below, device_id_type=MESH,
        ),
    ]
    for c in halo:
        c.start()
    loads[1].wait()
    fill_weights(cw_ref, w_ref)
    fill_permutation(s_ref)
    loads[2].wait()
    loads[3].wait()
    cell_gradients(g_ref, dw_ref, count, s_ref, ga_ref, ue_ref, grad_ref)
    for b in range(4):
        fill_inner(nb_ref, count, b, t_ref, q_ref, qe_ref)
        inner_forward(b, w_ref, q_ref, pre_ref)
        inner_block(b, pre_ref, grad_ref, hid_ref, sh_ref)
    stash_edges(pre_ref, grad_ref, pe_ref, ge_ref)
    dg_ref[...] = inner_down(hid_ref, s_ref, ga_ref)
    for dy in range(3):
        cg_ref[dy] = dot(sh_ref[...], q_ref[dy], NN)

    for c in halo:
        c.wait()
    fill_halo(hi_in_ref, lo_ref, hi_ref)
    for b in range(4):
        fill_outer(nb_ref, b, lo_ref, hi_ref, qe_ref)
    sums = outer_forward(w_ref, qe_ref)

    acts = edge_planes(sums, pe_ref, ge_ref, ue_ref, hid_ref, dg_ref, down_ref)
    swap_down = remote(down_ref.at[1 - core], mate_down, cs.at[0], cr.at[0], sibling)
    swap_down.start()
    conv_gradient(acts, qe_ref, cg_ref, conv_ref)
    swap_conv = remote(conv_ref.at[1 - core], mate_conv, cs.at[1], cr.at[1], sibling)
    swap_conv.start()

    def summed(at):
        return (
            conv_ref[core, at] + mate_conv[at],
            down_ref[core, at] + mate_down[at],
        )

    swap_down.wait_recv()
    swap_conv.wait_recv()
    copies = []
    for i, (peer, at) in enumerate(order):
        conv, down = summed(at)
        outgoing[i, 0:CONV_ROWS] = conv.astype(BF16)
        outgoing[i, CONV_ROWS:ROWS] = down.astype(BF16)
        copies.append(remote(outgoing.at[i], parts.at[i], ss.at[i], rs.at[i], peer))
        copies[-1].start()
    total = jnp.concatenate(summed(me), 0)
    for i in reversed(range(NXY - 1)):
        copies[i].wait_recv()
        total = total + parts[i].astype(F32)

    along[z] = total.astype(BF16)
    lines = []
    for i, peer in enumerate(line):
        lines.append(remote(along.at[z], along.at[z], zs.at[i], zr.at[i], peer))
        lines[-1].start()
    for c in [swap_down, swap_conv] + copies:
        c.wait_send()
    for c in lines:
        c.wait_recv()
    total = along[0].astype(F32)
    for i in range(1, NZ):
        total = total + along[i].astype(F32)

    half = core * NXY
    own = o_ref.at[half + me]
    o_ref[half + me] = total
    last = []
    for i, (peer, _) in enumerate(order):
        last.append(remote(own, own, gs.at[i], gr.at[i], peer))
        last[-1].start()
    shared = [remote(own, own, es.at[NXY - 1], er.at[NXY - 1], sibling)]
    shared[0].start()
    for c in lines:
        c.wait_send()
    for i in reversed(range(NXY - 1)):
        last[i].wait_recv()
        _, at = peers[-plane[i][0] % NY, -plane[i][1] % NX]
        piece = o_ref.at[half + at]
        shared.append(remote(piece, piece, es.at[i], er.at[i], sibling))
        shared[-1].start()
    for c in last:
        c.wait_send()
    for c in shared:
        c.wait()


def section(features, neighbours, counts, cotangent, conv_weight, down_weight):
    dma = pltpu.SemaphoreType.DMA
    vm = pltpu.VMEM
    near, line = NXY - 1, NZ - 1

    return pl.pallas_call(
        section_kernel,
        out_shape=(
            pltpu.VMEM((4, 64, 512), BF16),
            pltpu.VMEM((32, ROWS, 128), F32),
        ),
        in_specs=[SM, SM, ANY, ANY, ANY, ANY],
        out_specs=(VM, VM),
        scratch_shapes=[
            vm((4, 64, 512), BF16), vm((4, 64, 128), BF16), vm((27, 64, 64), BF16), vm((8, 64, 128), BF16),
            vm((2, 2, 64, 128), BF16), vm((2, 2, 64, 128), BF16),
            vm((5, 8, 8, 8, 128), F32), vm((9, 8, 8, 128), F32), vm((9, 8, 8, 128), F32),
            vm((3, 2048, 256), BF16), vm((3, 3, 512, 256), BF16), vm((3, 192, 192), BF16),
            vm((512, 512), BF16), vm((256, 128), BF16), vm((4, 64, 512), F32), vm((4, 64, 512), F32),
            vm((192, 2048), BF16),
            vm((2, 64, 256), F32), vm((2, 64, 256), F32), vm((2, 128, 256), BF16),
            vm((512, 128), F32), vm((3, 192, 256), F32),
            vm((2, NXY, CONV_ROWS, 128), F32), vm((2, NXY, DOWN_ROWS, 128), F32),
            vm((NXY, CONV_ROWS, 128), F32), vm((NXY, DOWN_ROWS, 128), F32),
            vm((near, ROWS, 128), BF16), vm((near, ROWS, 128), BF16), vm((NZ, ROWS, 128), BF16),
            dma((4,)), dma((2,)), dma((2,)), dma((2,)), dma((2,)), dma((near,)), dma((near,)),
            dma((line,)), dma((line,)), dma((near,)), dma((near,)), dma((NXY,)), dma((NXY,)),
        ],
        compiler_params=pltpu.CompilerParams(
            collective_id=0, has_side_effects=True, vmem_limit_bytes=56 << 20
        ),
        name="section",
    )(neighbours, counts, features, cotangent, conv_weight, down_weight)


def unpack_kernel(v_ref, hid_ref, conv_hbm, down_hbm, hid_hbm, conv_ref, sem):
    moves = [
        pltpu.make_async_copy(v_ref.at[:, pl.ds(CONV_ROWS, DOWN_ROWS), :], down_hbm, sem.at[0]),
        pltpu.make_async_copy(hid_ref, hid_hbm, sem.at[1]),
    ]
    for m in moves:
        m.start()
    conv = v_ref[:, 0:CONV_ROWS].reshape(1024, 128)
    for dx in range(3):
        for dy in range(3):
            at = dy * 192 + dx * 64
            pair = conv[at : at + 64]
            conv_ref[dx * 9 + dy * 3] = pair[:, 0:64]
            conv_ref[dx * 9 + dy * 3 + 1] = pair[:, 64:128]
            at = 768 + dx * 64 if dy == 2 else 576 + dx * 64
            side = 64 if dy == 1 else 0
            conv_ref[dx * 9 + dy * 3 + 2] = conv[at : at + 64, side : side + 64]
        part = pl.ds(dx * 9, 9)
        moves.append(
            pltpu.make_async_copy(conv_ref.at[part], conv_hbm.at[part], sem.at[2 + dx])
        )
        moves[-1].start()
    for m in moves:
        m.wait()


def unpack(pieces, hidden):
    return pl.pallas_call(
        unpack_kernel,
        out_shape=(
            jax.ShapeDtypeStruct((27, 64, 64), F32),
            jax.ShapeDtypeStruct((32, DOWN_ROWS, 128), F32),
            jax.ShapeDtypeStruct((4, 64, 512), BF16),
        ),
        in_specs=[VM, VM],
        out_specs=(ANY, ANY, ANY),
        scratch_shapes=[pltpu.VMEM((27, 64, 64), F32), pltpu.SemaphoreType.DMA((5,))],
        compiler_params=pltpu.CompilerParams(vmem_limit_bytes=48 << 20),
        name="unpack",
    )(pieces, hidden)


def body(features, neighbours, counts, cotangent, conv_weight, down_weight):
    down_rows = jnp.swapaxes(down_weight, 1, 2)
    hidden, pieces = section(features, neighbours, counts, cotangent, conv_weight, down_rows)
    conv_grad, down_grad, hidden = unpack(pieces, hidden)
    return hidden, conv_grad, jnp.swapaxes(down_grad.reshape(8, 64, 128), 1, 2)


def solution(mesh):
    both = ("space", "rep")
    return jax.shard_map(
        body,
        mesh=mesh,
        in_specs=(
            P(both, None, None), P(both, None), P(both), P(both, None, None), P(), P(),
        ),
        out_specs=(P(both, None, None), P(), P()),
        check_vma=False,
    )
```

```python
import jax
import jax.numpy as jnp
from jax import lax
from jax.experimental import pallas as pl
from jax.experimental.pallas import tpu as pltpu
from jax.sharding import PartitionSpec as P

MESH = pl.DeviceIdType.MESH
F32, BF16 = jnp.float32, jnp.bfloat16
VM = pl.BlockSpec(memory_space=pltpu.VMEM)
ANY = pl.BlockSpec(memory_space=pl.ANY)
NX, NY, NZ = 4, 4, 8
NXY = NX * NY
CONV_ROWS, DOWN_ROWS = 32, 16
ROWS = CONV_ROWS + DOWN_ROWS


def dot(a, b, dims):
    return lax.dot_general(a, b, (dims, ((), ())), preferred_element_type=F32)


NN, NT, TN = ((1,), (0,)), ((1,), (1,)), ((0,), (0,))


def voxels_in_rows(block):
    wide = block.astype(F32)
    return jnp.concatenate([wide, wide], 0).T


def fill_weights(cw_ref, w_ref):
    for dy in range(3):
        for dx in range(3):
            row = [cw_ref[dx * 9 + dy * 3 + dz].astype(F32) for dz in range(3)]
            w_ref[dy, dx * 64 : dx * 64 + 64, :] = jnp.concatenate(row, 1).astype(BF16)


def fill_tables(f_ref, t_ref, lo_ref, hi_ref):
    for j in range(4):
        for q in range(4):
            part = voxels_in_rows(f_ref[j, :, q * 128 : q * 128 + 128])
            t_ref[j, q * 2 : q * 2 + 2] = part.reshape(2, 8, 8, 128)
        lo_ref[j] = t_ref[j, 7]
        hi_ref[j] = t_ref[j, 0]
    t_ref[4] = jnp.zeros((8, 8, 8, 128), F32)
    lo_ref[8] = jnp.zeros((8, 8, 128), F32)
    hi_ref[8] = jnp.zeros((8, 8, 128), F32)


def first_half(shape):
    return lax.broadcasted_iota(jnp.int32, shape, 1) < 64


def pack_halo(lo_ref, hi_ref, out_ref):
    first = first_half((64, 128))
    for way, table in enumerate((lo_ref, hi_ref)):
        for j in range(0, 4, 2):
            pair = [table[j + i].reshape(64, 128) for i in range(2)]
            out_ref[way, j // 2] = jnp.where(first, *pair).astype(BF16)


def fill_halo(in_ref, lo_ref, hi_ref):
    first = first_half((64, 128))
    for way, table in enumerate((lo_ref, hi_ref)):
        for j in range(0, 4, 2):
            pair = in_ref[way, j // 2].astype(F32)
            turned = pltpu.roll(pair, 64, 1)
            table[4 + j] = jnp.where(first, pair, turned).reshape(8, 8, 128)
            table[5 + j] = jnp.where(first, turned, pair).reshape(8, 8, 128)


def store_plane(put, middle, below, above):
    z = lax.broadcasted_iota(jnp.int32, (10, 8, 128), 1)
    first = lax.broadcasted_iota(jnp.int32, (10, 8, 128), 2) < 64
    minus = pltpu.roll(jnp.where(z == 7, below, middle), 1, 1)
    plus = pltpu.roll(jnp.where(z == 0, above, middle), 7, 1)
    left = jnp.where(first, minus, middle)
    for dy in range(3):
        put(dy, 0, left[dy : dy + 8].reshape(64, 128).astype(BF16))
        put(dy, 128, plus[dy : dy + 8].reshape(64, 128).astype(BF16))


def link(nb_ref, b, ox, oy, oz, zero):
    j = nb_ref[b, (ox + 1) * 9 + (oy + 1) * 3 + oz + 1]
    return jnp.where(j < 0, zero, j)


def fill_inner(nb_ref, count, b, t_ref, q_ref, qe_ref):
    own = jnp.where(b < count, b, 4)
    idx = [[link(nb_ref, b, 0, oy, oz, 4) for oy in (-1, 0, 1)] for oz in (0, -1, 1)]
    idx[0][1] = own
    for xp in range(1, 9):
        cols = [
            jnp.concatenate(
                [t_ref[i0, xp - 1, 7:8], t_ref[i1, xp - 1], t_ref[i2, xp - 1, 0:1]], 0
            )
            for i0, i1, i2 in idx
        ]
        row, edge = b * 512 + (xp - 1) * 64, b * 64

        def put(dy, lane, rows, row=row, edge=edge, xp=xp):
            q_ref[dy, row : row + 64, lane : lane + 128] = rows
            if xp in (1, 2):
                qe_ref[dy, xp, edge : edge + 64, lane : lane + 128] = rows
            if xp in (7, 8):
                qe_ref[dy, xp - 7, 256 + edge : 320 + edge, lane : lane + 128] = rows

        store_plane(put, *cols)


def fill_outer(nb_ref, b, lo_ref, hi_ref, qe_ref):
    for ox, side, table in ((-1, 0, lo_ref), (1, 1, hi_ref)):
        cols = []
        for oz in (0, -1, 1):
            i0, i1, i2 = [link(nb_ref, b, ox, oy, oz, 8) for oy in (-1, 0, 1)]
            cols.append(jnp.concatenate([table[i0, 7:8], table[i1], table[i2, 0:1]], 0))

        row = side * 256 + b * 64

        def put(dy, lane, rows, side=side, row=row):
            qe_ref[dy, 2 * side, row : row + 64, lane : lane + 128] = rows

        store_plane(put, *cols)


def regroup(m, outer, inner):
    first = first_half((64, 128))
    out = []
    for i in range(0, inner, 2):
        even, odd = [], []
        for o in range(0, outer, 2):
            x0 = m[o * 64 : o * 64 + 64, i * 64 : i * 64 + 128]
            x1 = m[o * 64 + 64 : o * 64 + 128, i * 64 : i * 64 + 128]
            even.append(jnp.where(first, x0, pltpu.roll(x1, 64, 1)))
            odd.append(jnp.where(first, pltpu.roll(x0, 64, 1), x1))
        out += [jnp.concatenate(even, 1), jnp.concatenate(odd, 1)]
    return jnp.concatenate(out, 0)


def fill_permutation(s_ref):
    v = lax.broadcasted_iota(jnp.int32, (64, 512), 1)
    u = lax.broadcasted_iota(jnp.int32, (64, 512), 0)
    place = (v // 64 % 2) * 4 + (v // 8 % 2) * 2 + v % 2
    cell = (v // 128) * 16 + (v // 16 % 4) * 4 + v % 8 // 2
    at = place * 64 + cell - u
    for t in range(8):
        s_ref[t * 64 : t * 64 + 64] = (at == t * 64).astype(F32).astype(BF16)


def cell_gradients(g_ref, dw_ref, count, s_ref, ga_ref, ue_ref, grad_ref):
    slot = lax.broadcasted_iota(jnp.int32, (256, 128), 0) // 64
    grads = jnp.where(slot < count, g_ref[...].reshape(256, 128).astype(F32), 0.0)
    ga_ref[...] = grads.astype(BF16)
    every = dot(dw_ref[...].reshape(512, 128), ga_ref[...], NT)
    every = regroup(every, 8, 4).astype(BF16)
    grad_ref[...] = dot(every, s_ref[...], NN).reshape(4, 64, 512)
    r = lax.broadcasted_iota(jnp.int32, (256, 256), 0)
    v = lax.broadcasted_iota(jnp.int32, (256, 256), 1)
    cell = v // 64 * 64 + v // 16 % 4 * 4 + v % 8 // 2
    turned = grads.T.astype(BF16)
    for side in range(2):
        spread = (r == cell + 48 * side).astype(F32).astype(BF16)
        ue_ref[side] = dot(turned, spread, NN).astype(BF16)


def inner_down(hid_ref, s_ref, ga_ref):
    cells = dot(hid_ref[...].reshape(256, 512), s_ref[...], NT)
    return dot(regroup(cells, 4, 8).astype(BF16), ga_ref[...], NN)


def inner_forward(b, w_ref, q_ref, pre_ref):
    acc = jnp.zeros((192, 512), F32)
    for dy in range(3):
        acc += dot(w_ref[dy], q_ref[dy, b * 512 : b * 512 + 512, 0:192], NT)
    gap = jnp.zeros((64, 64), F32)
    low = jnp.concatenate([gap, acc[0:64, 0:448]], 1)
    high = jnp.concatenate([acc[128:192, 64:512], gap], 1)
    pre_ref[b] = acc[64:128] + low + high


def outer_forward(w_ref, qe_ref):
    low, high = jnp.zeros((64, 256), F32), jnp.zeros((64, 256), F32)
    for dy in range(3):
        low += dot(w_ref[dy, 0:64], qe_ref[dy, 0, 0:256, 0:192], NT)
        high += dot(w_ref[dy, 128:192], qe_ref[dy, 2, 256:512, 0:192], NT)
    return low, high


def inner_block(b, pre_ref, grad_ref, hid_ref, sh_ref):
    lane = lax.broadcasted_iota(jnp.int32, (64, 512), 1)
    inside = (lane >= 64) & (lane < 448)
    gap = jnp.zeros((64, 64), F32)
    pre = jnp.where(inside, pre_ref[b], 0.0)
    hidden = jnp.maximum(pre, 0.0)
    hid_ref[b] = hidden.astype(BF16)
    cols = slice(b * 512, b * 512 + 512)
    act = jnp.where(pre > 0, grad_ref[b], 0.0)
    sh_ref[0:64, cols] = jnp.concatenate([act[:, 64:512], gap], 1).astype(BF16)
    sh_ref[64:128, cols] = act.astype(BF16)
    sh_ref[128:192, cols] = jnp.concatenate([gap, act[:, 0:448]], 1).astype(BF16)


def edge_lanes(side):
    return slice(448, 512) if side else slice(0, 64)


def stash_edges(pre_ref, grad_ref, pe_ref, ge_ref):
    for side in range(2):
        at = edge_lanes(side)
        pe_ref[side] = jnp.concatenate([pre_ref[b, :, at] for b in range(4)], 1)
        ge_ref[side] = jnp.concatenate([grad_ref[b, :, at] for b in range(4)], 1)


def edge_planes(sums, pe_ref, ge_ref, ue_ref, hid_ref, dg_ref, down_ref):
    v = lax.broadcasted_iota(jnp.int32, (64, 256), 1)
    place = (v // 8 % 2) * 2 + v % 2
    first = lax.broadcasted_iota(jnp.int32, (64, 128), 1) < 64
    acts = []
    for side in range(2):
        pre = pe_ref[side] + sums[side]
        hidden = jnp.maximum(pre, 0.0)
        acts.append(jnp.where(pre > 0, ge_ref[side], 0.0))
        spread = jnp.concatenate([jnp.where(place == t, hidden, 0.0) for t in range(4)], 0)
        down = dg_ref[side * 256 : side * 256 + 256] + dot(spread.astype(BF16), ue_ref[side], NT)
        for p in range(NXY):
            down_ref[side, p] = down[p * 16 : p * 16 + 16]
        tile = slice(384, 512) if side else slice(0, 128)
        for b in range(4):
            mine = hidden[:, b // 2 * 128 : b // 2 * 128 + 128]
            if b % 2 != side:
                mine = pltpu.roll(mine, 64, 1)
            old = hid_ref[b, :, tile].astype(F32)
            hid_ref[b, :, tile] = jnp.where(first != (side == 1), mine, old).astype(BF16)
    return jnp.concatenate(acts, 1).astype(BF16)


def put_rows(v_ref, at, rows):
    for i in range(0, rows.shape[0], CONV_ROWS):
        p = (at + i) // CONV_ROWS
        v_ref[p // NXY, p % NXY] = rows[i : i + CONV_ROWS]


def conv_gradient(acts, qe_ref, cg_ref, conv_ref):
    plus = []
    for dy in range(3):
        parts = [
            cg_ref[dy, dx * 64 : dx * 64 + 64] + dot(acts, qe_ref[dy, dx], NN) for dx in range(3)
        ]
        grads = jnp.concatenate(parts, 0)
        put_rows(conv_ref, dy * 192, grads[:, 0:128])
        plus.append(grads[:, 128:256])
    first = lax.broadcasted_iota(jnp.int32, (192, 128), 1) < 64
    put_rows(conv_ref, 576, jnp.where(first, plus[0], plus[1]))
    put_rows(conv_ref, 768, plus[2])
    put_rows(conv_ref, 960, jnp.zeros((64, 128), F32))


def remote(src, dst, send, recv, peer):
    return pltpu.make_async_remote_copy(
        src, dst, send, recv, device_id=peer, device_id_type=MESH
    )


def section_kernel(
    nb_hbm, cnt_hbm, f_hbm, g_hbm, cw_hbm, dw_hbm, hid_ref, o_ref,
    nb_ref, cnt_ref, f_ref, g_ref, cw_ref, dw_ref, ho_ref, hi_in_ref, t_ref, lo_ref, hi_ref, q_ref, qe_ref, w_ref,
    s_ref, ga_ref, grad_ref, pre_ref, sh_ref, pe_ref, ge_ref, ue_ref, dg_ref, cg_ref,
    conv_ref, down_ref, mate_conv, mate_down, outgoing, parts, along,
    ls, hs, hr, cs, cr, ss, rs, zs, zr, gs, gr, es, er,
):
    strip, tile = lax.axis_index("space"), lax.axis_index("rep")
    z, rest = lax.div(strip, 8), lax.rem(strip, 8)
    y, x_hi = lax.div(rest, 2), lax.rem(rest, 2)
    x_lo, core = lax.div(tile, 2), lax.rem(tile, 2)
    x = x_hi * 2 + x_lo
    me = y * NX + x
    sibling = {"space": strip, "rep": x_lo * 2 + 1 - core}

    ys = [y] + [lax.rem(y + d, NY) for d in range(1, NY)]
    xs = [x] + [lax.rem(x + d, NX) for d in range(1, NX)]
    x_his = [lax.div(v, 2) for v in xs]
    tiles = [lax.rem(v, 2) * 2 + core for v in xs]
    rows = [z * 8 + v * 2 for v in ys]
    slots = [v * NX for v in ys]
    plane = [(dy, dx) for dy in range(NY) for dx in range(NX) if dy or dx]
    plane.sort(key=lambda o: -(min(o[0], NY - o[0]) + min(o[1], NX - o[1])))
    peers = {
        (dy, dx): ({"space": rows[dy] + x_his[dx], "rep": tiles[dx]}, slots[dy] + xs[dx])
        for dy, dx in plane
    }
    order = [peers[o] for o in plane]
    line = [{"space": lax.rem(z + d, NZ) * 8 + rest, "rep": tile} for d in (4, 3, 5, 2, 6, 1, 7)]
    strips = NX // 2 * NY * NZ
    above = {"space": lax.rem(strip + 1, strips), "rep": tile}
    below = {"space": lax.rem(strip + strips - 1, strips), "rep": tile}

    loads = [
        pltpu.make_async_copy(src, dst, ls.at[i])
        for i, (src, dst) in enumerate(
            ((f_hbm, f_ref), (cw_hbm, cw_ref), (g_hbm, g_ref), (dw_hbm, dw_ref), (nb_hbm, nb_ref), (cnt_hbm, cnt_ref))
        )
    ]
    loads[0].start()
    barrier = pltpu.get_barrier_semaphore()
    greet = [above, below] + [peer for peer, _ in order] + line + [sibling]
    for i, d in enumerate(greet):
        pl.semaphore_signal(barrier, inc=1, device_id=d, device_id_type=MESH)
        if i == 1:
            for c in loads[1:]:
                c.start()

    loads[0].wait()
    fill_tables(f_ref, t_ref, lo_ref, hi_ref)
    pack_halo(lo_ref, hi_ref, ho_ref)
    pl.semaphore_wait(barrier, len(greet))
    halo = [
        pltpu.make_async_remote_copy(
            ho_ref.at[0], hi_in_ref.at[0], hs.at[0], hr.at[0],
            device_id=above, device_id_type=MESH,
        ),
        pltpu.make_async_remote_copy(
            ho_ref.at[1], hi_in_ref.at[1], hs.at[1], hr.at[1],
            device_id=below, device_id_type=MESH,
        ),
    ]
    for c in halo:
        c.start()
    loads[1].wait()
    fill_weights(cw_ref, w_ref)
    fill_permutation(s_ref)
    for c in loads[2:]:
        c.wait()
    count = cnt_ref[0]
    cell_gradients(g_ref, dw_ref, count, s_ref, ga_ref, ue_ref, grad_ref)
    for b in range(4):
        fill_inner(nb_ref, count, b, t_ref, q_ref, qe_ref)
        inner_forward(b, w_ref, q_ref, pre_ref)
        inner_block(b, pre_ref, grad_ref, hid_ref, sh_ref)
    stash_edges(pre_ref, grad_ref, pe_ref, ge_ref)
    dg_ref[...] = inner_down(hid_ref, s_ref, ga_ref)
    for dy in range(3):
        cg_ref[dy] = dot(sh_ref[...], q_ref[dy], NN)

    for c in halo:
        c.wait()
    fill_halo(hi_in_ref, lo_ref, hi_ref)
    for b in range(4):
        fill_outer(nb_ref, b, lo_ref, hi_ref, qe_ref)
    sums = outer_forward(w_ref, qe_ref)

    acts = edge_planes(sums, pe_ref, ge_ref, ue_ref, hid_ref, dg_ref, down_ref)
    swap_down = remote(down_ref.at[1 - core], mate_down, cs.at[0], cr.at[0], sibling)
    swap_down.start()
    conv_gradient(acts, qe_ref, cg_ref, conv_ref)
    swap_conv = remote(conv_ref.at[1 - core], mate_conv, cs.at[1], cr.at[1], sibling)
    swap_conv.start()

    def summed(at):
        return (
            conv_ref[core, at] + mate_conv[at],
            down_ref[core, at] + mate_down[at],
        )

    swap_down.wait_recv()
    swap_conv.wait_recv()
    copies = []
    for i, (peer, at) in enumerate(order):
        conv, down = summed(at)
        outgoing[i, 0:CONV_ROWS] = conv.astype(BF16)
        outgoing[i, CONV_ROWS:ROWS] = down.astype(BF16)
        copies.append(remote(outgoing.at[i], parts.at[i], ss.at[i], rs.at[i], peer))
        copies[-1].start()
    total = jnp.concatenate(summed(me), 0)
    for i in reversed(range(NXY - 1)):
        copies[i].wait_recv()
        total = total + parts[i].astype(F32)

    along[z] = total.astype(BF16)
    lines = []
    for i, peer in enumerate(line):
        lines.append(remote(along.at[z], along.at[z], zs.at[i], zr.at[i], peer))
        lines[-1].start()
    for c in [swap_down, swap_conv] + copies:
        c.wait_send()
    for c in lines:
        c.wait_recv()
    total = along[0].astype(F32)
    for i in range(1, NZ):
        total = total + along[i].astype(F32)

    half = core * NXY
    own = o_ref.at[half + me]
    o_ref[half + me] = total
    last = []
    for i, (peer, _) in enumerate(order):
        last.append(remote(own, own, gs.at[i], gr.at[i], peer))
        last[-1].start()
    shared = [remote(own, own, es.at[NXY - 1], er.at[NXY - 1], sibling)]
    shared[0].start()
    for c in lines:
        c.wait_send()
    for i in reversed(range(NXY - 1)):
        last[i].wait_recv()
        _, at = peers[-plane[i][0] % NY, -plane[i][1] % NX]
        piece = o_ref.at[half + at]
        shared.append(remote(piece, piece, es.at[i], er.at[i], sibling))
        shared[-1].start()
    for c in last:
        c.wait_send()
    for c in shared:
        c.wait()


def section(features, neighbours, counts, cotangent, conv_weight, down_weight):
    dma = pltpu.SemaphoreType.DMA
    vm = pltpu.VMEM
    near, line = NXY - 1, NZ - 1

    return pl.pallas_call(
        section_kernel,
        out_shape=(
            pltpu.VMEM((4, 64, 512), BF16),
            pltpu.VMEM((32, ROWS, 128), F32),
        ),
        in_specs=[ANY] * 6,
        out_specs=(VM, VM),
        scratch_shapes=[
            pltpu.SMEM((4, 27), jnp.int32), pltpu.SMEM((1,), jnp.int32),
            vm((4, 64, 512), BF16), vm((4, 64, 128), BF16), vm((27, 64, 64), BF16), vm((8, 64, 128), BF16),
            vm((2, 2, 64, 128), BF16), vm((2, 2, 64, 128), BF16),
            vm((5, 8, 8, 8, 128), F32), vm((9, 8, 8, 128), F32), vm((9, 8, 8, 128), F32),
            vm((3, 2048, 256), BF16), vm((3, 3, 512, 256), BF16), vm((3, 192, 192), BF16),
            vm((512, 512), BF16), vm((256, 128), BF16), vm((4, 64, 512), F32), vm((4, 64, 512), F32),
            vm((192, 2048), BF16),
            vm((2, 64, 256), F32), vm((2, 64, 256), F32), vm((2, 128, 256), BF16),
            vm((512, 128), F32), vm((3, 192, 256), F32),
            vm((2, NXY, CONV_ROWS, 128), F32), vm((2, NXY, DOWN_ROWS, 128), F32),
            vm((NXY, CONV_ROWS, 128), F32), vm((NXY, DOWN_ROWS, 128), F32),
            vm((near, ROWS, 128), BF16), vm((near, ROWS, 128), BF16), vm((NZ, ROWS, 128), BF16),
            dma((6,)), dma((2,)), dma((2,)), dma((2,)), dma((2,)), dma((near,)), dma((near,)),
            dma((line,)), dma((line,)), dma((near,)), dma((near,)), dma((NXY,)), dma((NXY,)),
        ],
        compiler_params=pltpu.CompilerParams(
            collective_id=0, has_side_effects=True, vmem_limit_bytes=56 << 20
        ),
        name="section",
    )(neighbours, counts, features, cotangent, conv_weight, down_weight)


def unpack_kernel(v_ref, hid_ref, conv_hbm, down_hbm, hid_hbm, conv_ref, sem):
    moves = [
        pltpu.make_async_copy(v_ref.at[:, pl.ds(CONV_ROWS, DOWN_ROWS), :], down_hbm, sem.at[0]),
        pltpu.make_async_copy(hid_ref, hid_hbm, sem.at[1]),
    ]
    for m in moves:
        m.start()
    conv = v_ref[:, 0:CONV_ROWS].reshape(1024, 128)
    for dx in range(3):
        for dy in range(3):
            at = dy * 192 + dx * 64
            pair = conv[at : at + 64]
            conv_ref[dx * 9 + dy * 3] = pair[:, 0:64]
            conv_ref[dx * 9 + dy * 3 + 1] = pair[:, 64:128]
            at = 768 + dx * 64 if dy == 2 else 576 + dx * 64
            side = 64 if dy == 1 else 0
            conv_ref[dx * 9 + dy * 3 + 2] = conv[at : at + 64, side : side + 64]
        part = pl.ds(dx * 9, 9)
        moves.append(
            pltpu.make_async_copy(conv_ref.at[part], conv_hbm.at[part], sem.at[2 + dx])
        )
        moves[-1].start()
    for m in moves:
        m.wait()


def unpack(pieces, hidden):
    return pl.pallas_call(
        unpack_kernel,
        out_shape=(
            jax.ShapeDtypeStruct((27, 64, 64), F32),
            jax.ShapeDtypeStruct((32, DOWN_ROWS, 128), F32),
            jax.ShapeDtypeStruct((4, 64, 512), BF16),
        ),
        in_specs=[VM, VM],
        out_specs=(ANY, ANY, ANY),
        scratch_shapes=[pltpu.VMEM((27, 64, 64), F32), pltpu.SemaphoreType.DMA((5,))],
        compiler_params=pltpu.CompilerParams(vmem_limit_bytes=48 << 20),
        name="unpack",
    )(pieces, hidden)


def body(features, neighbours, counts, cotangent, conv_weight, down_weight):
    down_rows = jnp.swapaxes(down_weight, 1, 2)
    hidden, pieces = section(features, neighbours, counts, cotangent, conv_weight, down_rows)
    conv_grad, down_grad, hidden = unpack(pieces, hidden)
    return hidden, conv_grad, jnp.swapaxes(down_grad.reshape(8, 64, 128), 1, 2)


def solution(mesh):
    both = ("space", "rep")
    return jax.shard_map(
        body,
        mesh=mesh,
        in_specs=(
            P(both, None, None), P(both, None), P(both), P(both, None, None), P(), P(),
        ),
        out_specs=(P(both, None, None), P(), P()),
        check_vma=False,
    )
```

```python
import jax
import jax.numpy as jnp
from jax import lax
from jax.experimental import pallas as pl
from jax.experimental.pallas import tpu as pltpu
from jax.sharding import PartitionSpec as P

MESH = pl.DeviceIdType.MESH
F32, BF16 = jnp.float32, jnp.bfloat16
VM = pl.BlockSpec(memory_space=pltpu.VMEM)
ANY = pl.BlockSpec(memory_space=pl.ANY)
NX, NY, NZ = 4, 4, 8
NXY = NX * NY
CONV_ROWS, DOWN_ROWS = 32, 16
ROWS = CONV_ROWS + DOWN_ROWS


def dot(a, b, dims):
    return lax.dot_general(a, b, (dims, ((), ())), preferred_element_type=F32)


NN, NT, TN = ((1,), (0,)), ((1,), (1,)), ((0,), (0,))


def voxels_in_rows(block):
    wide = block.astype(F32)
    return jnp.concatenate([wide, wide], 0).T


def fill_weights(cw_ref, w_ref):
    for dy in range(3):
        for dx in range(3):
            row = [cw_ref[dx * 9 + dy * 3 + dz].astype(F32) for dz in range(3)]
            w_ref[dy, dx * 64 : dx * 64 + 64, :] = jnp.concatenate(row, 1).astype(BF16)


def fill_tables(f_ref, t_ref, lo_ref, hi_ref):
    for j in range(4):
        for q in range(4):
            part = voxels_in_rows(f_ref[j, :, q * 128 : q * 128 + 128])
            t_ref[j, q * 2 : q * 2 + 2] = part.reshape(2, 8, 8, 128)
        lo_ref[j] = t_ref[j, 7]
        hi_ref[j] = t_ref[j, 0]
    t_ref[4] = jnp.zeros((8, 8, 8, 128), F32)
    lo_ref[8] = jnp.zeros((8, 8, 128), F32)
    hi_ref[8] = jnp.zeros((8, 8, 128), F32)


def first_half(shape):
    return lax.broadcasted_iota(jnp.int32, shape, 1) < 64


def pack_halo(lo_ref, hi_ref, out_ref):
    first = first_half((64, 128))
    for way, table in enumerate((lo_ref, hi_ref)):
        for j in range(0, 4, 2):
            pair = [table[j + i].reshape(64, 128) for i in range(2)]
            out_ref[way, j // 2] = jnp.where(first, *pair).astype(BF16)


def fill_halo(in_ref, lo_ref, hi_ref):
    first = first_half((64, 128))
    for way, table in enumerate((lo_ref, hi_ref)):
        for j in range(0, 4, 2):
            pair = in_ref[way, j // 2].astype(F32)
            turned = pltpu.roll(pair, 64, 1)
            table[4 + j] = jnp.where(first, pair, turned).reshape(8, 8, 128)
            table[5 + j] = jnp.where(first, turned, pair).reshape(8, 8, 128)


def store_plane(put, middle, below, above):
    z = lax.broadcasted_iota(jnp.int32, (10, 8, 128), 1)
    first = lax.broadcasted_iota(jnp.int32, (10, 8, 128), 2) < 64
    minus = pltpu.roll(jnp.where(z == 7, below, middle), 1, 1)
    plus = pltpu.roll(jnp.where(z == 0, above, middle), 7, 1)
    left = jnp.where(first, minus, middle)
    for dy in range(3):
        put(dy, 0, left[dy : dy + 8].reshape(64, 128).astype(BF16))
        put(dy, 128, plus[dy : dy + 8].reshape(64, 128).astype(BF16))


def link(nb_ref, b, ox, oy, oz, zero):
    j = nb_ref[b, (ox + 1) * 9 + (oy + 1) * 3 + oz + 1]
    return jnp.where(j < 0, zero, j)


def fill_inner(nb_ref, count, b, t_ref, q_ref, qe_ref):
    own = jnp.where(b < count, b, 4)
    idx = [[link(nb_ref, b, 0, oy, oz, 4) for oy in (-1, 0, 1)] for oz in (0, -1, 1)]
    idx[0][1] = own
    for xp in range(1, 9):
        cols = [
            jnp.concatenate(
                [t_ref[i0, xp - 1, 7:8], t_ref[i1, xp - 1], t_ref[i2, xp - 1, 0:1]], 0
            )
            for i0, i1, i2 in idx
        ]
        row, edge = b * 512 + (xp - 1) * 64, b * 64

        def put(dy, lane, rows, row=row, edge=edge, xp=xp):
            q_ref[dy, row : row + 64, lane : lane + 128] = rows
            if xp in (1, 2):
                qe_ref[dy, xp, edge : edge + 64, lane : lane + 128] = rows
            if xp in (7, 8):
                qe_ref[dy, xp - 7, 256 + edge : 320 + edge, lane : lane + 128] = rows

        store_plane(put, *cols)


def fill_outer(nb_ref, b, lo_ref, hi_ref, qe_ref):
    for ox, side, table in ((-1, 0, lo_ref), (1, 1, hi_ref)):
        cols = []
        for oz in (0, -1, 1):
            i0, i1, i2 = [link(nb_ref, b, ox, oy, oz, 8) for oy in (-1, 0, 1)]
            cols.append(jnp.concatenate([table[i0, 7:8], table[i1], table[i2, 0:1]], 0))

        row = side * 256 + b * 64

        def put(dy, lane, rows, side=side, row=row):
            qe_ref[dy, 2 * side, row : row + 64, lane : lane + 128] = rows

        store_plane(put, *cols)


def regroup(m, outer, inner):
    first = first_half((64, 128))
    out = []
    for i in range(0, inner, 2):
        even, odd = [], []
        for o in range(0, outer, 2):
            x0 = m[o * 64 : o * 64 + 64, i * 64 : i * 64 + 128]
            x1 = m[o * 64 + 64 : o * 64 + 128, i * 64 : i * 64 + 128]
            even.append(jnp.where(first, x0, pltpu.roll(x1, 64, 1)))
            odd.append(jnp.where(first, pltpu.roll(x0, 64, 1), x1))
        out += [jnp.concatenate(even, 1), jnp.concatenate(odd, 1)]
    return jnp.concatenate(out, 0)


def fill_permutation(s_ref):
    v = lax.broadcasted_iota(jnp.int32, (64, 512), 1)
    u = lax.broadcasted_iota(jnp.int32, (64, 512), 0)
    place = (v // 64 % 2) * 4 + (v // 8 % 2) * 2 + v % 2
    cell = (v // 128) * 16 + (v // 16 % 4) * 4 + v % 8 // 2
    at = place * 64 + cell - u
    for t in range(8):
        s_ref[t * 64 : t * 64 + 64] = (at == t * 64).astype(F32).astype(BF16)


def cell_gradients(g_ref, dw_ref, count, s_ref, ga_ref, ue_ref, grad_ref):
    slot = lax.broadcasted_iota(jnp.int32, (256, 128), 0) // 64
    grads = jnp.where(slot < count, g_ref[...].reshape(256, 128).astype(F32), 0.0)
    ga_ref[...] = grads.astype(BF16)
    every = dot(dw_ref[...].reshape(512, 128), ga_ref[...], NT)
    every = regroup(every, 8, 4).astype(BF16)
    grad_ref[...] = dot(every, s_ref[...], NN).reshape(4, 64, 512)
    r = lax.broadcasted_iota(jnp.int32, (256, 256), 0)
    v = lax.broadcasted_iota(jnp.int32, (256, 256), 1)
    cell = v // 64 * 64 + v // 16 % 4 * 4 + v % 8 // 2
    turned = grads.T.astype(BF16)
    for side in range(2):
        spread = (r == cell + 48 * side).astype(F32).astype(BF16)
        ue_ref[side] = dot(turned, spread, NN).astype(BF16)


def inner_down(hid_ref, s_ref, ga_ref):
    cells = dot(hid_ref[...].reshape(256, 512), s_ref[...], NT)
    return dot(regroup(cells, 4, 8).astype(BF16), ga_ref[...], NN)


def inner_forward(b, w_ref, q_ref, pre_ref):
    acc = jnp.zeros((192, 512), F32)
    for dy in range(3):
        acc += dot(w_ref[dy], q_ref[dy, b * 512 : b * 512 + 512, 0:192], NT)
    gap = jnp.zeros((64, 64), F32)
    low = jnp.concatenate([gap, acc[0:64, 0:448]], 1)
    high = jnp.concatenate([acc[128:192, 64:512], gap], 1)
    pre_ref[b] = acc[64:128] + low + high


def outer_forward(w_ref, qe_ref):
    low, high = jnp.zeros((64, 256), F32), jnp.zeros((64, 256), F32)
    for dy in range(3):
        low += dot(w_ref[dy, 0:64], qe_ref[dy, 0, 0:256, 0:192], NT)
        high += dot(w_ref[dy, 128:192], qe_ref[dy, 2, 256:512, 0:192], NT)
    return low, high


def inner_block(b, pre_ref, grad_ref, hid_ref, sh_ref):
    lane = lax.broadcasted_iota(jnp.int32, (64, 512), 1)
    inside = (lane >= 64) & (lane < 448)
    gap = jnp.zeros((64, 64), F32)
    pre = jnp.where(inside, pre_ref[b], 0.0)
    hidden = jnp.maximum(pre, 0.0)
    hid_ref[b] = hidden.astype(BF16)
    cols = slice(b * 512, b * 512 + 512)
    act = jnp.where(pre > 0, grad_ref[b], 0.0)
    sh_ref[0:64, cols] = jnp.concatenate([act[:, 64:512], gap], 1).astype(BF16)
    sh_ref[64:128, cols] = act.astype(BF16)
    sh_ref[128:192, cols] = jnp.concatenate([gap, act[:, 0:448]], 1).astype(BF16)


def edge_lanes(side):
    return slice(448, 512) if side else slice(0, 64)


def stash_edges(pre_ref, grad_ref, pe_ref, ge_ref):
    for side in range(2):
        at = edge_lanes(side)
        pe_ref[side] = jnp.concatenate([pre_ref[b, :, at] for b in range(4)], 1)
        ge_ref[side] = jnp.concatenate([grad_ref[b, :, at] for b in range(4)], 1)


def edge_planes(sums, pe_ref, ge_ref, ue_ref, hid_ref, dg_ref, down_ref):
    v = lax.broadcasted_iota(jnp.int32, (64, 256), 1)
    place = (v // 8 % 2) * 2 + v % 2
    first = lax.broadcasted_iota(jnp.int32, (64, 128), 1) < 64
    acts = []
    for side in range(2):
        pre = pe_ref[side] + sums[side]
        hidden = jnp.maximum(pre, 0.0)
        acts.append(jnp.where(pre > 0, ge_ref[side], 0.0))
        spread = jnp.concatenate([jnp.where(place == t, hidden, 0.0) for t in range(4)], 0)
        down = dg_ref[side * 256 : side * 256 + 256] + dot(spread.astype(BF16), ue_ref[side], NT)
        for p in range(NXY):
            down_ref[side, p] = down[p * 16 : p * 16 + 16]
        tile = slice(384, 512) if side else slice(0, 128)
        for b in range(4):
            mine = hidden[:, b // 2 * 128 : b // 2 * 128 + 128]
            if b % 2 != side:
                mine = pltpu.roll(mine, 64, 1)
            old = hid_ref[b, :, tile].astype(F32)
            hid_ref[b, :, tile] = jnp.where(first != (side == 1), mine, old).astype(BF16)
    return jnp.concatenate(acts, 1).astype(BF16)


def put_rows(v_ref, at, rows):
    for i in range(0, rows.shape[0], CONV_ROWS):
        p = (at + i) // CONV_ROWS
        v_ref[p // NXY, p % NXY] = rows[i : i + CONV_ROWS]


def conv_gradient(acts, qe_ref, cg_ref, conv_ref):
    plus = []
    for dy in range(3):
        parts = [
            cg_ref[dy, dx * 64 : dx * 64 + 64] + dot(acts, qe_ref[dy, dx], NN) for dx in range(3)
        ]
        grads = jnp.concatenate(parts, 0)
        put_rows(conv_ref, dy * 192, grads[:, 0:128])
        plus.append(grads[:, 128:256])
    first = lax.broadcasted_iota(jnp.int32, (192, 128), 1) < 64
    put_rows(conv_ref, 576, jnp.where(first, plus[0], plus[1]))
    put_rows(conv_ref, 768, plus[2])
    put_rows(conv_ref, 960, jnp.zeros((64, 128), F32))


def remote(src, dst, send, recv, peer):
    return pltpu.make_async_remote_copy(
        src, dst, send, recv, device_id=peer, device_id_type=MESH
    )


def section_kernel(
    nb_hbm, cnt_hbm, f_hbm, g_hbm, cw_hbm, dw_hbm, hid_ref, o_ref,
    nb_ref, cnt_ref, f_ref, g_ref, cw_ref, dw_ref, ho_ref, hi_in_ref, t_ref, lo_ref, hi_ref, q_ref, qe_ref, w_ref,
    s_ref, ga_ref, grad_ref, pre_ref, sh_ref, pe_ref, ge_ref, ue_ref, dg_ref, cg_ref,
    conv_ref, down_ref, mate_conv, mate_down, outgoing, parts, along,
    ls, hs, hr, cs, cr, ss, rs, zs, zr, gs, gr, es, er,
):
    strip, tile = lax.axis_index("space"), lax.axis_index("rep")
    z, rest = lax.div(strip, 8), lax.rem(strip, 8)
    y, x_hi = lax.div(rest, 2), lax.rem(rest, 2)
    x_lo, core = lax.div(tile, 2), lax.rem(tile, 2)
    x = x_hi * 2 + x_lo
    me = y * NX + x
    sibling = {"space": strip, "rep": x_lo * 2 + 1 - core}

    ys = [y] + [lax.rem(y + d, NY) for d in range(1, NY)]
    xs = [x] + [lax.rem(x + d, NX) for d in range(1, NX)]
    x_his = [lax.div(v, 2) for v in xs]
    tiles = [lax.rem(v, 2) * 2 + core for v in xs]
    rows = [z * 8 + v * 2 for v in ys]
    slots = [v * NX for v in ys]
    plane = [(dy, dx) for dy in range(NY) for dx in range(NX) if dy or dx]
    plane.sort(key=lambda o: -(min(o[0], NY - o[0]) + min(o[1], NX - o[1])))
    peers = {
        (dy, dx): ({"space": rows[dy] + x_his[dx], "rep": tiles[dx]}, slots[dy] + xs[dx])
        for dy, dx in plane
    }
    order = [peers[o] for o in plane]
    line = [{"space": lax.rem(z + d, NZ) * 8 + rest, "rep": tile} for d in (4, 3, 5, 2, 6, 1, 7)]
    strips = NX // 2 * NY * NZ
    above = {"space": lax.rem(strip + 1, strips), "rep": tile}
    below = {"space": lax.rem(strip + strips - 1, strips), "rep": tile}

    loads = [
        pltpu.make_async_copy(src, dst, ls.at[i])
        for i, (src, dst) in enumerate(
            ((f_hbm, f_ref), (cw_hbm, cw_ref), (g_hbm, g_ref), (dw_hbm, dw_ref), (nb_hbm, nb_ref), (cnt_hbm, cnt_ref))
        )
    ]
    loads[0].start()
    barrier = pltpu.get_barrier_semaphore()
    greet = [above, below] + [peer for peer, _ in order] + line + [sibling]
    for i, d in enumerate(greet):
        pl.semaphore_signal(barrier, inc=1, device_id=d, device_id_type=MESH)
        if i == 1:
            for c in loads[1:]:
                c.start()

    loads[0].wait()
    fill_tables(f_ref, t_ref, lo_ref, hi_ref)
    pack_halo(lo_ref, hi_ref, ho_ref)
    pl.semaphore_wait(barrier, len(greet))
    halo = [
        pltpu.make_async_remote_copy(
            ho_ref.at[0], hi_in_ref.at[0], hs.at[0], hr.at[0],
            device_id=above, device_id_type=MESH,
        ),
        pltpu.make_async_remote_copy(
            ho_ref.at[1], hi_in_ref.at[1], hs.at[1], hr.at[1],
            device_id=below, device_id_type=MESH,
        ),
    ]
    for c in halo:
        c.start()
    loads[1].wait()
    fill_weights(cw_ref, w_ref)
    fill_permutation(s_ref)
    for c in loads[2:]:
        c.wait()
    count = cnt_ref[0]
    cell_gradients(g_ref, dw_ref, count, s_ref, ga_ref, ue_ref, grad_ref)
    for b in range(4):
        fill_inner(nb_ref, count, b, t_ref, q_ref, qe_ref)
        inner_forward(b, w_ref, q_ref, pre_ref)
        inner_block(b, pre_ref, grad_ref, hid_ref, sh_ref)
    stash_edges(pre_ref, grad_ref, pe_ref, ge_ref)
    dg_ref[...] = inner_down(hid_ref, s_ref, ga_ref)
    for dy in range(3):
        cg_ref[dy] = dot(sh_ref[...], q_ref[dy], NN)

    for c in halo:
        c.wait()
    fill_halo(hi_in_ref, lo_ref, hi_ref)
    for b in range(4):
        fill_outer(nb_ref, b, lo_ref, hi_ref, qe_ref)
    sums = outer_forward(w_ref, qe_ref)

    acts = edge_planes(sums, pe_ref, ge_ref, ue_ref, hid_ref, dg_ref, down_ref)
    swap_down = remote(down_ref.at[1 - core], mate_down, cs.at[0], cr.at[0], sibling)
    swap_down.start()
    conv_gradient(acts, qe_ref, cg_ref, conv_ref)
    swap_conv = remote(conv_ref.at[1 - core], mate_conv, cs.at[1], cr.at[1], sibling)
    swap_conv.start()

    def summed(at):
        return (
            conv_ref[core, at] + mate_conv[at],
            down_ref[core, at] + mate_down[at],
        )

    swap_down.wait_recv()
    swap_conv.wait_recv()
    for i, (peer, at) in enumerate(order):
        conv, down = summed(at)
        outgoing[i, 0:CONV_ROWS] = conv.astype(BF16)
        outgoing[i, CONV_ROWS:ROWS] = down.astype(BF16)
        remote(outgoing.at[i], parts.at[i], ss.at[0], rs.at[0], peer).start()
    total = jnp.concatenate(summed(me), 0)
    scattered = remote(outgoing, parts, ss.at[0], rs.at[0], sibling)
    scattered.wait_recv()
    for i in range(NXY - 1):
        total = total + parts[i].astype(F32)

    along[z] = total.astype(BF16)
    for peer in line:
        remote(along.at[z], along.at[z], zs.at[0], zr.at[0], peer).start()
    swap_down.wait_send()
    swap_conv.wait_send()
    scattered.wait_send()
    most = along.at[pl.ds(0, NZ - 1)]
    spread = remote(most, most, zs.at[0], zr.at[0], sibling)
    spread.wait_recv()
    total = along[0].astype(F32)
    for i in range(1, NZ):
        total = total + along[i].astype(F32)

    half = core * NXY
    own = o_ref.at[half + me]
    o_ref[half + me] = total
    last = []
    for i, (peer, _) in enumerate(order):
        last.append(remote(own, own, gs.at[0], gr.at[i], peer))
        last[-1].start()
    remote(own, own, es.at[0], er.at[0], sibling).start()
    spread.wait_send()
    for i in reversed(range(NXY - 1)):
        last[i].wait_recv()
        _, at = peers[-plane[i][0] % NY, -plane[i][1] % NX]
        piece = o_ref.at[half + at]
        remote(piece, piece, es.at[0], er.at[0], sibling).start()
    sent = o_ref.at[pl.ds(half, NXY - 1)]
    remote(sent, sent, gs.at[0], gr.at[0], sibling).wait_send()
    block = o_ref.at[pl.ds(half, NXY)]
    remote(block, block, es.at[0], er.at[0], sibling).wait()


def section(features, neighbours, counts, cotangent, conv_weight, down_weight):
    dma = pltpu.SemaphoreType.DMA
    vm = pltpu.VMEM
    near = NXY - 1

    return pl.pallas_call(
        section_kernel,
        out_shape=(
            pltpu.VMEM((4, 64, 512), BF16),
            pltpu.VMEM((32, ROWS, 128), F32),
        ),
        in_specs=[ANY] * 6,
        out_specs=(VM, VM),
        scratch_shapes=[
            pltpu.SMEM((4, 27), jnp.int32), pltpu.SMEM((1,), jnp.int32),
            vm((4, 64, 512), BF16), vm((4, 64, 128), BF16), vm((27, 64, 64), BF16), vm((8, 64, 128), BF16),
            vm((2, 2, 64, 128), BF16), vm((2, 2, 64, 128), BF16),
            vm((5, 8, 8, 8, 128), F32), vm((9, 8, 8, 128), F32), vm((9, 8, 8, 128), F32),
            vm((3, 2048, 256), BF16), vm((3, 3, 512, 256), BF16), vm((3, 192, 192), BF16),
            vm((512, 512), BF16), vm((256, 128), BF16), vm((4, 64, 512), F32), vm((4, 64, 512), F32),
            vm((192, 2048), BF16),
            vm((2, 64, 256), F32), vm((2, 64, 256), F32), vm((2, 128, 256), BF16),
            vm((512, 128), F32), vm((3, 192, 256), F32),
            vm((2, NXY, CONV_ROWS, 128), F32), vm((2, NXY, DOWN_ROWS, 128), F32),
            vm((NXY, CONV_ROWS, 128), F32), vm((NXY, DOWN_ROWS, 128), F32),
            vm((near, ROWS, 128), BF16), vm((near, ROWS, 128), BF16), vm((NZ, ROWS, 128), BF16),
            dma((6,)), dma((2,)), dma((2,)), dma((2,)), dma((2,)), dma((1,)), dma((1,)),
            dma((1,)), dma((1,)), dma((1,)), dma((near,)), dma((1,)), dma((1,)),
        ],
        compiler_params=pltpu.CompilerParams(
            collective_id=0, has_side_effects=True, vmem_limit_bytes=56 << 20
        ),
        name="section",
    )(neighbours, counts, features, cotangent, conv_weight, down_weight)


def unpack_kernel(v_ref, hid_ref, conv_hbm, down_hbm, hid_hbm, conv_ref, sem):
    moves = [
        pltpu.make_async_copy(v_ref.at[:, pl.ds(CONV_ROWS, DOWN_ROWS), :], down_hbm, sem.at[0]),
        pltpu.make_async_copy(hid_ref, hid_hbm, sem.at[1]),
    ]
    for m in moves:
        m.start()
    conv = v_ref[:, 0:CONV_ROWS].reshape(1024, 128)
    for dx in range(3):
        for dy in range(3):
            at = dy * 192 + dx * 64
            pair = conv[at : at + 64]
            conv_ref[dx * 9 + dy * 3] = pair[:, 0:64]
            conv_ref[dx * 9 + dy * 3 + 1] = pair[:, 64:128]
            at = 768 + dx * 64 if dy == 2 else 576 + dx * 64
            side = 64 if dy == 1 else 0
            conv_ref[dx * 9 + dy * 3 + 2] = conv[at : at + 64, side : side + 64]
        part = pl.ds(dx * 9, 9)
        moves.append(
            pltpu.make_async_copy(conv_ref.at[part], conv_hbm.at[part], sem.at[2 + dx])
        )
        moves[-1].start()
    for m in moves:
        m.wait()


def unpack(pieces, hidden):
    return pl.pallas_call(
        unpack_kernel,
        out_shape=(
            jax.ShapeDtypeStruct((27, 64, 64), F32),
            jax.ShapeDtypeStruct((32, DOWN_ROWS, 128), F32),
            jax.ShapeDtypeStruct((4, 64, 512), BF16),
        ),
        in_specs=[VM, VM],
        out_specs=(ANY, ANY, ANY),
        scratch_shapes=[pltpu.VMEM((27, 64, 64), F32), pltpu.SemaphoreType.DMA((5,))],
        compiler_params=pltpu.CompilerParams(vmem_limit_bytes=48 << 20),
        name="unpack",
    )(pieces, hidden)


def body(features, neighbours, counts, cotangent, conv_weight, down_weight):
    down_rows = jnp.swapaxes(down_weight, 1, 2)
    hidden, pieces = section(features, neighbours, counts, cotangent, conv_weight, down_rows)
    conv_grad, down_grad, hidden = unpack(pieces, hidden)
    return hidden, conv_grad, jnp.swapaxes(down_grad.reshape(8, 64, 128), 1, 2)


def solution(mesh):
    both = ("space", "rep")
    return jax.shard_map(
        body,
        mesh=mesh,
        in_specs=(
            P(both, None, None), P(both, None), P(both), P(both, None, None), P(), P(),
        ),
        out_specs=(P(both, None, None), P(), P()),
        check_vma=False,
    )
```

```python
import jax
import jax.numpy as jnp
from jax import lax
from jax.experimental import pallas as pl
from jax.experimental.pallas import tpu as pltpu
from jax.sharding import PartitionSpec as P

MESH = pl.DeviceIdType.MESH
F32, BF16 = jnp.float32, jnp.bfloat16
VM = pl.BlockSpec(memory_space=pltpu.VMEM)
ANY = pl.BlockSpec(memory_space=pl.ANY)
NX, NY, NZ = 4, 4, 8
NXY = NX * NY
CONV_ROWS, DOWN_ROWS = 32, 16
ROWS = CONV_ROWS + DOWN_ROWS


def dot(a, b, dims):
    return lax.dot_general(a, b, (dims, ((), ())), preferred_element_type=F32)


NN, NT, TN = ((1,), (0,)), ((1,), (1,)), ((0,), (0,))


def voxels_in_rows(block):
    wide = block.astype(F32)
    return jnp.concatenate([wide, wide], 0).T


def fill_weights(cw_ref, w_ref):
    for dy in range(3):
        for dx in range(3):
            row = [cw_ref[dx * 9 + dy * 3 + dz].astype(F32) for dz in range(3)]
            w_ref[dy, dx * 64 : dx * 64 + 64, :] = jnp.concatenate(row, 1).astype(BF16)


def fill_tables(f_ref, t_ref, lo_ref, hi_ref):
    for j in range(4):
        for q in range(4):
            part = voxels_in_rows(f_ref[j, :, q * 128 : q * 128 + 128])
            t_ref[j, q * 2 : q * 2 + 2] = part.reshape(2, 8, 8, 128)
        lo_ref[j] = t_ref[j, 7]
        hi_ref[j] = t_ref[j, 0]
    t_ref[4] = jnp.zeros((8, 8, 8, 128), F32)
    lo_ref[8] = jnp.zeros((8, 8, 128), F32)
    hi_ref[8] = jnp.zeros((8, 8, 128), F32)


def first_half(shape):
    return lax.broadcasted_iota(jnp.int32, shape, 1) < 64


def pack_halo(lo_ref, hi_ref, out_ref):
    first = first_half((64, 128))
    for way, table in enumerate((lo_ref, hi_ref)):
        for j in range(0, 4, 2):
            pair = [table[j + i].reshape(64, 128) for i in range(2)]
            out_ref[way, j // 2] = jnp.where(first, *pair).astype(BF16)


def fill_halo(in_ref, lo_ref, hi_ref):
    first = first_half((64, 128))
    for way, table in enumerate((lo_ref, hi_ref)):
        for j in range(0, 4, 2):
            pair = in_ref[way, j // 2].astype(F32)
            turned = pltpu.roll(pair, 64, 1)
            table[4 + j] = jnp.where(first, pair, turned).reshape(8, 8, 128)
            table[5 + j] = jnp.where(first, turned, pair).reshape(8, 8, 128)


def store_plane(put, middle, below, above):
    z = lax.broadcasted_iota(jnp.int32, (10, 8, 128), 1)
    first = lax.broadcasted_iota(jnp.int32, (10, 8, 128), 2) < 64
    minus = pltpu.roll(jnp.where(z == 7, below, middle), 1, 1)
    plus = pltpu.roll(jnp.where(z == 0, above, middle), 7, 1)
    left = jnp.where(first, minus, middle)
    for dy in range(3):
        put(dy, 0, left[dy : dy + 8].reshape(64, 128).astype(BF16))
        put(dy, 128, plus[dy : dy + 8].reshape(64, 128).astype(BF16))


def link(nb_ref, b, ox, oy, oz, zero):
    j = nb_ref[b, (ox + 1) * 9 + (oy + 1) * 3 + oz + 1]
    return jnp.where(j < 0, zero, j)


def fill_inner(nb_ref, count, b, t_ref, q_ref, qe_ref):
    own = jnp.where(b < count, b, 4)
    idx = [[link(nb_ref, b, 0, oy, oz, 4) for oy in (-1, 0, 1)] for oz in (0, -1, 1)]
    idx[0][1] = own
    for xp in range(1, 9):
        cols = [
            jnp.concatenate(
                [t_ref[i0, xp - 1, 7:8], t_ref[i1, xp - 1], t_ref[i2, xp - 1, 0:1]], 0
            )
            for i0, i1, i2 in idx
        ]
        row, edge = b * 512 + (xp - 1) * 64, b * 64

        def put(dy, lane, rows, row=row, edge=edge, xp=xp):
            q_ref[dy, row : row + 64, lane : lane + 128] = rows
            if xp in (1, 2):
                qe_ref[dy, xp, edge : edge + 64, lane : lane + 128] = rows
            if xp in (7, 8):
                qe_ref[dy, xp - 7, 256 + edge : 320 + edge, lane : lane + 128] = rows

        store_plane(put, *cols)


def fill_outer(nb_ref, b, lo_ref, hi_ref, qe_ref):
    for ox, side, table in ((-1, 0, lo_ref), (1, 1, hi_ref)):
        cols = []
        for oz in (0, -1, 1):
            i0, i1, i2 = [link(nb_ref, b, ox, oy, oz, 8) for oy in (-1, 0, 1)]
            cols.append(jnp.concatenate([table[i0, 7:8], table[i1], table[i2, 0:1]], 0))

        row = side * 256 + b * 64

        def put(dy, lane, rows, side=side, row=row):
            qe_ref[dy, 2 * side, row : row + 64, lane : lane + 128] = rows

        store_plane(put, *cols)


def regroup(m, outer, inner):
    first = first_half((64, 128))
    out = []
    for i in range(0, inner, 2):
        even, odd = [], []
        for o in range(0, outer, 2):
            x0 = m[o * 64 : o * 64 + 64, i * 64 : i * 64 + 128]
            x1 = m[o * 64 + 64 : o * 64 + 128, i * 64 : i * 64 + 128]
            even.append(jnp.where(first, x0, pltpu.roll(x1, 64, 1)))
            odd.append(jnp.where(first, pltpu.roll(x0, 64, 1), x1))
        out += [jnp.concatenate(even, 1), jnp.concatenate(odd, 1)]
    return jnp.concatenate(out, 0)


def fill_permutation(s_ref):
    v = lax.broadcasted_iota(jnp.int32, (64, 512), 1)
    u = lax.broadcasted_iota(jnp.int32, (64, 512), 0)
    place = (v // 64 % 2) * 4 + (v // 8 % 2) * 2 + v % 2
    cell = (v // 128) * 16 + (v // 16 % 4) * 4 + v % 8 // 2
    at = place * 64 + cell - u
    for t in range(8):
        s_ref[t * 64 : t * 64 + 64] = (at == t * 64).astype(F32).astype(BF16)


def cell_gradients(g_ref, dw_ref, count, s_ref, ga_ref, ue_ref, grad_ref):
    slot = lax.broadcasted_iota(jnp.int32, (256, 128), 0) // 64
    grads = jnp.where(slot < count, g_ref[...].reshape(256, 128).astype(F32), 0.0)
    ga_ref[...] = grads.astype(BF16)
    every = dot(dw_ref[...].reshape(512, 128), ga_ref[...], NT)
    every = regroup(every, 8, 4).astype(BF16)
    grad_ref[...] = dot(every, s_ref[...], NN).reshape(4, 64, 512)
    r = lax.broadcasted_iota(jnp.int32, (256, 256), 0)
    v = lax.broadcasted_iota(jnp.int32, (256, 256), 1)
    cell = v // 64 * 64 + v // 16 % 4 * 4 + v % 8 // 2
    turned = grads.T.astype(BF16)
    for side in range(2):
        spread = (r == cell + 48 * side).astype(F32).astype(BF16)
        ue_ref[side] = dot(turned, spread, NN).astype(BF16)


def inner_down(hid_ref, s_ref, ga_ref):
    cells = dot(hid_ref[...].reshape(256, 512), s_ref[...], NT)
    return dot(regroup(cells, 4, 8).astype(BF16), ga_ref[...], NN)


def inner_forward(b, w_ref, q_ref, pre_ref):
    acc = jnp.zeros((192, 512), F32)
    for dy in range(3):
        acc += dot(w_ref[dy], q_ref[dy, b * 512 : b * 512 + 512, 0:192], NT)
    gap = jnp.zeros((64, 64), F32)
    low = jnp.concatenate([gap, acc[0:64, 0:448]], 1)
    high = jnp.concatenate([acc[128:192, 64:512], gap], 1)
    pre_ref[b] = acc[64:128] + low + high


def outer_forward(w_ref, qe_ref):
    low, high = jnp.zeros((64, 256), F32), jnp.zeros((64, 256), F32)
    for dy in range(3):
        low += dot(w_ref[dy, 0:64], qe_ref[dy, 0, 0:256, 0:192], NT)
        high += dot(w_ref[dy, 128:192], qe_ref[dy, 2, 256:512, 0:192], NT)
    return low, high


def inner_block(b, pre_ref, grad_ref, hid_ref, sh_ref):
    lane = lax.broadcasted_iota(jnp.int32, (64, 512), 1)
    inside = (lane >= 64) & (lane < 448)
    gap = jnp.zeros((64, 64), F32)
    pre = jnp.where(inside, pre_ref[b], 0.0)
    hidden = jnp.maximum(pre, 0.0)
    hid_ref[b] = hidden.astype(BF16)
    cols = slice(b * 512, b * 512 + 512)
    act = jnp.where(pre > 0, grad_ref[b], 0.0)
    sh_ref[0:64, cols] = jnp.concatenate([act[:, 64:512], gap], 1).astype(BF16)
    sh_ref[64:128, cols] = act.astype(BF16)
    sh_ref[128:192, cols] = jnp.concatenate([gap, act[:, 0:448]], 1).astype(BF16)


def edge_lanes(side):
    return slice(448, 512) if side else slice(0, 64)


def stash_edges(pre_ref, grad_ref, pe_ref, ge_ref):
    for side in range(2):
        at = edge_lanes(side)
        pe_ref[side] = jnp.concatenate([pre_ref[b, :, at] for b in range(4)], 1)
        ge_ref[side] = jnp.concatenate([grad_ref[b, :, at] for b in range(4)], 1)


def edge_planes(sums, pe_ref, ge_ref, ue_ref, hid_ref, dg_ref, down_ref):
    v = lax.broadcasted_iota(jnp.int32, (64, 256), 1)
    place = (v // 8 % 2) * 2 + v % 2
    first = lax.broadcasted_iota(jnp.int32, (64, 128), 1) < 64
    acts = []
    for side in range(2):
        pre = pe_ref[side] + sums[side]
        hidden = jnp.maximum(pre, 0.0)
        acts.append(jnp.where(pre > 0, ge_ref[side], 0.0))
        spread = jnp.concatenate([jnp.where(place == t, hidden, 0.0) for t in range(4)], 0)
        down = dg_ref[side * 256 : side * 256 + 256] + dot(spread.astype(BF16), ue_ref[side], NT)
        for p in range(NXY):
            down_ref[side, p] = down[p * 16 : p * 16 + 16]
        tile = slice(384, 512) if side else slice(0, 128)
        for b in range(4):
            mine = hidden[:, b // 2 * 128 : b // 2 * 128 + 128]
            if b % 2 != side:
                mine = pltpu.roll(mine, 64, 1)
            old = hid_ref[b, :, tile].astype(F32)
            hid_ref[b, :, tile] = jnp.where(first != (side == 1), mine, old).astype(BF16)
    return jnp.concatenate(acts, 1).astype(BF16)


def put_rows(v_ref, at, rows):
    for i in range(0, rows.shape[0], CONV_ROWS):
        p = (at + i) // CONV_ROWS
        v_ref[p // NXY, p % NXY] = rows[i : i + CONV_ROWS]


def conv_gradient(acts, qe_ref, cg_ref, conv_ref):
    plus = []
    for dy in range(3):
        parts = [
            cg_ref[dy, dx * 64 : dx * 64 + 64] + dot(acts, qe_ref[dy, dx], NN) for dx in range(3)
        ]
        grads = jnp.concatenate(parts, 0)
        put_rows(conv_ref, dy * 192, grads[:, 0:128])
        plus.append(grads[:, 128:256])
    first = lax.broadcasted_iota(jnp.int32, (192, 128), 1) < 64
    put_rows(conv_ref, 576, jnp.where(first, plus[0], plus[1]))
    put_rows(conv_ref, 768, plus[2])
    put_rows(conv_ref, 960, jnp.zeros((64, 128), F32))


def remote(src, dst, send, recv, peer):
    return pltpu.make_async_remote_copy(
        src, dst, send, recv, device_id=peer, device_id_type=MESH
    )


def section_kernel(
    nb_hbm, cnt_hbm, f_hbm, g_hbm, cw_hbm, dw_hbm, hid_ref, o_ref,
    nb_ref, cnt_ref, f_ref, g_ref, cw_ref, dw_ref, ho_ref, hi_in_ref, t_ref, lo_ref, hi_ref, q_ref, qe_ref, w_ref,
    s_ref, ga_ref, grad_ref, pre_ref, sh_ref, pe_ref, ge_ref, ue_ref, dg_ref, cg_ref,
    conv_ref, down_ref, mate_conv, mate_down, outgoing, parts, along,
    ls, hs, hr, cs, cr, ss, rs, zs, zr, gs, gr, es, er,
):
    strip, tile = lax.axis_index("space"), lax.axis_index("rep")
    z, rest = lax.div(strip, 8), lax.rem(strip, 8)
    y, x_hi = lax.div(rest, 2), lax.rem(rest, 2)
    x_lo, core = lax.div(tile, 2), lax.rem(tile, 2)
    x = x_hi * 2 + x_lo
    me = y * NX + x
    sibling = {"space": strip, "rep": x_lo * 2 + 1 - core}

    ys = [y] + [lax.rem(y + d, NY) for d in range(1, NY)]
    xs = [x] + [lax.rem(x + d, NX) for d in range(1, NX)]
    x_his = [lax.div(v, 2) for v in xs]
    tiles = [lax.rem(v, 2) * 2 + core for v in xs]
    rows = [z * 8 + v * 2 for v in ys]
    slots = [v * NX for v in ys]
    plane = [(dy, dx) for dy in range(NY) for dx in range(NX) if dy or dx]
    plane.sort(key=lambda o: -(min(o[0], NY - o[0]) + min(o[1], NX - o[1])))
    plane = [plane[i] for i in (0, 1, 4, 2, 3, 6, 7, 9, 10, 5, 8, 11, 14, 12, 13)]
    peers = {
        (dy, dx): ({"space": rows[dy] + x_his[dx], "rep": tiles[dx]}, slots[dy] + xs[dx])
        for dy, dx in plane
    }
    order = [peers[o] for o in plane]
    line = [{"space": lax.rem(z + d, NZ) * 8 + rest, "rep": tile} for d in (4, 3, 5, 2, 6, 1, 7)]
    strips = NX // 2 * NY * NZ
    above = {"space": lax.rem(strip + 1, strips), "rep": tile}
    below = {"space": lax.rem(strip + strips - 1, strips), "rep": tile}

    loads = [
        pltpu.make_async_copy(src, dst, ls.at[i])
        for i, (src, dst) in enumerate(
            ((f_hbm, f_ref), (cw_hbm, cw_ref), (g_hbm, g_ref), (dw_hbm, dw_ref), (nb_hbm, nb_ref), (cnt_hbm, cnt_ref))
        )
    ]
    loads[0].start()
    barrier = pltpu.get_barrier_semaphore()
    greet = [above, below] + [peer for peer, _ in order] + line + [sibling]
    for i, d in enumerate(greet):
        pl.semaphore_signal(barrier, inc=1, device_id=d, device_id_type=MESH)
        if i == 1:
            for c in loads[1:]:
                c.start()

    loads[0].wait()
    fill_tables(f_ref, t_ref, lo_ref, hi_ref)
    pack_halo(lo_ref, hi_ref, ho_ref)
    pl.semaphore_wait(barrier, len(greet))
    halo = [
        pltpu.make_async_remote_copy(
            ho_ref.at[0], hi_in_ref.at[0], hs.at[0], hr.at[0],
            device_id=above, device_id_type=MESH,
        ),
        pltpu.make_async_remote_copy(
            ho_ref.at[1], hi_in_ref.at[1], hs.at[1], hr.at[1],
            device_id=below, device_id_type=MESH,
        ),
    ]
    for c in halo:
        c.start()
    loads[1].wait()
    fill_weights(cw_ref, w_ref)
    fill_permutation(s_ref)
    for c in loads[2:]:
        c.wait()
    count = cnt_ref[0]
    cell_gradients(g_ref, dw_ref, count, s_ref, ga_ref, ue_ref, grad_ref)
    for b in range(4):
        fill_inner(nb_ref, count, b, t_ref, q_ref, qe_ref)
        inner_forward(b, w_ref, q_ref, pre_ref)
        inner_block(b, pre_ref, grad_ref, hid_ref, sh_ref)
    stash_edges(pre_ref, grad_ref, pe_ref, ge_ref)
    dg_ref[...] = inner_down(hid_ref, s_ref, ga_ref)
    for dy in range(3):
        cg_ref[dy] = dot(sh_ref[...], q_ref[dy], NN)

    for c in halo:
        c.wait()
    fill_halo(hi_in_ref, lo_ref, hi_ref)
    for b in range(4):
        fill_outer(nb_ref, b, lo_ref, hi_ref, qe_ref)
    sums = outer_forward(w_ref, qe_ref)

    acts = edge_planes(sums, pe_ref, ge_ref, ue_ref, hid_ref, dg_ref, down_ref)
    swap_down = remote(down_ref.at[1 - core], mate_down, cs.at[0], cr.at[0], sibling)
    swap_down.start()
    conv_gradient(acts, qe_ref, cg_ref, conv_ref)
    swap_conv = remote(conv_ref.at[1 - core], mate_conv, cs.at[1], cr.at[1], sibling)
    swap_conv.start()

    def summed(at):
        return (
            conv_ref[core, at] + mate_conv[at],
            down_ref[core, at] + mate_down[at],
        )

    swap_down.wait_recv()
    swap_conv.wait_recv()
    for i, (peer, at) in enumerate(order):
        conv, down = summed(at)
        outgoing[i, 0:CONV_ROWS] = conv.astype(BF16)
        outgoing[i, CONV_ROWS:ROWS] = down.astype(BF16)
        remote(outgoing.at[i], parts.at[i], ss.at[0], rs.at[0], peer).start()
    total = jnp.concatenate(summed(me), 0)
    scattered = remote(outgoing, parts, ss.at[0], rs.at[0], sibling)
    scattered.wait_recv()
    for i in range(NXY - 1):
        total = total + parts[i].astype(F32)

    along[z] = total.astype(BF16)
    for peer in line:
        remote(along.at[z], along.at[z], zs.at[0], zr.at[0], peer).start()
    swap_down.wait_send()
    swap_conv.wait_send()
    scattered.wait_send()
    most = along.at[pl.ds(0, NZ - 1)]
    spread = remote(most, most, zs.at[0], zr.at[0], sibling)
    spread.wait_recv()
    total = along[0].astype(F32)
    for i in range(1, NZ):
        total = total + along[i].astype(F32)

    half = core * NXY
    own = o_ref.at[half + me]
    o_ref[half + me] = total
    last = []
    for i, (peer, _) in enumerate(order):
        last.append(remote(own, own, gs.at[0], gr.at[i], peer))
        last[-1].start()
    remote(own, own, es.at[0], er.at[0], sibling).start()
    spread.wait_send()
    for i in reversed(range(NXY - 1)):
        last[i].wait_recv()
        _, at = peers[-plane[i][0] % NY, -plane[i][1] % NX]
        piece = o_ref.at[half + at]
        remote(piece, piece, es.at[0], er.at[0], sibling).start()
    sent = o_ref.at[pl.ds(half, NXY - 1)]
    remote(sent, sent, gs.at[0], gr.at[0], sibling).wait_send()
    block = o_ref.at[pl.ds(half, NXY)]
    remote(block, block, es.at[0], er.at[0], sibling).wait()


def section(features, neighbours, counts, cotangent, conv_weight, down_weight):
    dma = pltpu.SemaphoreType.DMA
    vm = pltpu.VMEM
    near = NXY - 1

    return pl.pallas_call(
        section_kernel,
        out_shape=(
            pltpu.VMEM((4, 64, 512), BF16),
            pltpu.VMEM((32, ROWS, 128), F32),
        ),
        in_specs=[ANY] * 6,
        out_specs=(VM, VM),
        scratch_shapes=[
            pltpu.SMEM((4, 27), jnp.int32), pltpu.SMEM((1,), jnp.int32),
            vm((4, 64, 512), BF16), vm((4, 64, 128), BF16), vm((27, 64, 64), BF16), vm((8, 64, 128), BF16),
            vm((2, 2, 64, 128), BF16), vm((2, 2, 64, 128), BF16),
            vm((5, 8, 8, 8, 128), F32), vm((9, 8, 8, 128), F32), vm((9, 8, 8, 128), F32),
            vm((3, 2048, 256), BF16), vm((3, 3, 512, 256), BF16), vm((3, 192, 192), BF16),
            vm((512, 512), BF16), vm((256, 128), BF16), vm((4, 64, 512), F32), vm((4, 64, 512), F32),
            vm((192, 2048), BF16),
            vm((2, 64, 256), F32), vm((2, 64, 256), F32), vm((2, 128, 256), BF16),
            vm((512, 128), F32), vm((3, 192, 256), F32),
            vm((2, NXY, CONV_ROWS, 128), F32), vm((2, NXY, DOWN_ROWS, 128), F32),
            vm((NXY, CONV_ROWS, 128), F32), vm((NXY, DOWN_ROWS, 128), F32),
            vm((near, ROWS, 128), BF16), vm((near, ROWS, 128), BF16), vm((NZ, ROWS, 128), BF16),
            dma((6,)), dma((2,)), dma((2,)), dma((2,)), dma((2,)), dma((1,)), dma((1,)),
            dma((1,)), dma((1,)), dma((1,)), dma((near,)), dma((1,)), dma((1,)),
        ],
        compiler_params=pltpu.CompilerParams(
            collective_id=0, has_side_effects=True, vmem_limit_bytes=56 << 20
        ),
        name="section",
    )(neighbours, counts, features, cotangent, conv_weight, down_weight)


def unpack_kernel(v_ref, hid_ref, conv_hbm, down_hbm, hid_hbm, conv_ref, sem):
    moves = [
        pltpu.make_async_copy(v_ref.at[:, pl.ds(CONV_ROWS, DOWN_ROWS), :], down_hbm, sem.at[0]),
        pltpu.make_async_copy(hid_ref, hid_hbm, sem.at[1]),
    ]
    for m in moves:
        m.start()
    conv = v_ref[:, 0:CONV_ROWS].reshape(1024, 128)
    for dx in range(3):
        for dy in range(3):
            at = dy * 192 + dx * 64
            pair = conv[at : at + 64]
            conv_ref[dx * 9 + dy * 3] = pair[:, 0:64]
            conv_ref[dx * 9 + dy * 3 + 1] = pair[:, 64:128]
            at = 768 + dx * 64 if dy == 2 else 576 + dx * 64
            side = 64 if dy == 1 else 0
            conv_ref[dx * 9 + dy * 3 + 2] = conv[at : at + 64, side : side + 64]
        part = pl.ds(dx * 9, 9)
        moves.append(
            pltpu.make_async_copy(conv_ref.at[part], conv_hbm.at[part], sem.at[2 + dx])
        )
        moves[-1].start()
    for m in moves:
        m.wait()


def unpack(pieces, hidden):
    return pl.pallas_call(
        unpack_kernel,
        out_shape=(
            jax.ShapeDtypeStruct((27, 64, 64), F32),
            jax.ShapeDtypeStruct((32, DOWN_ROWS, 128), F32),
            jax.ShapeDtypeStruct((4, 64, 512), BF16),
        ),
        in_specs=[VM, VM],
        out_specs=(ANY, ANY, ANY),
        scratch_shapes=[pltpu.VMEM((27, 64, 64), F32), pltpu.SemaphoreType.DMA((5,))],
        compiler_params=pltpu.CompilerParams(vmem_limit_bytes=48 << 20),
        name="unpack",
    )(pieces, hidden)


def body(features, neighbours, counts, cotangent, conv_weight, down_weight):
    down_rows = jnp.swapaxes(down_weight, 1, 2)
    hidden, pieces = section(features, neighbours, counts, cotangent, conv_weight, down_rows)
    conv_grad, down_grad, hidden = unpack(pieces, hidden)
    return hidden, conv_grad, jnp.swapaxes(down_grad.reshape(8, 64, 128), 1, 2)


def solution(mesh):
    both = ("space", "rep")
    return jax.shard_map(
        body,
        mesh=mesh,
        in_specs=(
            P(both, None, None), P(both, None), P(both), P(both, None, None), P(), P(),
        ),
        out_specs=(P(both, None, None), P(), P()),
        check_vma=False,
    )
```

```python
import jax
import jax.numpy as jnp
from jax import lax
from jax.experimental import pallas as pl
from jax.experimental.pallas import tpu as pltpu
from jax.sharding import PartitionSpec as P

MESH = pl.DeviceIdType.MESH
F32, BF16 = jnp.float32, jnp.bfloat16
VM = pl.BlockSpec(memory_space=pltpu.VMEM)
ANY = pl.BlockSpec(memory_space=pl.ANY)
NX, NY, NZ = 4, 4, 8
NXY = NX * NY
CONV_ROWS, DOWN_ROWS = 32, 16
ROWS = CONV_ROWS + DOWN_ROWS
FAR = 5


def dot(a, b, dims):
    return lax.dot_general(a, b, (dims, ((), ())), preferred_element_type=F32)


NN, NT, TN = ((1,), (0,)), ((1,), (1,)), ((0,), (0,))


def voxels_in_rows(block):
    wide = block.astype(F32)
    return jnp.concatenate([wide, wide], 0).T


def fill_weights(cw_ref, w_ref):
    for dy in range(3):
        for dx in range(3):
            row = [cw_ref[dx * 9 + dy * 3 + dz].astype(F32) for dz in range(3)]
            w_ref[dy, dx * 64 : dx * 64 + 64, :] = jnp.concatenate(row, 1).astype(BF16)


def fill_tables(f_ref, t_ref, lo_ref, hi_ref):
    for j in range(4):
        for q in range(4):
            part = voxels_in_rows(f_ref[j, :, q * 128 : q * 128 + 128])
            t_ref[j, q * 2 : q * 2 + 2] = part.reshape(2, 8, 8, 128)
        lo_ref[j] = t_ref[j, 7]
        hi_ref[j] = t_ref[j, 0]
    t_ref[4] = jnp.zeros((8, 8, 8, 128), F32)
    lo_ref[8] = jnp.zeros((8, 8, 128), F32)
    hi_ref[8] = jnp.zeros((8, 8, 128), F32)


def first_half(shape):
    return lax.broadcasted_iota(jnp.int32, shape, 1) < 64


def pack_halo(lo_ref, hi_ref, out_ref):
    first = first_half((64, 128))
    for way, table in enumerate((lo_ref, hi_ref)):
        for j in range(0, 4, 2):
            pair = [table[j + i].reshape(64, 128) for i in range(2)]
            out_ref[way, j // 2] = jnp.where(first, *pair).astype(BF16)


def fill_halo(in_ref, lo_ref, hi_ref):
    first = first_half((64, 128))
    for way, table in enumerate((lo_ref, hi_ref)):
        for j in range(0, 4, 2):
            pair = in_ref[way, j // 2].astype(F32)
            turned = pltpu.roll(pair, 64, 1)
            table[4 + j] = jnp.where(first, pair, turned).reshape(8, 8, 128)
            table[5 + j] = jnp.where(first, turned, pair).reshape(8, 8, 128)


def store_plane(put, middle, below, above):
    z = lax.broadcasted_iota(jnp.int32, (10, 8, 128), 1)
    first = lax.broadcasted_iota(jnp.int32, (10, 8, 128), 2) < 64
    minus = pltpu.roll(jnp.where(z == 7, below, middle), 1, 1)
    plus = pltpu.roll(jnp.where(z == 0, above, middle), 7, 1)
    left = jnp.where(first, minus, middle)
    for dy in range(3):
        put(dy, 0, left[dy : dy + 8].reshape(64, 128).astype(BF16))
        put(dy, 128, plus[dy : dy + 8].reshape(64, 128).astype(BF16))


def link(nb_ref, b, ox, oy, oz, zero):
    j = nb_ref[b, (ox + 1) * 9 + (oy + 1) * 3 + oz + 1]
    return jnp.where(j < 0, zero, j)


def fill_inner(nb_ref, count, b, t_ref, q_ref, qe_ref):
    own = jnp.where(b < count, b, 4)
    idx = [[link(nb_ref, b, 0, oy, oz, 4) for oy in (-1, 0, 1)] for oz in (0, -1, 1)]
    idx[0][1] = own
    for xp in range(1, 9):
        cols = [
            jnp.concatenate(
                [t_ref[i0, xp - 1, 7:8], t_ref[i1, xp - 1], t_ref[i2, xp - 1, 0:1]], 0
            )
            for i0, i1, i2 in idx
        ]
        row, edge = b * 512 + (xp - 1) * 64, b * 64

        def put(dy, lane, rows, row=row, edge=edge, xp=xp):
            q_ref[dy, row : row + 64, lane : lane + 128] = rows
            if xp in (1, 2):
                qe_ref[dy, xp, edge : edge + 64, lane : lane + 128] = rows
            if xp in (7, 8):
                qe_ref[dy, xp - 7, 256 + edge : 320 + edge, lane : lane + 128] = rows

        store_plane(put, *cols)


def fill_outer(nb_ref, b, lo_ref, hi_ref, qe_ref):
    for ox, side, table in ((-1, 0, lo_ref), (1, 1, hi_ref)):
        cols = []
        for oz in (0, -1, 1):
            i0, i1, i2 = [link(nb_ref, b, ox, oy, oz, 8) for oy in (-1, 0, 1)]
            cols.append(jnp.concatenate([table[i0, 7:8], table[i1], table[i2, 0:1]], 0))

        row = side * 256 + b * 64

        def put(dy, lane, rows, side=side, row=row):
            qe_ref[dy, 2 * side, row : row + 64, lane : lane + 128] = rows

        store_plane(put, *cols)


def regroup(m, outer, inner):
    first = first_half((64, 128))
    out = []
    for i in range(0, inner, 2):
        even, odd = [], []
        for o in range(0, outer, 2):
            x0 = m[o * 64 : o * 64 + 64, i * 64 : i * 64 + 128]
            x1 = m[o * 64 + 64 : o * 64 + 128, i * 64 : i * 64 + 128]
            even.append(jnp.where(first, x0, pltpu.roll(x1, 64, 1)))
            odd.append(jnp.where(first, pltpu.roll(x0, 64, 1), x1))
        out += [jnp.concatenate(even, 1), jnp.concatenate(odd, 1)]
    return jnp.concatenate(out, 0)


def fill_permutation(s_ref):
    v = lax.broadcasted_iota(jnp.int32, (64, 512), 1)
    u = lax.broadcasted_iota(jnp.int32, (64, 512), 0)
    place = (v // 64 % 2) * 4 + (v // 8 % 2) * 2 + v % 2
    cell = (v // 128) * 16 + (v // 16 % 4) * 4 + v % 8 // 2
    at = place * 64 + cell - u
    for t in range(8):
        s_ref[t * 64 : t * 64 + 64] = (at == t * 64).astype(F32).astype(BF16)


def cell_gradients(g_ref, dw_ref, count, s_ref, ga_ref, ue_ref, grad_ref):
    slot = lax.broadcasted_iota(jnp.int32, (256, 128), 0) // 64
    grads = jnp.where(slot < count, g_ref[...].reshape(256, 128).astype(F32), 0.0)
    ga_ref[...] = grads.astype(BF16)
    every = dot(dw_ref[...].reshape(512, 128), ga_ref[...], NT)
    every = regroup(every, 8, 4).astype(BF16)
    grad_ref[...] = dot(every, s_ref[...], NN).reshape(4, 64, 512)
    r = lax.broadcasted_iota(jnp.int32, (256, 256), 0)
    v = lax.broadcasted_iota(jnp.int32, (256, 256), 1)
    cell = v // 64 * 64 + v // 16 % 4 * 4 + v % 8 // 2
    turned = grads.T.astype(BF16)
    for side in range(2):
        spread = (r == cell + 48 * side).astype(F32).astype(BF16)
        ue_ref[side] = dot(turned, spread, NN).astype(BF16)


def inner_down(hid_ref, s_ref, ga_ref):
    cells = dot(hid_ref[...].reshape(256, 512), s_ref[...], NT)
    return dot(regroup(cells, 4, 8).astype(BF16), ga_ref[...], NN)


def inner_forward(b, w_ref, q_ref, pre_ref):
    acc = jnp.zeros((192, 512), F32)
    for dy in range(3):
        acc += dot(w_ref[dy], q_ref[dy, b * 512 : b * 512 + 512, 0:192], NT)
    gap = jnp.zeros((64, 64), F32)
    low = jnp.concatenate([gap, acc[0:64, 0:448]], 1)
    high = jnp.concatenate([acc[128:192, 64:512], gap], 1)
    pre_ref[b] = acc[64:128] + low + high


def outer_forward(w_ref, qe_ref):
    low, high = jnp.zeros((64, 256), F32), jnp.zeros((64, 256), F32)
    for dy in range(3):
        low += dot(w_ref[dy, 0:64], qe_ref[dy, 0, 0:256, 0:192], NT)
        high += dot(w_ref[dy, 128:192], qe_ref[dy, 2, 256:512, 0:192], NT)
    return low, high


def inner_block(b, pre_ref, grad_ref, hid_ref, sh_ref):
    lane = lax.broadcasted_iota(jnp.int32, (64, 512), 1)
    inside = (lane >= 64) & (lane < 448)
    gap = jnp.zeros((64, 64), F32)
    pre = jnp.where(inside, pre_ref[b], 0.0)
    hidden = jnp.maximum(pre, 0.0)
    hid_ref[b] = hidden.astype(BF16)
    cols = slice(b * 512, b * 512 + 512)
    act = jnp.where(pre > 0, grad_ref[b], 0.0)
    sh_ref[0:64, cols] = jnp.concatenate([act[:, 64:512], gap], 1).astype(BF16)
    sh_ref[64:128, cols] = act.astype(BF16)
    sh_ref[128:192, cols] = jnp.concatenate([gap, act[:, 0:448]], 1).astype(BF16)


def edge_lanes(side):
    return slice(448, 512) if side else slice(0, 64)


def stash_edges(pre_ref, grad_ref, pe_ref, ge_ref):
    for side in range(2):
        at = edge_lanes(side)
        pe_ref[side] = jnp.concatenate([pre_ref[b, :, at] for b in range(4)], 1)
        ge_ref[side] = jnp.concatenate([grad_ref[b, :, at] for b in range(4)], 1)


def edge_planes(sums, pe_ref, ge_ref, ue_ref, dg_ref, down_ref):
    v = lax.broadcasted_iota(jnp.int32, (64, 256), 1)
    place = (v // 8 % 2) * 2 + v % 2
    acts = []
    for side in range(2):
        pre = pe_ref[side] + sums[side]
        hidden = jnp.maximum(pre, 0.0)
        acts.append(jnp.where(pre > 0, ge_ref[side], 0.0))
        spread = jnp.concatenate([jnp.where(place == t, hidden, 0.0) for t in range(4)], 0)
        down = dg_ref[side * 256 : side * 256 + 256] + dot(spread.astype(BF16), ue_ref[side], NT)
        for p in range(NXY):
            down_ref[side, p] = down[p * 16 : p * 16 + 16]
    return jnp.concatenate(acts, 1).astype(BF16)


def edge_hidden(sums, pe_ref, hid_ref):
    first = first_half((64, 128))
    for side in range(2):
        hidden = jnp.maximum(pe_ref[side] + sums[side], 0.0)
        tile = slice(384, 512) if side else slice(0, 128)
        for b in range(4):
            mine = hidden[:, b // 2 * 128 : b // 2 * 128 + 128]
            if b % 2 != side:
                mine = pltpu.roll(mine, 64, 1)
            old = hid_ref[b, :, tile].astype(F32)
            hid_ref[b, :, tile] = jnp.where(first != (side == 1), mine, old).astype(BF16)


def put_rows(v_ref, at, rows):
    for i in range(0, rows.shape[0], CONV_ROWS):
        p = (at + i) // CONV_ROWS
        v_ref[p // NXY, p % NXY] = rows[i : i + CONV_ROWS]


def conv_gradient(acts, qe_ref, cg_ref, conv_ref):
    plus = []
    for dy in range(3):
        parts = [
            cg_ref[dy, dx * 64 : dx * 64 + 64] + dot(acts, qe_ref[dy, dx], NN) for dx in range(3)
        ]
        grads = jnp.concatenate(parts, 0)
        put_rows(conv_ref, dy * 192, grads[:, 0:128])
        plus.append(grads[:, 128:256])
    first = lax.broadcasted_iota(jnp.int32, (192, 128), 1) < 64
    put_rows(conv_ref, 576, jnp.where(first, plus[0], plus[1]))
    put_rows(conv_ref, 768, plus[2])
    put_rows(conv_ref, 960, jnp.zeros((64, 128), F32))


def remote(src, dst, send, recv, peer):
    return pltpu.make_async_remote_copy(
        src, dst, send, recv, device_id=peer, device_id_type=MESH
    )


def section_kernel(
    nb_hbm, cnt_hbm, f_hbm, g_hbm, cw_hbm, dw_hbm, hid_ref, o_ref,
    nb_ref, cnt_ref, f_ref, g_ref, cw_ref, dw_ref, ho_ref, hi_in_ref, t_ref, lo_ref, hi_ref, q_ref, qe_ref, w_ref,
    s_ref, ga_ref, grad_ref, pre_ref, sh_ref, pe_ref, ge_ref, ue_ref, dg_ref, cg_ref,
    conv_ref, down_ref, mate_conv, mate_down, outgoing, parts, far_out, far_in, along,
    ls, hs, hr, cs, cr, ss, rs, zs, zr, gs, gr, es, er, fs, fr,
):
    strip, tile = lax.axis_index("space"), lax.axis_index("rep")
    z, rest = lax.div(strip, 8), lax.rem(strip, 8)
    y, x_hi = lax.div(rest, 2), lax.rem(rest, 2)
    x_lo, core = lax.div(tile, 2), lax.rem(tile, 2)
    x = x_hi * 2 + x_lo
    me = y * NX + x
    sibling = {"space": strip, "rep": x_lo * 2 + 1 - core}

    ys = [y] + [lax.rem(y + d, NY) for d in range(1, NY)]
    xs = [x] + [lax.rem(x + d, NX) for d in range(1, NX)]
    x_his = [lax.div(v, 2) for v in xs]
    tiles = [lax.rem(v, 2) * 2 + core for v in xs]
    rows = [z * 8 + v * 2 for v in ys]
    slots = [v * NX for v in ys]
    plane = [(dy, dx) for dy in range(NY) for dx in range(NX) if dy or dx]
    plane.sort(key=lambda o: -(min(o[0], NY - o[0]) + min(o[1], NX - o[1])))
    plane = [plane[i] for i in (0, 1, 4, 2, 3, 6, 7, 9, 10, 5, 8, 11, 14, 12, 13)]
    peers = {
        (dy, dx): ({"space": rows[dy] + x_his[dx], "rep": tiles[dx]}, slots[dy] + xs[dx])
        for dy, dx in plane
    }
    order = [peers[o] for o in plane]
    far = order[:FAR]
    crossed = [{"space": rows[dy] + x_his[dx], "rep": tiles[dx] + 1 - 2 * core} for dy, dx in plane[:FAR]]
    line = [{"space": lax.rem(z + d, NZ) * 8 + rest, "rep": tile} for d in (4, 3, 5, 2, 6, 1, 7)]
    strips = NX // 2 * NY * NZ
    above = {"space": lax.rem(strip + 1, strips), "rep": tile}
    below = {"space": lax.rem(strip + strips - 1, strips), "rep": tile}

    loads = [
        pltpu.make_async_copy(src, dst, ls.at[i])
        for i, (src, dst) in enumerate(
            ((f_hbm, f_ref), (cw_hbm, cw_ref), (g_hbm, g_ref), (dw_hbm, dw_ref), (nb_hbm, nb_ref), (cnt_hbm, cnt_ref))
        )
    ]
    loads[0].start()
    barrier = pltpu.get_barrier_semaphore()
    greet = [above, below] + [peer for peer, _ in order] + crossed + line + [sibling]
    for i, d in enumerate(greet):
        pl.semaphore_signal(barrier, inc=1, device_id=d, device_id_type=MESH)
        if i == 1:
            for c in loads[1:]:
                c.start()

    loads[0].wait()
    fill_tables(f_ref, t_ref, lo_ref, hi_ref)
    pack_halo(lo_ref, hi_ref, ho_ref)
    pl.semaphore_wait(barrier, len(greet))
    halo = [
        pltpu.make_async_remote_copy(
            ho_ref.at[0], hi_in_ref.at[0], hs.at[0], hr.at[0],
            device_id=above, device_id_type=MESH,
        ),
        pltpu.make_async_remote_copy(
            ho_ref.at[1], hi_in_ref.at[1], hs.at[1], hr.at[1],
            device_id=below, device_id_type=MESH,
        ),
    ]
    for c in halo:
        c.start()
    loads[1].wait()
    fill_weights(cw_ref, w_ref)
    fill_permutation(s_ref)
    for c in loads[2:]:
        c.wait()
    count = cnt_ref[0]
    cell_gradients(g_ref, dw_ref, count, s_ref, ga_ref, ue_ref, grad_ref)
    for b in range(4):
        fill_inner(nb_ref, count, b, t_ref, q_ref, qe_ref)
        inner_forward(b, w_ref, q_ref, pre_ref)
        inner_block(b, pre_ref, grad_ref, hid_ref, sh_ref)
    stash_edges(pre_ref, grad_ref, pe_ref, ge_ref)
    dg_ref[...] = inner_down(hid_ref, s_ref, ga_ref)
    for dy in range(3):
        cg_ref[dy] = dot(sh_ref[...], q_ref[dy], NN)

    for c in halo:
        c.wait()
    fill_halo(hi_in_ref, lo_ref, hi_ref)
    for b in range(4):
        fill_outer(nb_ref, b, lo_ref, hi_ref, qe_ref)
    sums = outer_forward(w_ref, qe_ref)

    acts = edge_planes(sums, pe_ref, ge_ref, ue_ref, dg_ref, down_ref)
    swap_down = remote(down_ref.at[1 - core], mate_down, cs.at[0], cr.at[0], sibling)
    swap_down.start()
    conv_gradient(acts, qe_ref, cg_ref, conv_ref)
    for i, (peer, at) in enumerate(far):
        for k, (half, target) in enumerate(((core, peer), (1 - core, crossed[i]))):
            slot = 2 * i + k
            far_out[slot, 0:CONV_ROWS] = conv_ref[half, at].astype(BF16)
            far_out[slot, CONV_ROWS:ROWS] = down_ref[half, at].astype(BF16)
            remote(far_out.at[slot], far_in.at[slot], fs.at[0], fr.at[0], target).start()
    swap_conv = remote(conv_ref.at[1 - core], mate_conv, cs.at[1], cr.at[1], sibling)
    swap_conv.start()

    def summed(at):
        return (
            conv_ref[core, at] + mate_conv[at],
            down_ref[core, at] + mate_down[at],
        )

    swap_down.wait_recv()
    swap_conv.wait_recv()
    for i, (peer, at) in enumerate(order[FAR:]):
        conv, down = summed(at)
        outgoing[i, 0:CONV_ROWS] = conv.astype(BF16)
        outgoing[i, CONV_ROWS:ROWS] = down.astype(BF16)
        remote(outgoing.at[i], parts.at[i], ss.at[0], rs.at[0], peer).start()
    total = jnp.concatenate(summed(me), 0)
    scattered = remote(outgoing, parts, ss.at[0], rs.at[0], sibling)
    scattered.wait_recv()
    for i in range(NXY - 1 - FAR):
        total = total + parts[i].astype(F32)
    straight = remote(far_out, far_in, fs.at[0], fr.at[0], sibling)
    straight.wait_recv()
    for i in range(2 * FAR):
        total = total + far_in[i].astype(F32)

    along[z] = total.astype(BF16)
    for peer in line:
        remote(along.at[z], along.at[z], zs.at[0], zr.at[0], peer).start()
    edge_hidden(sums, pe_ref, hid_ref)
    swap_down.wait_send()
    swap_conv.wait_send()
    scattered.wait_send()
    straight.wait_send()
    most = along.at[pl.ds(0, NZ - 1)]
    spread = remote(most, most, zs.at[0], zr.at[0], sibling)
    spread.wait_recv()
    total = along[0].astype(F32)
    for i in range(1, NZ):
        total = total + along[i].astype(F32)

    half = core * NXY
    own = o_ref.at[half + me]
    o_ref[half + me] = total
    last = []
    for i, (peer, _) in enumerate(order):
        last.append(remote(own, own, gs.at[0], gr.at[i], peer))
        last[-1].start()
    remote(own, own, es.at[0], er.at[0], sibling).start()
    spread.wait_send()
    for i in reversed(range(NXY - 1)):
        last[i].wait_recv()
        _, at = peers[-plane[i][0] % NY, -plane[i][1] % NX]
        piece = o_ref.at[half + at]
        remote(piece, piece, es.at[0], er.at[0], sibling).start()
    sent = o_ref.at[pl.ds(half, NXY - 1)]
    remote(sent, sent, gs.at[0], gr.at[0], sibling).wait_send()
    block = o_ref.at[pl.ds(half, NXY)]
    remote(block, block, es.at[0], er.at[0], sibling).wait()


def section(features, neighbours, counts, cotangent, conv_weight, down_weight):
    dma = pltpu.SemaphoreType.DMA
    vm = pltpu.VMEM
    near = NXY - 1

    return pl.pallas_call(
        section_kernel,
        out_shape=(
            pltpu.VMEM((4, 64, 512), BF16),
            pltpu.VMEM((32, ROWS, 128), F32),
        ),
        in_specs=[ANY] * 6,
        out_specs=(VM, VM),
        scratch_shapes=[
            pltpu.SMEM((4, 27), jnp.int32), pltpu.SMEM((1,), jnp.int32),
            vm((4, 64, 512), BF16), vm((4, 64, 128), BF16), vm((27, 64, 64), BF16), vm((8, 64, 128), BF16),
            vm((2, 2, 64, 128), BF16), vm((2, 2, 64, 128), BF16),
            vm((5, 8, 8, 8, 128), F32), vm((9, 8, 8, 128), F32), vm((9, 8, 8, 128), F32),
            vm((3, 2048, 256), BF16), vm((3, 3, 512, 256), BF16), vm((3, 192, 192), BF16),
            vm((512, 512), BF16), vm((256, 128), BF16), vm((4, 64, 512), F32), vm((4, 64, 512), F32),
            vm((192, 2048), BF16),
            vm((2, 64, 256), F32), vm((2, 64, 256), F32), vm((2, 128, 256), BF16),
            vm((512, 128), F32), vm((3, 192, 256), F32),
            vm((2, NXY, CONV_ROWS, 128), F32), vm((2, NXY, DOWN_ROWS, 128), F32),
            vm((NXY, CONV_ROWS, 128), F32), vm((NXY, DOWN_ROWS, 128), F32),
            vm((near - FAR, ROWS, 128), BF16), vm((near - FAR, ROWS, 128), BF16),
            vm((2 * FAR, ROWS, 128), BF16), vm((2 * FAR, ROWS, 128), BF16), vm((NZ, ROWS, 128), BF16),
            dma((6,)), dma((2,)), dma((2,)), dma((2,)), dma((2,)), dma((1,)), dma((1,)),
            dma((1,)), dma((1,)), dma((1,)), dma((near,)), dma((1,)), dma((1,)), dma((1,)), dma((1,)),
        ],
        compiler_params=pltpu.CompilerParams(
            collective_id=0, has_side_effects=True, vmem_limit_bytes=56 << 20
        ),
        name="section",
    )(neighbours, counts, features, cotangent, conv_weight, down_weight)


def unpack_kernel(v_ref, hid_ref, conv_hbm, down_hbm, hid_hbm, conv_ref, sem):
    moves = [
        pltpu.make_async_copy(v_ref.at[:, pl.ds(CONV_ROWS, DOWN_ROWS), :], down_hbm, sem.at[0]),
        pltpu.make_async_copy(hid_ref, hid_hbm, sem.at[1]),
    ]
    for m in moves:
        m.start()
    conv = v_ref[:, 0:CONV_ROWS].reshape(1024, 128)
    for dx in range(3):
        for dy in range(3):
            at = dy * 192 + dx * 64
            pair = conv[at : at + 64]
            conv_ref[dx * 9 + dy * 3] = pair[:, 0:64]
            conv_ref[dx * 9 + dy * 3 + 1] = pair[:, 64:128]
            at = 768 + dx * 64 if dy == 2 else 576 + dx * 64
            side = 64 if dy == 1 else 0
            conv_ref[dx * 9 + dy * 3 + 2] = conv[at : at + 64, side : side + 64]
        part = pl.ds(dx * 9, 9)
        moves.append(
            pltpu.make_async_copy(conv_ref.at[part], conv_hbm.at[part], sem.at[2 + dx])
        )
        moves[-1].start()
    for m in moves:
        m.wait()


def unpack(pieces, hidden):
    return pl.pallas_call(
        unpack_kernel,
        out_shape=(
            jax.ShapeDtypeStruct((27, 64, 64), F32),
            jax.ShapeDtypeStruct((32, DOWN_ROWS, 128), F32),
            jax.ShapeDtypeStruct((4, 64, 512), BF16),
        ),
        in_specs=[VM, VM],
        out_specs=(ANY, ANY, ANY),
        scratch_shapes=[pltpu.VMEM((27, 64, 64), F32), pltpu.SemaphoreType.DMA((5,))],
        compiler_params=pltpu.CompilerParams(vmem_limit_bytes=48 << 20),
        name="unpack",
    )(pieces, hidden)


def body(features, neighbours, counts, cotangent, conv_weight, down_weight):
    down_rows = jnp.swapaxes(down_weight, 1, 2)
    hidden, pieces = section(features, neighbours, counts, cotangent, conv_weight, down_rows)
    conv_grad, down_grad, hidden = unpack(pieces, hidden)
    return hidden, conv_grad, jnp.swapaxes(down_grad.reshape(8, 64, 128), 1, 2)


def solution(mesh):
    both = ("space", "rep")
    return jax.shard_map(
        body,
        mesh=mesh,
        in_specs=(
            P(both, None, None), P(both, None), P(both), P(both, None, None), P(), P(),
        ),
        out_specs=(P(both, None, None), P(), P()),
        check_vma=False,
    )
```

```python
import jax
import jax.numpy as jnp
from jax import lax
from jax.experimental import pallas as pl
from jax.experimental.pallas import tpu as pltpu
from jax.sharding import PartitionSpec as P

MESH = pl.DeviceIdType.MESH
F32, BF16 = jnp.float32, jnp.bfloat16
VM = pl.BlockSpec(memory_space=pltpu.VMEM)
ANY = pl.BlockSpec(memory_space=pl.ANY)
NX, NY, NZ = 4, 4, 8
NXY = NX * NY
CONV_ROWS, DOWN_ROWS = 32, 16
ROWS = CONV_ROWS + DOWN_ROWS


def dot(a, b, dims):
    return lax.dot_general(a, b, (dims, ((), ())), preferred_element_type=F32)


NN, NT, TN = ((1,), (0,)), ((1,), (1,)), ((0,), (0,))


def voxels_in_rows(block):
    wide = block.astype(F32)
    return jnp.concatenate([wide, wide], 0).T


def fill_weights(cw_ref, w_ref):
    for dy in range(3):
        for dx in range(3):
            row = [cw_ref[dx * 9 + dy * 3 + dz].astype(F32) for dz in range(3)]
            w_ref[dy, dx * 64 : dx * 64 + 64, :] = jnp.concatenate(row, 1).astype(BF16)


def fill_tables(f_ref, t_ref, lo_ref, hi_ref):
    for j in range(4):
        for q in range(4):
            part = voxels_in_rows(f_ref[j, :, q * 128 : q * 128 + 128])
            t_ref[j, q * 2 : q * 2 + 2] = part.reshape(2, 8, 8, 128)
        lo_ref[j] = t_ref[j, 7]
        hi_ref[j] = t_ref[j, 0]
    t_ref[4] = jnp.zeros((8, 8, 8, 128), F32)
    lo_ref[8] = jnp.zeros((8, 8, 128), F32)
    hi_ref[8] = jnp.zeros((8, 8, 128), F32)


def first_half(shape):
    return lax.broadcasted_iota(jnp.int32, shape, 1) < 64


def pack_halo(lo_ref, hi_ref, out_ref):
    first = first_half((64, 128))
    for way, table in enumerate((lo_ref, hi_ref)):
        for j in range(0, 4, 2):
            pair = [table[j + i].reshape(64, 128) for i in range(2)]
            out_ref[way, j // 2] = jnp.where(first, *pair).astype(BF16)


def fill_halo(in_ref, lo_ref, hi_ref):
    first = first_half((64, 128))
    for way, table in enumerate((lo_ref, hi_ref)):
        for j in range(0, 4, 2):
            pair = in_ref[way, j // 2].astype(F32)
            turned = pltpu.roll(pair, 64, 1)
            table[4 + j] = jnp.where(first, pair, turned).reshape(8, 8, 128)
            table[5 + j] = jnp.where(first, turned, pair).reshape(8, 8, 128)


def store_plane(put, middle, below, above):
    z = lax.broadcasted_iota(jnp.int32, (10, 8, 128), 1)
    first = lax.broadcasted_iota(jnp.int32, (10, 8, 128), 2) < 64
    minus = pltpu.roll(jnp.where(z == 7, below, middle), 1, 1)
    plus = pltpu.roll(jnp.where(z == 0, above, middle), 7, 1)
    left = jnp.where(first, minus, middle)
    for dy in range(3):
        put(dy, 0, left[dy : dy + 8].reshape(64, 128).astype(BF16))
        put(dy, 128, plus[dy : dy + 8].reshape(64, 128).astype(BF16))


def link(nb_ref, b, ox, oy, oz, zero):
    j = nb_ref[b, (ox + 1) * 9 + (oy + 1) * 3 + oz + 1]
    return jnp.where(j < 0, zero, j)


def fill_inner(nb_ref, count, b, t_ref, q_ref, qe_ref):
    own = jnp.where(b < count, b, 4)
    idx = [[link(nb_ref, b, 0, oy, oz, 4) for oy in (-1, 0, 1)] for oz in (0, -1, 1)]
    idx[0][1] = own
    for xp in range(1, 9):
        cols = [
            jnp.concatenate(
                [t_ref[i0, xp - 1, 7:8], t_ref[i1, xp - 1], t_ref[i2, xp - 1, 0:1]], 0
            )
            for i0, i1, i2 in idx
        ]
        row, edge = b * 512 + (xp - 1) * 64, b * 64

        def put(dy, lane, rows, row=row, edge=edge, xp=xp):
            q_ref[dy, row : row + 64, lane : lane + 128] = rows
            if xp in (1, 2):
                qe_ref[dy, xp, edge : edge + 64, lane : lane + 128] = rows
            if xp in (7, 8):
                qe_ref[dy, xp - 7, 256 + edge : 320 + edge, lane : lane + 128] = rows

        store_plane(put, *cols)


def fill_outer(nb_ref, b, lo_ref, hi_ref, qe_ref):
    for ox, side, table in ((-1, 0, lo_ref), (1, 1, hi_ref)):
        cols = []
        for oz in (0, -1, 1):
            i0, i1, i2 = [link(nb_ref, b, ox, oy, oz, 8) for oy in (-1, 0, 1)]
            cols.append(jnp.concatenate([table[i0, 7:8], table[i1], table[i2, 0:1]], 0))

        row = side * 256 + b * 64

        def put(dy, lane, rows, side=side, row=row):
            qe_ref[dy, 2 * side, row : row + 64, lane : lane + 128] = rows

        store_plane(put, *cols)


def regroup(m, outer, inner):
    first = first_half((64, 128))
    out = []
    for i in range(0, inner, 2):
        even, odd = [], []
        for o in range(0, outer, 2):
            x0 = m[o * 64 : o * 64 + 64, i * 64 : i * 64 + 128]
            x1 = m[o * 64 + 64 : o * 64 + 128, i * 64 : i * 64 + 128]
            even.append(jnp.where(first, x0, pltpu.roll(x1, 64, 1)))
            odd.append(jnp.where(first, pltpu.roll(x0, 64, 1), x1))
        out += [jnp.concatenate(even, 1), jnp.concatenate(odd, 1)]
    return jnp.concatenate(out, 0)


def fill_permutation(s_ref):
    v = lax.broadcasted_iota(jnp.int32, (64, 512), 1)
    u = lax.broadcasted_iota(jnp.int32, (64, 512), 0)
    place = (v // 64 % 2) * 4 + (v // 8 % 2) * 2 + v % 2
    cell = (v // 128) * 16 + (v // 16 % 4) * 4 + v % 8 // 2
    at = place * 64 + cell - u
    for t in range(8):
        s_ref[t * 64 : t * 64 + 64] = (at == t * 64).astype(F32).astype(BF16)


def cell_gradients(g_ref, dw_ref, count, s_ref, ga_ref, ue_ref, grad_ref):
    slot = lax.broadcasted_iota(jnp.int32, (256, 128), 0) // 64
    grads = jnp.where(slot < count, g_ref[...].reshape(256, 128).astype(F32), 0.0)
    ga_ref[...] = grads.astype(BF16)
    every = dot(dw_ref[...].reshape(512, 128), ga_ref[...], NT)
    every = regroup(every, 8, 4).astype(BF16)
    grad_ref[...] = dot(every, s_ref[...], NN).reshape(4, 64, 512)
    r = lax.broadcasted_iota(jnp.int32, (256, 256), 0)
    v = lax.broadcasted_iota(jnp.int32, (256, 256), 1)
    cell = v // 64 * 64 + v // 16 % 4 * 4 + v % 8 // 2
    turned = grads.T.astype(BF16)
    for side in range(2):
        spread = (r == cell + 48 * side).astype(F32).astype(BF16)
        ue_ref[side] = dot(turned, spread, NN).astype(BF16)


def inner_down(hid_ref, s_ref, ga_ref):
    cells = dot(hid_ref[...].reshape(256, 512), s_ref[...], NT)
    return dot(regroup(cells, 4, 8).astype(BF16), ga_ref[...], NN)


def inner_forward(b, w_ref, q_ref, pre_ref):
    acc = jnp.zeros((192, 512), F32)
    for dy in range(3):
        acc += dot(w_ref[dy], q_ref[dy, b * 512 : b * 512 + 512, 0:192], NT)
    gap = jnp.zeros((64, 64), F32)
    low = jnp.concatenate([gap, acc[0:64, 0:448]], 1)
    high = jnp.concatenate([acc[128:192, 64:512], gap], 1)
    pre_ref[b] = acc[64:128] + low + high


def outer_forward(w_ref, qe_ref):
    low, high = jnp.zeros((64, 256), F32), jnp.zeros((64, 256), F32)
    for dy in range(3):
        low += dot(w_ref[dy, 0:64], qe_ref[dy, 0, 0:256, 0:192], NT)
        high += dot(w_ref[dy, 128:192], qe_ref[dy, 2, 256:512, 0:192], NT)
    return low, high


def inner_block(b, pre_ref, grad_ref, hid_ref, sh_ref):
    lane = lax.broadcasted_iota(jnp.int32, (64, 512), 1)
    inside = (lane >= 64) & (lane < 448)
    gap = jnp.zeros((64, 64), F32)
    pre = jnp.where(inside, pre_ref[b], 0.0)
    hidden = jnp.maximum(pre, 0.0)
    hid_ref[b] = hidden.astype(BF16)
    cols = slice(b * 512, b * 512 + 512)
    act = jnp.where(pre > 0, grad_ref[b], 0.0)
    sh_ref[0:64, cols] = jnp.concatenate([act[:, 64:512], gap], 1).astype(BF16)
    sh_ref[64:128, cols] = act.astype(BF16)
    sh_ref[128:192, cols] = jnp.concatenate([gap, act[:, 0:448]], 1).astype(BF16)


def edge_lanes(side):
    return slice(448, 512) if side else slice(0, 64)


def stash_edges(pre_ref, grad_ref, pe_ref, ge_ref):
    for side in range(2):
        at = edge_lanes(side)
        pe_ref[side] = jnp.concatenate([pre_ref[b, :, at] for b in range(4)], 1)
        ge_ref[side] = jnp.concatenate([grad_ref[b, :, at] for b in range(4)], 1)


def edge_planes(sums, pe_ref, ge_ref, ue_ref, dg_ref, down_ref):
    v = lax.broadcasted_iota(jnp.int32, (64, 256), 1)
    place = (v // 8 % 2) * 2 + v % 2
    acts = []
    for side in range(2):
        pre = pe_ref[side] + sums[side]
        hidden = jnp.maximum(pre, 0.0)
        acts.append(jnp.where(pre > 0, ge_ref[side], 0.0))
        spread = jnp.concatenate([jnp.where(place == t, hidden, 0.0) for t in range(4)], 0)
        down = dg_ref[side * 256 : side * 256 + 256] + dot(spread.astype(BF16), ue_ref[side], NT)
        for p in range(NXY):
            down_ref[side, p] = down[p * 16 : p * 16 + 16]
    return jnp.concatenate(acts, 1).astype(BF16)


def edge_hidden(sums, pe_ref, hid_ref):
    first = first_half((64, 128))
    for side in range(2):
        hidden = jnp.maximum(pe_ref[side] + sums[side], 0.0)
        tile = slice(384, 512) if side else slice(0, 128)
        for b in range(4):
            mine = hidden[:, b // 2 * 128 : b // 2 * 128 + 128]
            if b % 2 != side:
                mine = pltpu.roll(mine, 64, 1)
            old = hid_ref[b, :, tile].astype(F32)
            hid_ref[b, :, tile] = jnp.where(first != (side == 1), mine, old).astype(BF16)


def put_rows(v_ref, at, rows):
    for i in range(0, rows.shape[0], CONV_ROWS):
        p = (at + i) // CONV_ROWS
        v_ref[p // NXY, p % NXY] = rows[i : i + CONV_ROWS]


def conv_gradient(acts, qe_ref, cg_ref, conv_ref):
    plus = []
    for dy in range(3):
        parts = [
            cg_ref[dy, dx * 64 : dx * 64 + 64] + dot(acts, qe_ref[dy, dx], NN) for dx in range(3)
        ]
        grads = jnp.concatenate(parts, 0)
        put_rows(conv_ref, dy * 192, grads[:, 0:128])
        plus.append(grads[:, 128:256])
    first = lax.broadcasted_iota(jnp.int32, (192, 128), 1) < 64
    put_rows(conv_ref, 576, jnp.where(first, plus[0], plus[1]))
    put_rows(conv_ref, 768, plus[2])
    put_rows(conv_ref, 960, jnp.zeros((64, 128), F32))


def remote(src, dst, send, recv, peer):
    return pltpu.make_async_remote_copy(
        src, dst, send, recv, device_id=peer, device_id_type=MESH
    )


def section_kernel(
    nb_hbm, cnt_hbm, f_hbm, g_hbm, cw_hbm, dw_hbm, hid_ref, o_ref,
    nb_ref, cnt_ref, f_ref, g_ref, cw_ref, dw_ref, ho_ref, hi_in_ref, t_ref, lo_ref, hi_ref, q_ref, qe_ref, w_ref,
    s_ref, ga_ref, grad_ref, pre_ref, sh_ref, pe_ref, ge_ref, ue_ref, dg_ref, cg_ref,
    conv_ref, down_ref, mate_conv, mate_down, outgoing, parts, along,
    ls, hs, hr, cs, cr, ss, rs, zs, zr, gs, gr, es, er,
):
    strip, tile = lax.axis_index("space"), lax.axis_index("rep")
    z, rest = lax.div(strip, 8), lax.rem(strip, 8)
    y, x_hi = lax.div(rest, 2), lax.rem(rest, 2)
    x_lo, core = lax.div(tile, 2), lax.rem(tile, 2)
    x = x_hi * 2 + x_lo
    me = y * NX + x
    sibling = {"space": strip, "rep": x_lo * 2 + 1 - core}

    ys = [y] + [lax.rem(y + d, NY) for d in range(1, NY)]
    xs = [x] + [lax.rem(x + d, NX) for d in range(1, NX)]
    x_his = [lax.div(v, 2) for v in xs]
    tiles = [lax.rem(v, 2) * 2 + core for v in xs]
    rows = [z * 8 + v * 2 for v in ys]
    slots = [v * NX for v in ys]
    plane = [(dy, dx) for dy in range(NY) for dx in range(NX) if dy or dx]
    plane.sort(key=lambda o: -(min(o[0], NY - o[0]) + min(o[1], NX - o[1])))
    plane = [plane[i] for i in (0, 1, 4, 2, 3, 6, 7, 9, 10, 5, 8, 11, 14, 12, 13)]
    peers = {
        (dy, dx): ({"space": rows[dy] + x_his[dx], "rep": tiles[dx]}, slots[dy] + xs[dx])
        for dy, dx in plane
    }
    order = [peers[o] for o in plane]
    line = [{"space": lax.rem(z + d, NZ) * 8 + rest, "rep": tile} for d in (4, 3, 5, 2, 6, 1, 7)]
    strips = NX // 2 * NY * NZ
    above = {"space": lax.rem(strip + 1, strips), "rep": tile}
    below = {"space": lax.rem(strip + strips - 1, strips), "rep": tile}

    loads = [
        pltpu.make_async_copy(src, dst, ls.at[i])
        for i, (src, dst) in enumerate(
            ((f_hbm, f_ref), (cw_hbm, cw_ref), (g_hbm, g_ref), (dw_hbm, dw_ref), (nb_hbm, nb_ref), (cnt_hbm, cnt_ref))
        )
    ]
    loads[0].start()
    barrier = pltpu.get_barrier_semaphore()
    greet = [above, below] + [peer for peer, _ in order] + line + [sibling]
    for i, d in enumerate(greet):
        pl.semaphore_signal(barrier, inc=1, device_id=d, device_id_type=MESH)
        if i == 1:
            for c in loads[1:]:
                c.start()

    loads[0].wait()
    fill_tables(f_ref, t_ref, lo_ref, hi_ref)
    pack_halo(lo_ref, hi_ref, ho_ref)
    pl.semaphore_wait(barrier, len(greet))
    halo = [
        pltpu.make_async_remote_copy(
            ho_ref.at[0], hi_in_ref.at[0], hs.at[0], hr.at[0],
            device_id=above, device_id_type=MESH,
        ),
        pltpu.make_async_remote_copy(
            ho_ref.at[1], hi_in_ref.at[1], hs.at[1], hr.at[1],
            device_id=below, device_id_type=MESH,
        ),
    ]
    for c in halo:
        c.start()
    loads[1].wait()
    fill_weights(cw_ref, w_ref)
    fill_permutation(s_ref)
    for c in loads[2:]:
        c.wait()
    count = cnt_ref[0]
    cell_gradients(g_ref, dw_ref, count, s_ref, ga_ref, ue_ref, grad_ref)
    for b in range(4):
        fill_inner(nb_ref, count, b, t_ref, q_ref, qe_ref)
        inner_forward(b, w_ref, q_ref, pre_ref)
        inner_block(b, pre_ref, grad_ref, hid_ref, sh_ref)
    stash_edges(pre_ref, grad_ref, pe_ref, ge_ref)
    dg_ref[...] = inner_down(hid_ref, s_ref, ga_ref)
    for dy in range(3):
        cg_ref[dy] = dot(sh_ref[...], q_ref[dy], NN)

    for c in halo:
        c.wait()
    fill_halo(hi_in_ref, lo_ref, hi_ref)
    for b in range(4):
        fill_outer(nb_ref, b, lo_ref, hi_ref, qe_ref)
    sums = outer_forward(w_ref, qe_ref)

    acts = edge_planes(sums, pe_ref, ge_ref, ue_ref, dg_ref, down_ref)
    swap_down = remote(down_ref.at[1 - core], mate_down, cs.at[0], cr.at[0], sibling)
    swap_down.start()
    conv_gradient(acts, qe_ref, cg_ref, conv_ref)
    swap_conv = remote(conv_ref.at[1 - core], mate_conv, cs.at[1], cr.at[1], sibling)
    swap_conv.start()

    def summed(at):
        return (
            conv_ref[core, at] + mate_conv[at],
            down_ref[core, at] + mate_down[at],
        )

    swap_down.wait_recv()
    swap_conv.wait_recv()
    for i, (peer, at) in enumerate(order):
        conv, down = summed(at)
        outgoing[i, 0:CONV_ROWS] = conv.astype(BF16)
        outgoing[i, CONV_ROWS:ROWS] = down.astype(BF16)
        remote(outgoing.at[i], parts.at[i], ss.at[0], rs.at[0], peer).start()
    total = jnp.concatenate(summed(me), 0)
    scattered = remote(outgoing, parts, ss.at[0], rs.at[0], sibling)
    scattered.wait_recv()
    for i in range(NXY - 1):
        total = total + parts[i].astype(F32)

    along[z] = total.astype(BF16)
    for peer in line:
        remote(along.at[z], along.at[z], zs.at[0], zr.at[0], peer).start()
    edge_hidden(sums, pe_ref, hid_ref)
    swap_down.wait_send()
    swap_conv.wait_send()
    scattered.wait_send()
    most = along.at[pl.ds(0, NZ - 1)]
    spread = remote(most, most, zs.at[0], zr.at[0], sibling)
    spread.wait_recv()
    total = along[0].astype(F32)
    for i in range(1, NZ):
        total = total + along[i].astype(F32)

    half = core * NXY
    own = o_ref.at[half + me]
    o_ref[half + me] = total
    last = []
    for i, (peer, _) in enumerate(order):
        last.append(remote(own, own, gs.at[0], gr.at[i], peer))
        last[-1].start()
    remote(own, own, es.at[0], er.at[0], sibling).start()
    spread.wait_send()
    for i in reversed(range(NXY - 1)):
        last[i].wait_recv()
        _, at = peers[-plane[i][0] % NY, -plane[i][1] % NX]
        piece = o_ref.at[half + at]
        remote(piece, piece, es.at[0], er.at[0], sibling).start()
    sent = o_ref.at[pl.ds(half, NXY - 1)]
    remote(sent, sent, gs.at[0], gr.at[0], sibling).wait_send()
    block = o_ref.at[pl.ds(half, NXY)]
    remote(block, block, es.at[0], er.at[0], sibling).wait()


def section(features, neighbours, counts, cotangent, conv_weight, down_weight):
    dma = pltpu.SemaphoreType.DMA
    vm = pltpu.VMEM
    near = NXY - 1

    return pl.pallas_call(
        section_kernel,
        out_shape=(
            pltpu.VMEM((4, 64, 512), BF16),
            pltpu.VMEM((32, ROWS, 128), F32),
        ),
        in_specs=[ANY] * 6,
        out_specs=(VM, VM),
        scratch_shapes=[
            pltpu.SMEM((4, 27), jnp.int32), pltpu.SMEM((1,), jnp.int32),
            vm((4, 64, 512), BF16), vm((4, 64, 128), BF16), vm((27, 64, 64), BF16), vm((8, 64, 128), BF16),
            vm((2, 2, 64, 128), BF16), vm((2, 2, 64, 128), BF16),
            vm((5, 8, 8, 8, 128), F32), vm((9, 8, 8, 128), F32), vm((9, 8, 8, 128), F32),
            vm((3, 2048, 256), BF16), vm((3, 3, 512, 256), BF16), vm((3, 192, 192), BF16),
            vm((512, 512), BF16), vm((256, 128), BF16), vm((4, 64, 512), F32), vm((4, 64, 512), F32),
            vm((192, 2048), BF16),
            vm((2, 64, 256), F32), vm((2, 64, 256), F32), vm((2, 128, 256), BF16),
            vm((512, 128), F32), vm((3, 192, 256), F32),
            vm((2, NXY, CONV_ROWS, 128), F32), vm((2, NXY, DOWN_ROWS, 128), F32),
            vm((NXY, CONV_ROWS, 128), F32), vm((NXY, DOWN_ROWS, 128), F32),
            vm((near, ROWS, 128), BF16), vm((near, ROWS, 128), BF16), vm((NZ, ROWS, 128), BF16),
            dma((6,)), dma((2,)), dma((2,)), dma((2,)), dma((2,)), dma((1,)), dma((1,)),
            dma((1,)), dma((1,)), dma((1,)), dma((near,)), dma((1,)), dma((1,)),
        ],
        compiler_params=pltpu.CompilerParams(
            collective_id=0, has_side_effects=True, vmem_limit_bytes=56 << 20
        ),
        name="section",
    )(neighbours, counts, features, cotangent, conv_weight, down_weight)


def unpack_kernel(v_ref, hid_ref, conv_hbm, down_hbm, hid_hbm, conv_ref, sem):
    moves = [
        pltpu.make_async_copy(v_ref.at[:, pl.ds(CONV_ROWS, DOWN_ROWS), :], down_hbm, sem.at[0]),
        pltpu.make_async_copy(hid_ref, hid_hbm, sem.at[1]),
    ]
    for m in moves:
        m.start()
    conv = v_ref[:, 0:CONV_ROWS].reshape(1024, 128)
    for dx in range(3):
        for dy in range(3):
            at = dy * 192 + dx * 64
            pair = conv[at : at + 64]
            conv_ref[dx * 9 + dy * 3] = pair[:, 0:64]
            conv_ref[dx * 9 + dy * 3 + 1] = pair[:, 64:128]
            at = 768 + dx * 64 if dy == 2 else 576 + dx * 64
            side = 64 if dy == 1 else 0
            conv_ref[dx * 9 + dy * 3 + 2] = conv[at : at + 64, side : side + 64]
        part = pl.ds(dx * 9, 9)
        moves.append(
            pltpu.make_async_copy(conv_ref.at[part], conv_hbm.at[part], sem.at[2 + dx])
        )
        moves[-1].start()
    for m in moves:
        m.wait()


def unpack(pieces, hidden):
    return pl.pallas_call(
        unpack_kernel,
        out_shape=(
            jax.ShapeDtypeStruct((27, 64, 64), F32),
            jax.ShapeDtypeStruct((32, DOWN_ROWS, 128), F32),
            jax.ShapeDtypeStruct((4, 64, 512), BF16),
        ),
        in_specs=[VM, VM],
        out_specs=(ANY, ANY, ANY),
        scratch_shapes=[pltpu.VMEM((27, 64, 64), F32), pltpu.SemaphoreType.DMA((5,))],
        compiler_params=pltpu.CompilerParams(vmem_limit_bytes=48 << 20),
        name="unpack",
    )(pieces, hidden)


def body(features, neighbours, counts, cotangent, conv_weight, down_weight):
    down_rows = jnp.swapaxes(down_weight, 1, 2)
    hidden, pieces = section(features, neighbours, counts, cotangent, conv_weight, down_rows)
    conv_grad, down_grad, hidden = unpack(pieces, hidden)
    return hidden, conv_grad, jnp.swapaxes(down_grad.reshape(8, 64, 128), 1, 2)


def solution(mesh):
    both = ("space", "rep")
    return jax.shard_map(
        body,
        mesh=mesh,
        in_specs=(
            P(both, None, None), P(both, None), P(both), P(both, None, None), P(), P(),
        ),
        out_specs=(P(both, None, None), P(), P()),
        check_vma=False,
    )
```
